32 devices in a mesh: growth: 4 (over z), lat: 8 (over y, x, core).
Axes of the slice: x: 2, y: 2, z: 4, core: 2. Of those that a mesh axis runs over, the one named last changes fastest.
Arguments:
- source: float32 [32, 1024, 1024], P('growth', 'lat'), may hold values from -4 to 4
- spacing: float32 [32], P('growth'), may hold values from 0.5 to 2
Outputs:
- potential: float32 [32, 1024, 1024], P('growth', 'lat')
The draws below stay inside these ranges and needn't reach their ends.
All inputs are finite; a program needn't handle non-finite values.
Results may differ from the reference program's by a relative error of at most 0.0003.
Values sent between devices are 32-bit elements; how exact they have to be, the bound alone decides.
A program may use at most 128 MiB of HBM per device.

```python
import math
import jax
import jax.numpy as jnp
from jax import lax

NX = 1024
NY = 1024
NZ = 32


def draw_source(key, part):
    rough_part = jax.random.truncated_normal(key, -4.0, 4.0, (NZ, NX, NY), jnp.float32)
    return rough_part


def shard_levels(stream_key, dims, pieces, low, largest):
    def one(position, shards_of):
        draws = jax.random.uniform(jax.random.fold_in(jax.random.fold_in(stream_key, 6), position), (shards_of,), jnp.float32, low / len(pieces), largest / len(pieces))
        return jnp.repeat(jnp.exp(draws), dims[position] // shards_of).reshape((-1,) + (1,) * (len(dims) - position - 1))

    loudness = one(*pieces[0])
    for cut in pieces[1:]:
        loudness = loudness * one(*cut)
    return loudness


def setup_inputs(seed: int = 0) -> dict:
    splits = jax.random.split(jax.random.key(seed), 3)
    return {
        "source": draw_source(jax.random.fold_in(splits[2], 71), 0),
        "spacing": jnp.clip(jnp.exp(math.log(2.0) - 1.3862944 * jax.random.uniform(splits[1], (NZ,), jnp.float32) ** shard_levels(splits[1], (NZ,), ((0, 4),), -0.2, 0.2)), 0.5, 2.0),
    }


full_precision = lax.Precision.HIGHEST

def cosine_table(points):
    indices = jnp.arange(points, dtype=jnp.int32)
    phase = (2 * indices[None, :] + 1) * indices[:, None] % (4 * points)
    angle = phase.astype(jnp.float32) * (math.pi / (2.0 * points))
    scale = jnp.where(indices == 0, math.sqrt(1.0 / points), math.sqrt(2.0 / points)).astype(jnp.float32)
    return scale[:, None] * jnp.cos(angle)

def mode_eigenvalue(mode_ids, points):
    sine_half = jnp.sin(mode_ids.astype(jnp.float32) * (math.pi / (2.0 * points)))
    return 4.0 * sine_half * sine_half

def reference(source, spacing):
    table_x = cosine_table(NX)
    table_y = cosine_table(NY)

    def transform_plane(plane):
        inner_part = jnp.dot(table_x, plane, precision=full_precision, preferred_element_type=jnp.float32)
        return jnp.dot(inner_part, table_y.T, precision=full_precision, preferred_element_type=jnp.float32)
    spectral = lax.map(transform_plane, source)
    eigenvalue = mode_eigenvalue(jnp.arange(NX, dtype=jnp.int32), NX)[:, None] + mode_eigenvalue(jnp.arange(NY, dtype=jnp.int32), NY)[None, :]
    padded = jnp.concatenate([jnp.zeros((1,), jnp.float32), spacing, jnp.zeros((1,), jnp.float32)])
    conduct = 2.0 / (padded[:-1] + padded[1:])
    lower_face = conduct[:-1]
    upper_face = conduct[1:]

    def sweep(carried, row_data):
        factor, partial_value = carried
        face_below, face_above, height, spectral_row = row_data
        pivot = face_below + face_above + height * eigenvalue - face_below * factor
        factor = face_above / pivot
        partial_value = (height * spectral_row + face_below * partial_value) / pivot
        return ((factor, partial_value), (factor, partial_value))
    initial = (jnp.zeros((NX, NY), jnp.float32), jnp.zeros((NX, NY), jnp.float32))
    _, (factors, partials) = lax.scan(sweep, initial, (lower_face, upper_face, spacing, spectral))

    def substitute(above_value, row_data):
        factor, partial_value = row_data
        updated = partial_value + factor * above_value
        return (updated, updated)
    _, modal = lax.scan(substitute, jnp.zeros((NX, NY), jnp.float32), (factors, partials), reverse=True)

    def inverse_plane(plane):
        inner_part = jnp.dot(table_x.T, plane, precision=full_precision, preferred_element_type=jnp.float32)
        return jnp.dot(inner_part, table_y, precision=full_precision, preferred_element_type=jnp.float32)
    return lax.map(inverse_plane, modal)
```

```python
import functools
import math

import jax
import jax.numpy as jnp
import ml_dtypes
import numpy as np
from jax import lax
from jax.experimental import pallas as pl
from jax.experimental.pallas import tpu as pltpu
from jax.sharding import PartitionSpec as P

LANES = 128
PAIR = 256
MESH = pl.DeviceIdType.MESH
VMEM_BYTES = 56 * 1024 * 1024


def cosine_table(points):
    ids = np.arange(points, dtype=np.int64)
    phase = (2 * ids[None, :] + 1) * ids[:, None] % (4 * points)
    scale = np.where(ids == 0, math.sqrt(1.0 / points), math.sqrt(2.0 / points))
    return scale[:, None] * np.cos(phase * (math.pi / (2.0 * points)))


def eigenvalues(ids, points):
    return 4.0 * np.sin(np.asarray(ids) * (math.pi / (2.0 * points))) ** 2


def two_parts(table):
    high = table.astype(ml_dtypes.bfloat16)
    low = (table - high.astype(np.float64)).astype(ml_dtypes.bfloat16)
    return jnp.asarray(high), jnp.asarray(low)


def split(value):
    high = value.astype(jnp.bfloat16)
    low = (value - high.astype(jnp.float32)).astype(jnp.bfloat16)
    return high, low


def dot3(a_high, a_low, b_high, b_low):
    dot = functools.partial(jnp.dot, preferred_element_type=jnp.float32)
    return dot(a_high, b_high) + (dot(a_low, b_high) + dot(a_high, b_low))


def reciprocal(x):
    guess = pl.reciprocal(x, approx=True)
    return guess * (2.0 - x * guess)


def fill_conduct(heights_ref, cond_ref):
    heights = heights_ref[...]
    zero = jnp.zeros((1, LANES), jnp.float32)
    cond_ref[...] = 2.0 / (
        jnp.concatenate([zero, heights], axis=0) + jnp.concatenate([heights, zero], axis=0)
    )


def row(ref, z):
    return ref[pl.ds(z, 1), :]


def inverse_pivot(cond_ref, heights_ref, z, eigen, behind, face):
    diagonal = (row(cond_ref, z) + row(cond_ref, z + 1)) + row(heights_ref, z) * eigen
    return reciprocal(diagonal - (face * face) * behind)


def forward_kernel(
    slabs, lanes_count, src, spread, tyh, tyl, txh, txl, phi, lk, lb, lam,
    modal_out, jump_out, heights_out,
    heights, cond, xh, xl, f, inv_s, part_s, inv_low, inv_high, from_low, from_high,
    to_low, to_high, ends, ends_in, jumps, jumps_all, k_inv, k_part, g_modes, g_cuts,
    g_send, g_in, sem_h, sem_up, sem_down, sem_e, sem_r, sem_g,
):
    growth = lax.axis_index("growth")
    lat = lax.axis_index("lat")
    depth, m = f.shape[1], f.shape[2]
    half = m // 2
    nblk = f.shape[0]
    nz = slabs * depth
    width = src.shape[1]
    share = max(1, lanes_count // nblk)
    tiles = [slice(0, half), slice(half, m)]

    barrier = pltpu.get_barrier_semaphore()
    for off in range(1, slabs):
        pl.semaphore_signal(
            barrier, inc=1, device_id=(lax.rem(growth + off, slabs), lat), device_id_type=MESH
        )
    for off in range(1, lanes_count):
        pl.semaphore_signal(
            barrier, inc=1, device_id=(growth, lax.rem(lat + off, lanes_count)),
            device_id_type=MESH,
        )
    pl.semaphore_wait(barrier, slabs + lanes_count - 2)

    def height_copy(off, owner, target):
        return pltpu.make_async_remote_copy(
            src_ref=spread,
            dst_ref=heights.at[pl.ds(owner * depth, depth)],
            send_sem=sem_h.at[0, off],
            recv_sem=sem_h.at[1, off],
            device_id=(target, lat),
            device_id_type=MESH,
        )

    for off in range(1, slabs):
        height_copy(off, growth, lax.rem(growth + off, slabs)).start()
    heights[pl.ds(growth * depth, depth), :] = spread[...]
    rows = src.shape[0]

    def split_rows(i, carry):
        at = pl.ds(pl.multiple_of(i * m, m), m)
        high, low = split(src[at, :])
        xh[at, :] = high
        xl[at, :] = low
        return carry

    lax.fori_loop(0, depth, split_rows, 0)
    for off in range(1, slabs):
        behind = lax.rem(growth + slabs - off, slabs)
        copy = height_copy(off, behind, lax.rem(growth + off, slabs))
        copy.wait_send()
        copy.wait_recv()
    fill_conduct(heights, cond)
    heights_out[...] = heights[...]

    def eigen_of(i, tile):
        at = pl.ds(pl.multiple_of(i * LANES, LANES), LANES)
        return lk[tile, :] + lb[:, at]

    def outer_pivots(i, carry):
        eigen = [eigen_of(i, tile) for tile in tiles]
        zeros = tuple(jnp.zeros((half, LANES), jnp.float32) for _ in tiles)

        def up(z, inv):
            face = row(cond, z)
            return tuple(
                inverse_pivot(cond, heights, z, e, v, face) for e, v in zip(eigen, inv)
            )

        def down(k, inv):
            z = nz - 1 - k
            face = row(cond, z + 1)
            return tuple(
                inverse_pivot(cond, heights, z, e, v, face) for e, v in zip(eigen, inv)
            )

        low = lax.fori_loop(0, growth * depth, up, zeros)
        high = lax.fori_loop(0, nz - (growth + 1) * depth, down, zeros)
        for tile, a, b in zip(tiles, low, high):
            inv_low[i, tile, :] = a
            inv_high[i, tile, :] = b
        return carry

    lax.fori_loop(0, nblk, outer_pivots, 0)

    @pl.when(growth == 0)
    def _():
        from_low[...] = jnp.zeros_like(from_low)

    @pl.when(growth == slabs - 1)
    def _():
        from_high[...] = jnp.zeros_like(from_high)

    first = growth * depth
    chunk = min(512, rows)
    planes = chunk // m

    def transform(pair):
        columns = pl.ds(pl.multiple_of(pair * PAIR, PAIR), PAIR)

        def one(c, carry):
            at = pl.ds(pl.multiple_of(c * chunk, chunk), chunk)
            along_y = dot3(xh[at, :], xl[at, :], tyh[:, columns], tyl[:, columns])
            high, low = split(along_y)
            for k in range(planes):
                part = slice(k * m, (k + 1) * m)
                both = dot3(txh[...], txl[...], high[part, :], low[part, :])
                for side in range(PAIR // LANES):
                    f[pair * (PAIR // LANES) + side, c * planes + k] = both[
                        :, side * LANES : (side + 1) * LANES
                    ]
            return carry

        lax.fori_loop(0, rows // chunk, one, 0)

    def up_copy(i):
        return pltpu.make_async_remote_copy(
            src_ref=to_high.at[i], dst_ref=from_low.at[i],
            send_sem=sem_up.at[0, i], recv_sem=sem_up.at[1, i],
            device_id=(lax.rem(growth + 1, slabs), lat), device_id_type=MESH,
        )

    def down_copy(i):
        return pltpu.make_async_remote_copy(
            src_ref=to_low.at[i], dst_ref=from_high.at[i],
            send_sem=sem_down.at[0, i], recv_sem=sem_down.at[1, i],
            device_id=(lax.rem(growth + slabs - 1, slabs), lat), device_id_type=MESH,
        )

    def sweep_up(i):
        @pl.when(growth > 0)
        def _():
            up_copy(i).wait_recv()

        eigen = [eigen_of(i, tile) for tile in tiles]
        inv = [inv_low[i, tile, :] for tile in tiles]
        part = [from_low[i, tile, :] for tile in tiles]
        for k in range(depth):
            z = first + k
            face = row(cond, z)
            height = row(heights, z)
            for n, tile in enumerate(tiles):
                inv[n] = inverse_pivot(cond, heights, z, eigen[n], inv[n], face)
                part[n] = (height * f[i, k, tile, :] + face * part[n]) * inv[n]
                inv_s[i, k, tile, :] = inv[n]
                part_s[i, k, tile, :] = part[n]

        @pl.when(growth < slabs - 1)
        def _():
            for n, tile in enumerate(tiles):
                to_high[i, tile, :] = part[n]
            up_copy(i).start()

    def sweep_down(i):
        @pl.when(growth < slabs - 1)
        def _():
            down_copy(i).wait_recv()

        @pl.when(growth > 0)
        def _():
            eigen = [eigen_of(i, tile) for tile in tiles]
            inv = [inv_high[i, tile, :] for tile in tiles]
            part = [from_high[i, tile, :] for tile in tiles]
            for k in reversed(range(depth)):
                z = first + k
                face = row(cond, z + 1)
                height = row(heights, z)
                for n, tile in enumerate(tiles):
                    inv[n] = inverse_pivot(cond, heights, z, eigen[n], inv[n], face)
                    part[n] = (height * f[i, k, tile, :] + face * part[n]) * inv[n]
            for n, tile in enumerate(tiles):
                to_low[i, tile, :] = part[n]
            down_copy(i).start()

    def finish(i):
        face = row(cond, first + depth)
        value = []
        weight = [phi[tile, :] for tile in tiles]
        for n, tile in enumerate(tiles):
            inv = inv_s[i, depth - 1, tile, :]
            top = part_s[i, depth - 1, tile, :] + (face * inv) * from_high[i, tile, :]
            value.append(top * reciprocal(1.0 - (face * face) * inv * inv_high[i, tile, :]))
        for k in reversed(range(depth)):
            if k < depth - 1:
                face = row(cond, first + k + 1)
                for n, tile in enumerate(tiles):
                    value[n] = part_s[i, k, tile, :] + (face * inv_s[i, k, tile, :]) * value[n]
            sums = []
            for n, tile in enumerate(tiles):
                modal_out[i, k, tile, :] = value[n]
                sums.append(jnp.sum(weight[n] * value[n], axis=0, keepdims=True))
            ends[i, k : k + 1, :] = sums[0] + sums[1]
            ends[i, depth + k : depth + k + 1, :] = sums[0] - sums[1]

    per_pair = PAIR // LANES
    lag = slabs - 1

    def stage(tt, carry):
        @pl.when(tt < nblk // per_pair)
        def _():
            transform(tt)

        for side in range(per_pair):
            t = tt * per_pair + side
            up_i = t - growth
            down_i = t - (slabs - 1 - growth)
            end_i = t - lag

            @pl.when((up_i >= 0) & (up_i < nblk))
            def _():
                sweep_up(up_i)

            @pl.when((down_i >= 0) & (down_i < nblk))
            def _():
                sweep_down(down_i)

            @pl.when((end_i >= 0) & (end_i < nblk))
            def _():
                finish(end_i)

        return carry

    lax.fori_loop(0, pl.cdiv(nblk + lag, per_pair), stage, 0)

    def block_of(rank):
        return rank // share

    def ends_copy(off, owner, target):
        return pltpu.make_async_remote_copy(
            src_ref=ends.at[block_of(target)], dst_ref=ends_in.at[owner],
            send_sem=sem_e.at[0, off], recv_sem=sem_e.at[1, off],
            device_id=(growth, target), device_id_type=MESH,
        )

    for off in range(1, lanes_count):
        ends_copy(off, lat, lax.rem(lat + off, lanes_count)).start()
    ends_in[lat] = ends[block_of(lat)]

    def drain(i, carry):
        @pl.when(growth < slabs - 1)
        def _():
            up_copy(i).wait_send()

        @pl.when(growth > 0)
        def _():
            down_copy(i).wait_send()

        return carry

    lax.fori_loop(0, nblk, drain, 0)
    for off in range(1, lanes_count):
        copy = ends_copy(
            off, lax.rem(lat + lanes_count - off, lanes_count), lax.rem(lat + off, lanes_count)
        )
        copy.wait_send()
        copy.wait_recv()

    cuts = lanes_count - 1
    sines = [
        [
            math.sqrt(2.0 / lanes_count) * math.sin(math.pi * (c + 1) * (j + 1) / lanes_count)
            for j in range(cuts)
        ]
        for c in range(cuts)
    ]
    jump = [ends_in[c, depth:, :] - ends_in[c + 1, :depth, :] for c in range(cuts)]
    for j in range(cuts):
        total = jump[0] * sines[0][j]
        for c in range(1, cuts):
            total += jump[c] * sines[c][j]
        jumps[j] = total
    jumps_all[growth] = jumps[...]

    def jumps_copy(off, owner, target):
        return pltpu.make_async_remote_copy(
            src_ref=jumps, dst_ref=jumps_all.at[owner],
            send_sem=sem_r.at[0, off], recv_sem=sem_r.at[1, off],
            device_id=(target, lat), device_id_type=MESH,
        )

    for off in range(1, slabs):
        jumps_copy(off, growth, lax.rem(growth + off, slabs)).start()
    for off in range(1, slabs):
        copy = jumps_copy(
            off, lax.rem(growth + slabs - off, slabs), lax.rem(growth + off, slabs)
        )
        copy.wait_send()
        copy.wait_recv()

    block = pl.ds(pl.multiple_of(block_of(lat) * LANES, LANES), LANES)
    middle = nz // 2

    def correct(j, carry):
        def right(z):
            return row(heights, z) * jumps_all[z // depth, j, z % depth : z % depth + 1, :]

        for n, tile in enumerate(tiles):
            weight = lam[j, tile, :]
            eigen = weight + lb[:, block]
            zero = jnp.zeros((half, LANES), jnp.float32)
            inv_a, part_a, inv_b, part_b = zero, zero, zero, zero
            for k in range(middle):
                z = k
                face = row(cond, z)
                inv_a = inverse_pivot(cond, heights, z, eigen, inv_a, face)
                part_a = (right(z) + face * part_a) * inv_a
                k_inv[z] = inv_a
                k_part[z] = part_a
                z = nz - 1 - k
                face = row(cond, z + 1)
                inv_b = inverse_pivot(cond, heights, z, eigen, inv_b, face)
                part_b = (right(z) + face * part_b) * inv_b
                k_inv[z] = inv_b
                k_part[z] = part_b
            face = row(cond, middle)
            below = (part_a + (face * inv_a) * part_b) * reciprocal(
                1.0 - (face * face) * inv_a * inv_b
            )
            above = part_b + (face * inv_b) * below

            def put(z, value):
                total = jnp.sum(weight * value, axis=0, keepdims=True) * (1.0 / m)
                if n == 0:
                    held = jumps_all[z // depth, j, z % depth : z % depth + 1, :]
                else:
                    held = g_modes[j, z : z + 1, :]
                g_modes[j, z : z + 1, :] = held - total

            put(middle - 1, below)
            put(middle, above)
            for k in range(1, middle):
                z = middle - 1 - k
                below = k_part[z] + (row(cond, z + 1) * k_inv[z]) * below
                put(z, below)
                z = middle + k
                above = k_part[z] + (row(cond, z) * k_inv[z]) * above
                put(z, above)
        return carry

    lax.fori_loop(0, cuts, correct, 0)

    for c in range(cuts):
        total = g_modes[0] * sines[c][0]
        for j in range(1, cuts):
            total += g_modes[j] * sines[c][j]
        g_cuts[c] = total
    for d in range(lanes_count):
        low = g_cuts[d - 1] if d > 0 else jnp.zeros((nz, LANES), jnp.float32)
        high = g_cuts[d] if d < cuts else jnp.zeros((nz, LANES), jnp.float32)
        g_send[d, 0] = high - low
        g_send[d, 1] = -(high + low)

    def g_copy(off, owner, target):
        return pltpu.make_async_remote_copy(
            src_ref=g_send.at[target], dst_ref=g_in.at[block_of(owner)],
            send_sem=sem_g.at[0, off], recv_sem=sem_g.at[1, off],
            device_id=(growth, target), device_id_type=MESH,
        )

    def speaks(rank, act):
        if share == 1:
            act()
        else:
            pl.when(lax.rem(rank, share) == 0)(act)

    def own_block():
        g_in[block_of(lat)] = g_send[lat]

    for off in range(1, lanes_count):
        copy = g_copy(off, lat, lax.rem(lat + off, lanes_count))
        speaks(lat, copy.start)
    speaks(lat, own_block)
    for off in range(1, lanes_count):
        owner = lax.rem(lat + lanes_count - off, lanes_count)
        target = lax.rem(lat + off, lanes_count)
        speaks(lat, g_copy(off, lat, target).wait_send)
        speaks(owner, g_copy(off, owner, target).wait_recv)
    jump_out[...] = g_in[...]


def inverse_kernel(
    slabs, modal, jump, heights, tyh, tyl, txh, txl, phi, lk, lb,
    out,
    cond, inv_s, part_s, mh, ml, gh, gl,
):
    growth = lax.axis_index("growth")
    nblk, depth, m = modal.shape[:3]
    half = m // 2
    nz = slabs * depth
    tiles = [slice(0, half), slice(half, m)]
    first = growth * depth
    fill_conduct(heights, cond)
    per_pair = PAIR // LANES

    def correct(i, side):
        at = pl.ds(pl.multiple_of(i * LANES, LANES), LANES)
        eigen = [lk[tile, :] + lb[:, at] for tile in tiles]
        zero = jnp.zeros((half, LANES), jnp.float32)

        def advance(z, face, state):
            height = row(heights, z)
            new = []
            for n in range(2):
                inv, part = state[2 * n], state[2 * n + 1]
                inv = inverse_pivot(cond, heights, z, eigen[n], inv, face)
                right = height * jump[i, n, pl.ds(z, 1), :]
                new += [inv, (right + face * part) * inv]
            return tuple(new)

        def up(z, state):
            return advance(z, row(cond, z), state)

        def down(k, state):
            z = nz - 1 - k
            return advance(z, row(cond, z + 1), state)

        high = lax.fori_loop(0, nz - first - depth, down, (zero,) * 4)
        state = lax.fori_loop(0, first, up, (zero,) * 4)
        for k in range(depth):
            state = up(first + k, state)
            for n, tile in enumerate(tiles):
                inv_s[k, tile, :] = state[2 * n]
                part_s[k, tile, :] = state[2 * n + 1]
        face = row(cond, first + depth)
        value = []
        for n in range(2):
            inv, part = state[2 * n], state[2 * n + 1]
            top = part + (face * inv) * high[2 * n + 1]
            value.append(top * reciprocal(1.0 - (face * face) * inv * high[2 * n]))
        for k in reversed(range(depth)):
            if k < depth - 1:
                face = row(cond, first + k + 1)
            for n, tile in enumerate(tiles):
                if k < depth - 1:
                    value[n] = part_s[k, tile, :] + (face * inv_s[k, tile, :]) * value[n]
                a, b = split(modal[i, k, tile, :] - phi[tile, :] * value[n])
                columns = slice(side * LANES, (side + 1) * LANES)
                mh[k, tile, columns] = a
                ml[k, tile, columns] = b

    def pair(tt, carry):
        for side in range(per_pair):
            correct(tt * per_pair + side, side)
        columns = pl.ds(pl.multiple_of(tt * PAIR, PAIR), PAIR)
        for k in range(depth):
            a, b = split(dot3(txh[...], txl[...], mh[k], ml[k]))
            gh[k * m : (k + 1) * m, columns] = a
            gl[k * m : (k + 1) * m, columns] = b
        return carry

    lax.fori_loop(0, nblk // per_pair, pair, 0)

    rows = gh.shape[0]
    chunk = min(512, rows)
    width = out.shape[1]

    def columns_of(c, carry):
        columns = pl.ds(pl.multiple_of(c * PAIR, PAIR), PAIR)

        def rows_of(r, inner):
            at = pl.ds(pl.multiple_of(r * chunk, chunk), chunk)
            out[at, columns] = dot3(gh[at, :], gl[at, :], tyh[:, columns], tyl[:, columns])
            return inner

        return lax.fori_loop(0, rows // chunk, rows_of, carry)

    lax.fori_loop(0, width // PAIR, columns_of, 0)


def per_device(source, spacing):
    depth, m, width = source.shape
    lanes_count = lax.axis_size("lat")
    slabs = lax.axis_size("growth")
    nz = slabs * depth
    points = m * lanes_count
    nblk = width // LANES
    cuts = lanes_count - 1
    half = m // 2
    f32 = jnp.float32

    order = np.concatenate([np.arange(0, m, 2), np.arange(1, m, 2)])
    local = cosine_table(m)[order]
    along_y = cosine_table(width)
    tyh_t, tyl_t = two_parts(np.ascontiguousarray(along_y.T))
    tyh, tyl = two_parts(along_y)
    txh, txl = two_parts(local)
    txh_t, txl_t = two_parts(np.ascontiguousarray(local.T))

    def spread_lanes(column):
        return jnp.asarray(np.repeat(np.asarray(column, np.float32)[..., None], LANES, axis=-1))

    phi = spread_lanes(local[:, 0])
    lk = spread_lanes(eigenvalues(order, m))
    lb = jnp.asarray(eigenvalues(np.arange(width), width).astype(np.float32)[None, :])
    folds = []
    for j in range(1, lanes_count):
        ids = [k for k in range(1, points) if k % (2 * lanes_count) in (j, 2 * lanes_count - j)]
        folds.append(eigenvalues(ids, points))
    lam = spread_lanes(np.stack(folds))

    flat = source.reshape(depth * m, width)
    spread = jnp.broadcast_to(spacing[:, None], (depth, LANES))
    vmem = pl.BlockSpec(memory_space=pltpu.VMEM)
    dma = pltpu.SemaphoreType.DMA
    V = pltpu.VMEM
    modal, jump, heights = pl.pallas_call(
        functools.partial(forward_kernel, slabs, lanes_count),
        out_shape=(
            jax.ShapeDtypeStruct((nblk, depth, m, LANES), f32),
            jax.ShapeDtypeStruct((nblk, 2, nz, LANES), f32),
            jax.ShapeDtypeStruct((nz, LANES), f32),
        ),
        in_specs=[vmem] * 10,
        out_specs=(vmem, vmem, vmem),
        scratch_shapes=[
            V((nz, LANES), f32),
            V((nz + 1, LANES), f32),
            V((depth * m, width), jnp.bfloat16),
            V((depth * m, width), jnp.bfloat16),
            V((nblk, depth, m, LANES), f32),
            V((nblk, depth, m, LANES), f32),
            V((nblk, depth, m, LANES), f32),
            V((nblk, m, LANES), f32),
            V((nblk, m, LANES), f32),
            V((nblk, m, LANES), f32),
            V((nblk, m, LANES), f32),
            V((nblk, m, LANES), f32),
            V((nblk, m, LANES), f32),
            V((nblk, 2 * depth, LANES), f32),
            V((lanes_count, 2 * depth, LANES), f32),
            V((cuts, depth, LANES), f32),
            V((slabs, cuts, depth, LANES), f32),
            V((nz, half, LANES), f32),
            V((nz, half, LANES), f32),
            V((cuts, nz, LANES), f32),
            V((cuts, nz, LANES), f32),
            V((lanes_count, 2, nz, LANES), f32),
            V((nblk, 2, nz, LANES), f32),
            dma((2, slabs)),
            dma((2, nblk)),
            dma((2, nblk)),
            dma((2, lanes_count)),
            dma((2, slabs)),
            dma((2, lanes_count)),
        ],
        compiler_params=pltpu.CompilerParams(
            collective_id=0, has_side_effects=True, vmem_limit_bytes=VMEM_BYTES
        ),
        name="slab_solve",
    )(flat, spread, tyh_t, tyl_t, txh, txl, phi, lk, lb, lam)

    result = pl.pallas_call(
        functools.partial(inverse_kernel, slabs),
        out_shape=jax.ShapeDtypeStruct((depth * m, width), f32),
        in_specs=[vmem] * 10,
        out_specs=vmem,
        scratch_shapes=[
            V((nz + 1, LANES), f32),
            V((depth, m, LANES), f32),
            V((depth, m, LANES), f32),
            V((depth, m, PAIR), jnp.bfloat16),
            V((depth, m, PAIR), jnp.bfloat16),
            V((depth * m, width), jnp.bfloat16),
            V((depth * m, width), jnp.bfloat16),
        ],
        compiler_params=pltpu.CompilerParams(vmem_limit_bytes=VMEM_BYTES),
        name="face_correction",
    )(modal, jump, heights, tyh, tyl, txh_t, txl_t, phi, lk, lb)
    return result.reshape(depth, m, width)


def solution(mesh):
    return jax.shard_map(
        per_device,
        mesh=mesh,
        in_specs=(P("growth", "lat", None), P("growth")),
        out_specs=P("growth", "lat", None),
        check_vma=False,
    )
```

```python
import functools
import math

import jax
import jax.numpy as jnp
import ml_dtypes
import numpy as np
from jax import lax
from jax.experimental import pallas as pl
from jax.experimental.pallas import tpu as pltpu
from jax.sharding import PartitionSpec as P

LANES = 128
PAIR = 256
LAG = 2
MESH = pl.DeviceIdType.MESH
VMEM_BYTES = 56 * 1024 * 1024


def cosine_table(points):
    ids = np.arange(points, dtype=np.int64)
    phase = (2 * ids[None, :] + 1) * ids[:, None] % (4 * points)
    scale = np.where(ids == 0, math.sqrt(1.0 / points), math.sqrt(2.0 / points))
    return scale[:, None] * np.cos(phase * (math.pi / (2.0 * points)))


def eigenvalues(ids, points):
    return 4.0 * np.sin(np.asarray(ids) * (math.pi / (2.0 * points))) ** 2


def two_parts(table):
    high = table.astype(ml_dtypes.bfloat16)
    low = (table - high.astype(np.float64)).astype(ml_dtypes.bfloat16)
    return jnp.asarray(high), jnp.asarray(low)


def split(value):
    high = value.astype(jnp.bfloat16)
    low = (value - high.astype(jnp.float32)).astype(jnp.bfloat16)
    return high, low


def dot3(a_high, a_low, b_high, b_low):
    dot = functools.partial(jnp.dot, preferred_element_type=jnp.float32)
    return dot(a_high, b_high) + (dot(a_low, b_high) + dot(a_high, b_low))


def reciprocal(x):
    guess = pl.reciprocal(x, approx=True)
    return guess * (2.0 - x * guess)


def fill_conduct(heights_ref, cond_ref):
    heights = heights_ref[...]
    zero = jnp.zeros((1, LANES), jnp.float32)
    cond_ref[...] = 2.0 / (
        jnp.concatenate([zero, heights], axis=0) + jnp.concatenate([heights, zero], axis=0)
    )


def row(ref, z):
    return ref[pl.ds(z, 1), :]


def inverse_pivot(cond_ref, heights_ref, z, eigen, behind, face):
    diagonal = (row(cond_ref, z) + row(cond_ref, z + 1)) + row(heights_ref, z) * eigen
    return reciprocal(diagonal - (face * face) * behind)


def forward_kernel(
    slabs, lanes_count, src_in, spacing, tyh_in, tyl_in, txh, txl, phi, lk, lb, lam_in,
    modal_out, jump_out, heights_out,
    src, spread, tyh, tyl, lam, heights, cond, xh, xl, f, inv_s, part_s, inv_high, from_low, from_high,
    to_low, to_high, ends, ends_in, jumps, jumps_all, k_inv, k_part, g_modes, g_cuts,
    g_send, g_in, sem_in, sem_h, sem_up, sem_down, sem_e, sem_r, sem_g,
):
    growth = lax.axis_index("growth")
    lat = lax.axis_index("lat")
    depth, m = f.shape[1], f.shape[2]
    half = m // 2
    nblk = f.shape[0]
    nz = slabs * depth
    width = src.shape[1]
    share = max(1, lanes_count // nblk)
    tiles = [slice(0, half), slice(half, m)]
    lag = LAG * (slabs - 1)

    loads = [
        pltpu.make_async_copy(a, b, sem_in.at[n])
        for n, (a, b) in enumerate(
            [(src_in, src), (tyh_in, tyh), (tyl_in, tyl), (lam_in, lam)]
        )
    ]
    for load in loads:
        load.start()
    for k in range(depth):
        spread[k : k + 1, :] = jnp.full((1, LANES), spacing[k], jnp.float32)

    barrier = pltpu.get_barrier_semaphore()
    for off in range(1, slabs):
        pl.semaphore_signal(
            barrier, inc=1, device_id=(lax.rem(growth + off, slabs), lat), device_id_type=MESH
        )
    for off in range(1, lanes_count):
        pl.semaphore_signal(
            barrier, inc=1, device_id=(growth, lax.rem(lat + off, lanes_count)),
            device_id_type=MESH,
        )
    pl.semaphore_wait(barrier, slabs + lanes_count - 2)

    def height_copy(off, owner, target):
        return pltpu.make_async_remote_copy(
            src_ref=spread,
            dst_ref=heights.at[pl.ds(owner * depth, depth)],
            send_sem=sem_h.at[0, off],
            recv_sem=sem_h.at[1, off],
            device_id=(target, lat),
            device_id_type=MESH,
        )

    for off in range(1, slabs):
        height_copy(off, growth, lax.rem(growth + off, slabs)).start()
    heights[pl.ds(growth * depth, depth), :] = spread[...]
    rows = src.shape[0]
    loads[0].wait()

    def split_rows(i, carry):
        at = pl.ds(pl.multiple_of(i * m, m), m)
        high, low = split(src[at, :])
        xh[at, :] = high
        xl[at, :] = low
        return carry

    lax.fori_loop(0, depth, split_rows, 0)
    for off in range(1, slabs):
        behind = lax.rem(growth + slabs - off, slabs)
        copy = height_copy(off, behind, lax.rem(growth + off, slabs))
        copy.wait_send()
        copy.wait_recv()
    fill_conduct(heights, cond)
    heights_out[...] = heights[...]
    for load in loads[1:]:
        load.wait()

    def eigen_of(i, tile):
        at = pl.ds(pl.multiple_of(i * LANES, LANES), LANES)
        return lk[tile, :] + lb[:, at]

    def pivots_below(i):
        eigen = [eigen_of(i, tile) for tile in tiles]
        zeros = tuple(jnp.zeros((half, LANES), jnp.float32) for _ in tiles)

        def up(z, inv):
            face = row(cond, z)
            return tuple(
                inverse_pivot(cond, heights, z, e, v, face) for e, v in zip(eigen, inv)
            )

        return list(lax.fori_loop(0, growth * depth, up, zeros))

    def pivots_above(i):
        eigen = [eigen_of(i, tile) for tile in tiles]
        zeros = tuple(jnp.zeros((half, LANES), jnp.float32) for _ in tiles)

        def down(k, inv):
            z = nz - 1 - k
            face = row(cond, z + 1)
            return tuple(
                inverse_pivot(cond, heights, z, e, v, face) for e, v in zip(eigen, inv)
            )

        return list(lax.fori_loop(0, nz - (growth + 1) * depth, down, zeros))

    @pl.when(growth == 0)
    def _():
        from_low[...] = jnp.zeros_like(from_low)

    @pl.when(growth == slabs - 1)
    def _():
        from_high[...] = jnp.zeros_like(from_high)

    first = growth * depth
    chunk = min(512, rows)
    planes = chunk // m

    def transform(pair):
        columns = pl.ds(pl.multiple_of(pair * PAIR, PAIR), PAIR)

        def one(c, carry):
            at = pl.ds(pl.multiple_of(c * chunk, chunk), chunk)
            along_y = dot3(xh[at, :], xl[at, :], tyh[:, columns], tyl[:, columns])
            high, low = split(along_y)
            for k in range(planes):
                part = slice(k * m, (k + 1) * m)
                both = dot3(txh[...], txl[...], high[part, :], low[part, :])
                for side in range(PAIR // LANES):
                    f[pair * (PAIR // LANES) + side, c * planes + k] = both[
                        :, side * LANES : (side + 1) * LANES
                    ]
            return carry

        lax.fori_loop(0, rows // chunk, one, 0)

    def up_copy(i):
        return pltpu.make_async_remote_copy(
            src_ref=to_high.at[i], dst_ref=from_low.at[i],
            send_sem=sem_up.at[0, i], recv_sem=sem_up.at[1, i],
            device_id=(lax.rem(growth + 1, slabs), lat), device_id_type=MESH,
        )

    def down_copy(i):
        return pltpu.make_async_remote_copy(
            src_ref=to_low.at[i], dst_ref=from_high.at[i],
            send_sem=sem_down.at[0, i], recv_sem=sem_down.at[1, i],
            device_id=(lax.rem(growth + slabs - 1, slabs), lat), device_id_type=MESH,
        )

    def sweep_up(i):
        inv = pivots_below(i)

        @pl.when(growth > 0)
        def _():
            up_copy(i).wait_recv()

        eigen = [eigen_of(i, tile) for tile in tiles]
        part = [from_low[i, tile, :] for tile in tiles]
        for k in range(depth):
            z = first + k
            face = row(cond, z)
            height = row(heights, z)
            for n, tile in enumerate(tiles):
                inv[n] = inverse_pivot(cond, heights, z, eigen[n], inv[n], face)
                part[n] = (height * f[i, k, tile, :] + face * part[n]) * inv[n]
                inv_s[i, k, tile, :] = inv[n]
                part_s[i, k, tile, :] = part[n]

        @pl.when(growth < slabs - 1)
        def _():
            for n, tile in enumerate(tiles):
                to_high[i, tile, :] = part[n]
            up_copy(i).start()

    def sweep_down(i):
        for tile, value in zip(tiles, pivots_above(i)):
            inv_high[i, tile, :] = value

        @pl.when(growth < slabs - 1)
        def _():
            down_copy(i).wait_recv()

        @pl.when(growth > 0)
        def _():
            eigen = [eigen_of(i, tile) for tile in tiles]
            inv = [inv_high[i, tile, :] for tile in tiles]
            part = [from_high[i, tile, :] for tile in tiles]
            for k in reversed(range(depth)):
                z = first + k
                face = row(cond, z + 1)
                height = row(heights, z)
                for n, tile in enumerate(tiles):
                    inv[n] = inverse_pivot(cond, heights, z, eigen[n], inv[n], face)
                    part[n] = (height * f[i, k, tile, :] + face * part[n]) * inv[n]
            for n, tile in enumerate(tiles):
                to_low[i, tile, :] = part[n]
            down_copy(i).start()

    def finish(i):
        face = row(cond, first + depth)
        value = []
        weight = [phi[tile, :] for tile in tiles]
        for n, tile in enumerate(tiles):
            inv = inv_s[i, depth - 1, tile, :]
            top = part_s[i, depth - 1, tile, :] + (face * inv) * from_high[i, tile, :]
            value.append(top * reciprocal(1.0 - (face * face) * inv * inv_high[i, tile, :]))
        for k in reversed(range(depth)):
            if k < depth - 1:
                face = row(cond, first + k + 1)
                for n, tile in enumerate(tiles):
                    value[n] = part_s[i, k, tile, :] + (face * inv_s[i, k, tile, :]) * value[n]
            sums = []
            for n, tile in enumerate(tiles):
                modal_out[i, k, tile, :] = value[n]
                sums.append(jnp.sum(weight[n] * value[n], axis=0, keepdims=True))
            ends[i, k : k + 1, :] = sums[0] + sums[1]
            ends[i, depth + k : depth + k + 1, :] = sums[0] - sums[1]

    per_pair = PAIR // LANES
    cuts = lanes_count - 1
    middle = nz // 2
    per_step = pl.cdiv(cuts, lag)

    def face_pivots(j):
        weight = [lam[j, tile, :] for tile in tiles]
        at = pl.ds(pl.multiple_of((lat // share) * LANES, LANES), LANES)
        eigen = [w + lb[:, at] for w in weight]
        low = [jnp.zeros((half, LANES), jnp.float32) for _ in tiles]
        high = list(low)
        for k in range(middle):
            face = row(cond, k)
            z = nz - 1 - k
            face_high = row(cond, z + 1)
            for n, tile in enumerate(tiles):
                low[n] = inverse_pivot(cond, heights, k, eigen[n], low[n], face)
                k_inv[j, k, tile, :] = low[n]
                high[n] = inverse_pivot(cond, heights, z, eigen[n], high[n], face_high)
                k_inv[j, z, tile, :] = high[n]

    def stage(tt, carry):
        @pl.when(tt < nblk // per_pair)
        def _():
            transform(tt)

        for side in range(per_pair):
            t = tt * per_pair + side
            up_i = t - LAG * growth
            down_i = t - LAG * (slabs - 1 - growth)
            end_i = t - lag

            for n in range(per_step):
                j = (t - nblk) * per_step + n
                pl.when((j >= 0) & (j < cuts))(functools.partial(face_pivots, j))

            @pl.when((up_i >= 0) & (up_i < nblk))
            def _():
                sweep_up(up_i)

            @pl.when((down_i >= 0) & (down_i < nblk))
            def _():
                sweep_down(down_i)

            @pl.when((end_i >= 0) & (end_i < nblk))
            def _():
                finish(end_i)

        return carry

    lax.fori_loop(0, pl.cdiv(nblk + lag, per_pair), stage, 0)

    def block_of(rank):
        return rank // share

    def ends_copy(off, owner, target):
        return pltpu.make_async_remote_copy(
            src_ref=ends.at[block_of(target)], dst_ref=ends_in.at[owner],
            send_sem=sem_e.at[0, off], recv_sem=sem_e.at[1, off],
            device_id=(growth, target), device_id_type=MESH,
        )

    for off in range(1, lanes_count):
        ends_copy(off, lat, lax.rem(lat + off, lanes_count)).start()
    ends_in[lat] = ends[block_of(lat)]

    def drain(i, carry):
        @pl.when(growth < slabs - 1)
        def _():
            up_copy(i).wait_send()

        @pl.when(growth > 0)
        def _():
            down_copy(i).wait_send()

        return carry

    lax.fori_loop(0, nblk, drain, 0)
    for off in range(1, lanes_count):
        copy = ends_copy(
            off, lax.rem(lat + lanes_count - off, lanes_count), lax.rem(lat + off, lanes_count)
        )
        copy.wait_send()
        copy.wait_recv()

    sines = [
        [
            math.sqrt(2.0 / lanes_count) * math.sin(math.pi * (c + 1) * (j + 1) / lanes_count)
            for j in range(cuts)
        ]
        for c in range(cuts)
    ]
    jump = [ends_in[c, depth:, :] - ends_in[c + 1, :depth, :] for c in range(cuts)]
    for j in range(cuts):
        total = jump[0] * sines[0][j]
        for c in range(1, cuts):
            total += jump[c] * sines[c][j]
        jumps[j] = total
    jumps_all[growth] = jumps[...]

    def jumps_copy(off, owner, target):
        return pltpu.make_async_remote_copy(
            src_ref=jumps, dst_ref=jumps_all.at[owner],
            send_sem=sem_r.at[0, off], recv_sem=sem_r.at[1, off],
            device_id=(target, lat), device_id_type=MESH,
        )

    for off in range(1, slabs):
        jumps_copy(off, growth, lax.rem(growth + off, slabs)).start()
    for off in range(1, slabs):
        copy = jumps_copy(
            off, lax.rem(growth + slabs - off, slabs), lax.rem(growth + off, slabs)
        )
        copy.wait_send()
        copy.wait_recv()

    def correct(j, carry):
        def held(z):
            return jumps_all[z // depth, j, z % depth : z % depth + 1, :]

        weight = [lam[j, tile, :] for tile in tiles]
        low = [jnp.zeros((half, LANES), jnp.float32) for _ in tiles]
        high = list(low)
        for k in range(middle):
            z = nz - 1 - k
            face = row(cond, k)
            right = row(heights, k) * held(k)
            face_high = row(cond, z + 1)
            right_high = row(heights, z) * held(z)
            for n, tile in enumerate(tiles):
                low[n] = (right + face * low[n]) * k_inv[j, k, tile, :]
                k_part[k, tile, :] = low[n]
                high[n] = (right_high + face_high * high[n]) * k_inv[j, z, tile, :]
                k_part[z, tile, :] = high[n]

        def put(z, value):
            total = sum(
                jnp.sum(w * v, axis=0, keepdims=True) for w, v in zip(weight, value)
            )
            g_modes[j, z : z + 1, :] = held(z) - total * (1.0 / m)

        face = row(cond, middle)
        below, above = [], []
        for n, tile in enumerate(tiles):
            inv_a = face * k_inv[j, middle - 1, tile, :]
            inv_b = face * k_inv[j, middle, tile, :]
            below.append((low[n] + inv_a * high[n]) * reciprocal(1.0 - inv_a * inv_b))
            above.append(high[n] + inv_b * below[n])
        put(middle - 1, below)
        put(middle, above)
        for k in range(1, middle):
            z = middle - 1 - k
            face = row(cond, z + 1)
            for n, tile in enumerate(tiles):
                below[n] = k_part[z, tile, :] + (face * k_inv[j, z, tile, :]) * below[n]
            put(z, below)
            z = middle + k
            face = row(cond, z)
            for n, tile in enumerate(tiles):
                above[n] = k_part[z, tile, :] + (face * k_inv[j, z, tile, :]) * above[n]
            put(z, above)
        return carry

    lax.fori_loop(0, cuts, correct, 0)

    for c in range(cuts):
        total = g_modes[0] * sines[c][0]
        for j in range(1, cuts):
            total += g_modes[j] * sines[c][j]
        g_cuts[c] = total
    for d in range(lanes_count):
        low = g_cuts[d - 1] if d > 0 else jnp.zeros((nz, LANES), jnp.float32)
        high = g_cuts[d] if d < cuts else jnp.zeros((nz, LANES), jnp.float32)
        g_send[d, 0] = high - low
        g_send[d, 1] = -(high + low)

    def g_copy(off, owner, target):
        return pltpu.make_async_remote_copy(
            src_ref=g_send.at[target], dst_ref=g_in.at[block_of(owner)],
            send_sem=sem_g.at[0, off], recv_sem=sem_g.at[1, off],
            device_id=(growth, target), device_id_type=MESH,
        )

    def speaks(rank, act):
        if share == 1:
            act()
        else:
            pl.when(lax.rem(rank, share) == 0)(act)

    def own_block():
        g_in[block_of(lat)] = g_send[lat]

    for off in range(1, lanes_count):
        copy = g_copy(off, lat, lax.rem(lat + off, lanes_count))
        speaks(lat, copy.start)
    speaks(lat, own_block)
    for off in range(1, lanes_count):
        owner = lax.rem(lat + lanes_count - off, lanes_count)
        target = lax.rem(lat + off, lanes_count)
        speaks(lat, g_copy(off, lat, target).wait_send)
        speaks(owner, g_copy(off, owner, target).wait_recv)
    jump_out[...] = g_in[...]


def inverse_kernel(
    slabs, modal_in, jump, heights, tyh_in, tyl_in, txh, txl, phi, lk, lb,
    out_hbm,
    modal, tyh, tyl, out, sem_in, sem_out, cond, inv_s, part_s, mh, ml, gh, gl,
):
    growth = lax.axis_index("growth")
    nblk, depth, m = modal.shape[:3]
    per_pair = PAIR // LANES
    pairs = nblk // per_pair
    for n in range(pairs):
        part = pl.ds(n * per_pair, per_pair)
        pltpu.make_async_copy(modal_in.at[part], modal.at[part], sem_in.at[n]).start()
    tables = [
        pltpu.make_async_copy(tyh_in, tyh, sem_in.at[pairs]),
        pltpu.make_async_copy(tyl_in, tyl, sem_in.at[pairs + 1]),
    ]
    for load in tables:
        load.start()
    half = m // 2
    nz = slabs * depth
    tiles = [slice(0, half), slice(half, m)]
    first = growth * depth
    fill_conduct(heights, cond)

    def correct(i, side):
        at = pl.ds(pl.multiple_of(i * LANES, LANES), LANES)
        eigen = [lk[tile, :] + lb[:, at] for tile in tiles]
        zero = jnp.zeros((half, LANES), jnp.float32)

        def advance(z, face, state):
            height = row(heights, z)
            new = []
            for n in range(2):
                inv, part = state[2 * n], state[2 * n + 1]
                inv = inverse_pivot(cond, heights, z, eigen[n], inv, face)
                right = height * jump[i, n, pl.ds(z, 1), :]
                new += [inv, (right + face * part) * inv]
            return tuple(new)

        def up(z, state):
            return advance(z, row(cond, z), state)

        def down(k, state):
            z = nz - 1 - k
            return advance(z, row(cond, z + 1), state)

        high = lax.fori_loop(0, nz - first - depth, down, (zero,) * 4)
        state = lax.fori_loop(0, first, up, (zero,) * 4)
        for k in range(depth):
            state = up(first + k, state)
            for n, tile in enumerate(tiles):
                inv_s[k, tile, :] = state[2 * n]
                part_s[k, tile, :] = state[2 * n + 1]
        face = row(cond, first + depth)
        value = []
        for n in range(2):
            inv, part = state[2 * n], state[2 * n + 1]
            top = part + (face * inv) * high[2 * n + 1]
            value.append(top * reciprocal(1.0 - (face * face) * inv * high[2 * n]))
        for k in reversed(range(depth)):
            if k < depth - 1:
                face = row(cond, first + k + 1)
            for n, tile in enumerate(tiles):
                if k < depth - 1:
                    value[n] = part_s[k, tile, :] + (face * inv_s[k, tile, :]) * value[n]
                a, b = split(modal[i, k, tile, :] - phi[tile, :] * value[n])
                columns = slice(side * LANES, (side + 1) * LANES)
                mh[k, tile, columns] = a
                ml[k, tile, columns] = b

    def pair(tt, carry):
        part = pl.ds(tt * per_pair, per_pair)
        pltpu.make_async_copy(modal_in.at[part], modal.at[part], sem_in.at[tt]).wait()
        for side in range(per_pair):
            correct(tt * per_pair + side, side)
        columns = pl.ds(pl.multiple_of(tt * PAIR, PAIR), PAIR)
        for k in range(depth):
            a, b = split(dot3(txh[...], txl[...], mh[k], ml[k]))
            gh[k * m : (k + 1) * m, columns] = a
            gl[k * m : (k + 1) * m, columns] = b
        return carry

    lax.fori_loop(0, pairs, pair, 0)
    for load in tables:
        load.wait()

    rows = gh.shape[0]
    chunk = min(512, rows)
    width = out.shape[1]

    def columns_of(c, carry):
        columns = pl.ds(pl.multiple_of(c * PAIR, PAIR), PAIR)

        def rows_of(r, inner):
            at = pl.ds(pl.multiple_of(r * chunk, chunk), chunk)
            out[at, columns] = dot3(gh[at, :], gl[at, :], tyh[:, columns], tyl[:, columns])
            return inner

        lax.fori_loop(0, rows // chunk, rows_of, 0)
        store(columns, c).start()
        return carry

    def store(columns, c):
        return pltpu.make_async_copy(out.at[:, columns], out_hbm.at[:, columns], sem_out.at[c])

    lax.fori_loop(0, width // PAIR, columns_of, 0)
    for c in range(width // PAIR):
        store(slice(c * PAIR, (c + 1) * PAIR), c).wait()


def per_device(source, spacing):
    depth, m, width = source.shape
    lanes_count = lax.axis_size("lat")
    slabs = lax.axis_size("growth")
    nz = slabs * depth
    points = m * lanes_count
    nblk = width // LANES
    cuts = lanes_count - 1
    f32 = jnp.float32

    order = np.concatenate([np.arange(0, m, 2), np.arange(1, m, 2)])
    local = cosine_table(m)[order]
    along_y = cosine_table(width)
    tyh_t, tyl_t = two_parts(np.ascontiguousarray(along_y.T))
    tyh, tyl = two_parts(along_y)
    txh, txl = two_parts(local)
    txh_t, txl_t = two_parts(np.ascontiguousarray(local.T))

    def spread_lanes(column):
        return jnp.asarray(np.repeat(np.asarray(column, np.float32)[..., None], LANES, axis=-1))

    phi = spread_lanes(local[:, 0])
    lk = spread_lanes(eigenvalues(order, m))
    lb = jnp.asarray(eigenvalues(np.arange(width), width).astype(np.float32)[None, :])
    folds = []
    for j in range(1, lanes_count):
        ids = [k for k in range(1, points) if k % (2 * lanes_count) in (j, 2 * lanes_count - j)]
        folds.append(eigenvalues(ids, points))
    lam = spread_lanes(np.stack(folds))

    flat = source.reshape(depth * m, width)
    vmem = pl.BlockSpec(memory_space=pltpu.VMEM)
    smem = pl.BlockSpec(memory_space=pltpu.SMEM)
    anywhere = pl.BlockSpec(memory_space=pl.ANY)
    dma = pltpu.SemaphoreType.DMA
    V = pltpu.VMEM
    modal, jump, heights = pl.pallas_call(
        functools.partial(forward_kernel, slabs, lanes_count),
        out_shape=(
            jax.ShapeDtypeStruct((nblk, depth, m, LANES), f32),
            jax.ShapeDtypeStruct((nblk, 2, nz, LANES), f32),
            jax.ShapeDtypeStruct((nz, LANES), f32),
        ),
        in_specs=[anywhere, smem, anywhere, anywhere] + [vmem] * 5 + [anywhere],
        out_specs=(vmem, vmem, vmem),
        scratch_shapes=[
            V((depth * m, width), f32),
            V((depth, LANES), f32),
            V((width, width), jnp.bfloat16),
            V((width, width), jnp.bfloat16),
            V((cuts, m, LANES), f32),
            V((nz, LANES), f32),
            V((nz + 1, LANES), f32),
            V((depth * m, width), jnp.bfloat16),
            V((depth * m, width), jnp.bfloat16),
            V((nblk, depth, m, LANES), f32),
            V((nblk, depth, m, LANES), f32),
            V((nblk, depth, m, LANES), f32),
            V((nblk, m, LANES), f32),
            V((nblk, m, LANES), f32),
            V((nblk, m, LANES), f32),
            V((nblk, m, LANES), f32),
            V((nblk, m, LANES), f32),
            V((nblk, 2 * depth, LANES), f32),
            V((lanes_count, 2 * depth, LANES), f32),
            V((cuts, depth, LANES), f32),
            V((slabs, cuts, depth, LANES), f32),
            V((cuts, nz, m, LANES), f32),
            V((nz, m, LANES), f32),
            V((cuts, nz, LANES), f32),
            V((cuts, nz, LANES), f32),
            V((lanes_count, 2, nz, LANES), f32),
            V((nblk, 2, nz, LANES), f32),
            dma((4,)),
            dma((2, slabs)),
            dma((2, nblk)),
            dma((2, nblk)),
            dma((2, lanes_count)),
            dma((2, slabs)),
            dma((2, lanes_count)),
        ],
        compiler_params=pltpu.CompilerParams(
            collective_id=0, has_side_effects=True, vmem_limit_bytes=VMEM_BYTES
        ),
        name="slab_solve",
    )(flat, spacing, tyh_t, tyl_t, txh, txl, phi, lk, lb, lam)

    result = pl.pallas_call(
        functools.partial(inverse_kernel, slabs),
        out_shape=jax.ShapeDtypeStruct((depth * m, width), f32),
        in_specs=[anywhere, vmem, vmem, anywhere, anywhere] + [vmem] * 5,
        out_specs=anywhere,
        scratch_shapes=[
            V((nblk, depth, m, LANES), f32),
            V((width, width), jnp.bfloat16),
            V((width, width), jnp.bfloat16),
            V((depth * m, width), f32),
            dma((width // PAIR + 2,)),
            dma((width // PAIR,)),
            V((nz + 1, LANES), f32),
            V((depth, m, LANES), f32),
            V((depth, m, LANES), f32),
            V((depth, m, PAIR), jnp.bfloat16),
            V((depth, m, PAIR), jnp.bfloat16),
            V((depth * m, width), jnp.bfloat16),
            V((depth * m, width), jnp.bfloat16),
        ],
        compiler_params=pltpu.CompilerParams(vmem_limit_bytes=VMEM_BYTES),
        name="face_correction",
    )(modal, jump, heights, tyh, tyl, txh_t, txl_t, phi, lk, lb)
    return result.reshape(depth, m, width)


def solution(mesh):
    return jax.shard_map(
        per_device,
        mesh=mesh,
        in_specs=(P("growth", "lat", None), P("growth")),
        out_specs=P("growth", "lat", None),
        check_vma=False,
    )
```

```python
import functools
import math

import jax
import jax.numpy as jnp
import ml_dtypes
import numpy as np
from jax import lax
from jax.experimental import pallas as pl
from jax.experimental.pallas import tpu as pltpu
from jax.sharding import PartitionSpec as P

LANES = 128
PAIR = 256
LAG = 2
MESH = pl.DeviceIdType.MESH
VMEM_BYTES = 56 * 1024 * 1024


def cosine_table(points):
    ids = np.arange(points, dtype=np.int64)
    phase = (2 * ids[None, :] + 1) * ids[:, None] % (4 * points)
    scale = np.where(ids == 0, math.sqrt(1.0 / points), math.sqrt(2.0 / points))
    return scale[:, None] * np.cos(phase * (math.pi / (2.0 * points)))


def eigenvalues(ids, points):
    return 4.0 * np.sin(np.asarray(ids) * (math.pi / (2.0 * points))) ** 2


def two_parts(table):
    high = table.astype(ml_dtypes.bfloat16)
    low = (table - high.astype(np.float64)).astype(ml_dtypes.bfloat16)
    return high, low


def left_parts(table):
    high, low = two_parts(table)
    return jnp.asarray(np.concatenate([high, low, high], axis=-1))


def right_parts(table):
    high, low = two_parts(table)
    return jnp.asarray(np.concatenate([high, high, low], axis=-2))


def mirror(value):
    lanes = lax.broadcasted_iota(jnp.int32, value.shape, 1)
    return jnp.take_along_axis(value, LANES - 1 - lanes, axis=1, mode="promise_in_bounds")


def split(value):
    high = value.astype(jnp.bfloat16)
    low = (value - high.astype(jnp.float32)).astype(jnp.bfloat16)
    return high, low


def dot(a, b):
    return jnp.dot(a, b, preferred_element_type=jnp.float32)


def stacked(value):
    high, low = split(value)
    return jnp.concatenate([high, high, low], axis=0)


def reciprocal(x):
    guess = pl.reciprocal(x, approx=True)
    return guess * (2.0 - x * guess)


def fill_conduct(heights_ref, cond_ref):
    heights = heights_ref[...]
    zero = jnp.zeros((1, LANES), jnp.float32)
    cond_ref[...] = 2.0 / (
        jnp.concatenate([zero, heights], axis=0) + jnp.concatenate([heights, zero], axis=0)
    )


def row(ref, z):
    return ref[pl.ds(z, 1), :]


def inverse_pivot(cond_ref, heights_ref, z, eigen, behind, face):
    diagonal = (row(cond_ref, z) + row(cond_ref, z + 1)) + row(heights_ref, z) * eigen
    return reciprocal(diagonal - (face * face) * behind)


def forward_kernel(
    slabs, lanes_count, src_in, spacing, ty_in, tx, phi, lk, lb, lam_in,
    modal_out, jump_out, heights_out,
    src, spread, ty, lam, heights, cond, x3, f, inv_s, part_s, inv_high, from_low, from_high,
    to_low, to_high, ends, ends_in, jumps, jumps_all, k_inv, k_part, g_modes, g_cuts,
    g_send, g_in, sem_in, sem_h, sem_up, sem_down, sem_e, sem_r, sem_g,
):
    growth = lax.axis_index("growth")
    lat = lax.axis_index("lat")
    depth, m = f.shape[1], f.shape[2]
    half = m // 2
    nblk = f.shape[0]
    nz = slabs * depth
    width = src.shape[1]
    share = max(1, lanes_count // nblk)
    tiles = [slice(0, half), slice(half, m)]
    lag = LAG * (slabs - 1)

    loads = [
        pltpu.make_async_copy(a, b, sem_in.at[n])
        for n, (a, b) in enumerate(
            [(src_in, src), (ty_in, ty), (lam_in, lam)]
        )
    ]
    for load in loads:
        load.start()
    for k in range(depth):
        spread[k : k + 1, :] = jnp.full((1, LANES), spacing[k], jnp.float32)

    barrier = pltpu.get_barrier_semaphore()
    for off in range(1, slabs):
        pl.semaphore_signal(
            barrier, inc=1, device_id=(lax.rem(growth + off, slabs), lat), device_id_type=MESH
        )
    for off in range(1, lanes_count):
        pl.semaphore_signal(
            barrier, inc=1, device_id=(growth, lax.rem(lat + off, lanes_count)),
            device_id_type=MESH,
        )
    pl.semaphore_wait(barrier, slabs + lanes_count - 2)

    def height_copy(off, owner, target):
        return pltpu.make_async_remote_copy(
            src_ref=spread,
            dst_ref=heights.at[pl.ds(owner * depth, depth)],
            send_sem=sem_h.at[0, off],
            recv_sem=sem_h.at[1, off],
            device_id=(target, lat),
            device_id_type=MESH,
        )

    for off in range(1, slabs):
        height_copy(off, growth, lax.rem(growth + off, slabs)).start()
    heights[pl.ds(growth * depth, depth), :] = spread[...]
    rows = src.shape[0]
    loads[0].wait()

    mid = width // 2

    def split_rows(i, carry):
        at = pl.ds(pl.multiple_of(i * m, m), m)
        for q in range(mid // LANES):
            near = src[at, q * LANES : (q + 1) * LANES]
            far = mirror(src[at, width - (q + 1) * LANES : width - q * LANES])
            for n, value in enumerate((near + far, near - far)):
                high, low = split(value)
                for place, part in enumerate((high, low, high)):
                    start = place * mid + q * LANES
                    x3[n, at, start : start + LANES] = part
        return carry

    lax.fori_loop(0, depth, split_rows, 0)
    for off in range(1, slabs):
        behind = lax.rem(growth + slabs - off, slabs)
        copy = height_copy(off, behind, lax.rem(growth + off, slabs))
        copy.wait_send()
        copy.wait_recv()
    fill_conduct(heights, cond)
    heights_out[...] = heights[...]
    for load in loads[1:]:
        load.wait()

    def eigen_of(i, tile):
        at = pl.ds(pl.multiple_of(i * LANES, LANES), LANES)
        return lk[tile, :] + lb[:, at]

    def pivots_below(i):
        eigen = [eigen_of(i, tile) for tile in tiles]
        zeros = tuple(jnp.zeros((half, LANES), jnp.float32) for _ in tiles)

        def up(z, inv):
            face = row(cond, z)
            return tuple(
                inverse_pivot(cond, heights, z, e, v, face) for e, v in zip(eigen, inv)
            )

        return list(lax.fori_loop(0, growth * depth, up, zeros))

    def pivots_above(i):
        eigen = [eigen_of(i, tile) for tile in tiles]
        zeros = tuple(jnp.zeros((half, LANES), jnp.float32) for _ in tiles)

        def down(k, inv):
            z = nz - 1 - k
            face = row(cond, z + 1)
            return tuple(
                inverse_pivot(cond, heights, z, e, v, face) for e, v in zip(eigen, inv)
            )

        return list(lax.fori_loop(0, nz - (growth + 1) * depth, down, zeros))

    @pl.when(growth == 0)
    def _():
        from_low[...] = jnp.zeros_like(from_low)

    @pl.when(growth == slabs - 1)
    def _():
        from_high[...] = jnp.zeros_like(from_high)

    first = growth * depth
    chunk = min(512, rows)
    planes = chunk // m

    half_pairs = mid // PAIR

    def transform(pair):
        parity = pair // half_pairs
        columns = pl.ds(pl.multiple_of(lax.rem(pair, half_pairs) * PAIR, PAIR), PAIR)

        def one(c, carry):
            at = pl.ds(pl.multiple_of(c * chunk, chunk), chunk)
            along_y = dot(x3[parity, at, :], ty[parity, :, columns])
            for k in range(planes):
                part = slice(k * m, (k + 1) * m)
                both = dot(tx[...], stacked(along_y[part, :]))
                for side in range(PAIR // LANES):
                    f[pair * (PAIR // LANES) + side, c * planes + k] = both[
                        :, side * LANES : (side + 1) * LANES
                    ]
            return carry

        lax.fori_loop(0, rows // chunk, one, 0)

    def up_copy(i):
        return pltpu.make_async_remote_copy(
            src_ref=to_high.at[i], dst_ref=from_low.at[i],
            send_sem=sem_up.at[0, i], recv_sem=sem_up.at[1, i],
            device_id=(lax.rem(growth + 1, slabs), lat), device_id_type=MESH,
        )

    def down_copy(i):
        return pltpu.make_async_remote_copy(
            src_ref=to_low.at[i], dst_ref=from_high.at[i],
            send_sem=sem_down.at[0, i], recv_sem=sem_down.at[1, i],
            device_id=(lax.rem(growth + slabs - 1, slabs), lat), device_id_type=MESH,
        )

    def sweep_up(i):
        inv = pivots_below(i)

        @pl.when(growth > 0)
        def _():
            up_copy(i).wait_recv()

        eigen = [eigen_of(i, tile) for tile in tiles]
        part = [from_low[i, tile, :] for tile in tiles]
        for k in range(depth):
            z = first + k
            face = row(cond, z)
            height = row(heights, z)
            for n, tile in enumerate(tiles):
                inv[n] = inverse_pivot(cond, heights, z, eigen[n], inv[n], face)
                part[n] = (height * f[i, k, tile, :] + face * part[n]) * inv[n]
                inv_s[i, k, tile, :] = inv[n]
                part_s[i, k, tile, :] = part[n]

        @pl.when(growth < slabs - 1)
        def _():
            for n, tile in enumerate(tiles):
                to_high[i, tile, :] = part[n]
            up_copy(i).start()

    def sweep_down(i):
        for tile, value in zip(tiles, pivots_above(i)):
            inv_high[i, tile, :] = value

        @pl.when(growth < slabs - 1)
        def _():
            down_copy(i).wait_recv()

        @pl.when(growth > 0)
        def _():
            eigen = [eigen_of(i, tile) for tile in tiles]
            inv = [inv_high[i, tile, :] for tile in tiles]
            part = [from_high[i, tile, :] for tile in tiles]
            for k in reversed(range(depth)):
                z = first + k
                face = row(cond, z + 1)
                height = row(heights, z)
                for n, tile in enumerate(tiles):
                    inv[n] = inverse_pivot(cond, heights, z, eigen[n], inv[n], face)
                    part[n] = (height * f[i, k, tile, :] + face * part[n]) * inv[n]
            for n, tile in enumerate(tiles):
                to_low[i, tile, :] = part[n]
            down_copy(i).start()

    def finish(i):
        face = row(cond, first + depth)
        value = []
        weight = [phi[tile, :] for tile in tiles]
        for n, tile in enumerate(tiles):
            inv = inv_s[i, depth - 1, tile, :]
            top = part_s[i, depth - 1, tile, :] + (face * inv) * from_high[i, tile, :]
            value.append(top * reciprocal(1.0 - (face * face) * inv * inv_high[i, tile, :]))
        for k in reversed(range(depth)):
            if k < depth - 1:
                face = row(cond, first + k + 1)
                for n, tile in enumerate(tiles):
                    value[n] = part_s[i, k, tile, :] + (face * inv_s[i, k, tile, :]) * value[n]
            sums = []
            for n, tile in enumerate(tiles):
                modal_out[i, k, tile, :] = value[n]
                sums.append(jnp.sum(weight[n] * value[n], axis=0, keepdims=True))
            ends[i, k : k + 1, :] = sums[0] + sums[1]
            ends[i, depth + k : depth + k + 1, :] = sums[0] - sums[1]

    per_pair = PAIR // LANES
    cuts = lanes_count - 1
    middle = nz // 2
    per_step = pl.cdiv(cuts, lag)

    def face_pivots(j):
        weight = [lam[j, tile, :] for tile in tiles]
        at = pl.ds(pl.multiple_of((lat // share) * LANES, LANES), LANES)
        eigen = [w + lb[:, at] for w in weight]
        low = [jnp.zeros((half, LANES), jnp.float32) for _ in tiles]
        high = list(low)
        for k in range(middle):
            face = row(cond, k)
            z = nz - 1 - k
            face_high = row(cond, z + 1)
            for n, tile in enumerate(tiles):
                low[n] = inverse_pivot(cond, heights, k, eigen[n], low[n], face)
                k_inv[j, k, tile, :] = low[n]
                high[n] = inverse_pivot(cond, heights, z, eigen[n], high[n], face_high)
                k_inv[j, z, tile, :] = high[n]

    def stage(tt, carry):
        @pl.when(tt < nblk // per_pair)
        def _():
            transform(tt)

        for side in range(per_pair):
            t = tt * per_pair + side
            up_i = t - LAG * growth
            down_i = t - LAG * (slabs - 1 - growth)
            end_i = t - lag

            for n in range(per_step):
                j = (t - nblk) * per_step + n
                pl.when((j >= 0) & (j < cuts))(functools.partial(face_pivots, j))

            @pl.when((up_i >= 0) & (up_i < nblk))
            def _():
                sweep_up(up_i)

            @pl.when((down_i >= 0) & (down_i < nblk))
            def _():
                sweep_down(down_i)

            @pl.when((end_i >= 0) & (end_i < nblk))
            def _():
                finish(end_i)

        return carry

    lax.fori_loop(0, pl.cdiv(nblk + lag, per_pair), stage, 0)

    def block_of(rank):
        return rank // share

    def ends_copy(off, owner, target):
        return pltpu.make_async_remote_copy(
            src_ref=ends.at[block_of(target)], dst_ref=ends_in.at[owner],
            send_sem=sem_e.at[0, off], recv_sem=sem_e.at[1, off],
            device_id=(growth, target), device_id_type=MESH,
        )

    for off in range(1, lanes_count):
        ends_copy(off, lat, lax.rem(lat + off, lanes_count)).start()
    ends_in[lat] = ends[block_of(lat)]

    def drain(i, carry):
        @pl.when(growth < slabs - 1)
        def _():
            up_copy(i).wait_send()

        @pl.when(growth > 0)
        def _():
            down_copy(i).wait_send()

        return carry

    lax.fori_loop(0, nblk, drain, 0)
    for off in range(1, lanes_count):
        copy = ends_copy(
            off, lax.rem(lat + lanes_count - off, lanes_count), lax.rem(lat + off, lanes_count)
        )
        copy.wait_send()
        copy.wait_recv()

    sines = [
        [
            math.sqrt(2.0 / lanes_count) * math.sin(math.pi * (c + 1) * (j + 1) / lanes_count)
            for j in range(cuts)
        ]
        for c in range(cuts)
    ]
    jump = [ends_in[c, depth:, :] - ends_in[c + 1, :depth, :] for c in range(cuts)]
    for j in range(cuts):
        total = jump[0] * sines[0][j]
        for c in range(1, cuts):
            total += jump[c] * sines[c][j]
        jumps[j] = total
    jumps_all[growth] = jumps[...]

    def jumps_copy(off, owner, target):
        return pltpu.make_async_remote_copy(
            src_ref=jumps, dst_ref=jumps_all.at[owner],
            send_sem=sem_r.at[0, off], recv_sem=sem_r.at[1, off],
            device_id=(target, lat), device_id_type=MESH,
        )

    for off in range(1, slabs):
        jumps_copy(off, growth, lax.rem(growth + off, slabs)).start()
    for off in range(1, slabs):
        copy = jumps_copy(
            off, lax.rem(growth + slabs - off, slabs), lax.rem(growth + off, slabs)
        )
        copy.wait_send()
        copy.wait_recv()

    def correct(j, carry):
        def held(z):
            return jumps_all[z // depth, j, z % depth : z % depth + 1, :]

        weight = [lam[j, tile, :] for tile in tiles]
        low = [jnp.zeros((half, LANES), jnp.float32) for _ in tiles]
        high = list(low)
        for k in range(middle):
            z = nz - 1 - k
            face = row(cond, k)
            right = row(heights, k) * held(k)
            face_high = row(cond, z + 1)
            right_high = row(heights, z) * held(z)
            for n, tile in enumerate(tiles):
                low[n] = (right + face * low[n]) * k_inv[j, k, tile, :]
                k_part[k, tile, :] = low[n]
                high[n] = (right_high + face_high * high[n]) * k_inv[j, z, tile, :]
                k_part[z, tile, :] = high[n]

        def put(z, value):
            total = sum(
                jnp.sum(w * v, axis=0, keepdims=True) for w, v in zip(weight, value)
            )
            g_modes[j, z : z + 1, :] = held(z) - total * (1.0 / m)

        face = row(cond, middle)
        below, above = [], []
        for n, tile in enumerate(tiles):
            inv_a = face * k_inv[j, middle - 1, tile, :]
            inv_b = face * k_inv[j, middle, tile, :]
            below.append((low[n] + inv_a * high[n]) * reciprocal(1.0 - inv_a * inv_b))
            above.append(high[n] + inv_b * below[n])
        put(middle - 1, below)
        put(middle, above)
        for k in range(1, middle):
            z = middle - 1 - k
            face = row(cond, z + 1)
            for n, tile in enumerate(tiles):
                below[n] = k_part[z, tile, :] + (face * k_inv[j, z, tile, :]) * below[n]
            put(z, below)
            z = middle + k
            face = row(cond, z)
            for n, tile in enumerate(tiles):
                above[n] = k_part[z, tile, :] + (face * k_inv[j, z, tile, :]) * above[n]
            put(z, above)
        return carry

    lax.fori_loop(0, cuts, correct, 0)

    for c in range(cuts):
        total = g_modes[0] * sines[c][0]
        for j in range(1, cuts):
            total += g_modes[j] * sines[c][j]
        g_cuts[c] = total
    for d in range(lanes_count):
        low = g_cuts[d - 1] if d > 0 else jnp.zeros((nz, LANES), jnp.float32)
        high = g_cuts[d] if d < cuts else jnp.zeros((nz, LANES), jnp.float32)
        g_send[d, 0] = high - low
        g_send[d, 1] = -(high + low)

    def g_copy(off, owner, target):
        return pltpu.make_async_remote_copy(
            src_ref=g_send.at[target], dst_ref=g_in.at[block_of(owner)],
            send_sem=sem_g.at[0, off], recv_sem=sem_g.at[1, off],
            device_id=(growth, target), device_id_type=MESH,
        )

    def speaks(rank, act):
        if share == 1:
            act()
        else:
            pl.when(lax.rem(rank, share) == 0)(act)

    def own_block():
        g_in[block_of(lat)] = g_send[lat]

    for off in range(1, lanes_count):
        copy = g_copy(off, lat, lax.rem(lat + off, lanes_count))
        speaks(lat, copy.start)
    speaks(lat, own_block)
    for off in range(1, lanes_count):
        owner = lax.rem(lat + lanes_count - off, lanes_count)
        target = lax.rem(lat + off, lanes_count)
        speaks(lat, g_copy(off, lat, target).wait_send)
        speaks(owner, g_copy(off, owner, target).wait_recv)
    jump_out[...] = g_in[...]


def inverse_kernel(
    slabs, modal_in, jump, heights, ty_in, tx, phi, lk, lb,
    out_hbm,
    modal, ty, out, sem_in, sem_out, cond, inv_s, part_s, m3, g3,
):
    growth = lax.axis_index("growth")
    nblk, depth, m = modal.shape[:3]
    per_pair = PAIR // LANES
    pairs = nblk // per_pair
    for n in range(pairs):
        part = pl.ds(n * per_pair, per_pair)
        pltpu.make_async_copy(modal_in.at[part], modal.at[part], sem_in.at[n]).start()
    table = pltpu.make_async_copy(ty_in, ty, sem_in.at[pairs])
    table.start()
    half = m // 2
    nz = slabs * depth
    tiles = [slice(0, half), slice(half, m)]
    first = growth * depth
    fill_conduct(heights, cond)

    def correct(i, side):
        at = pl.ds(pl.multiple_of(i * LANES, LANES), LANES)
        eigen = [lk[tile, :] + lb[:, at] for tile in tiles]
        zero = jnp.zeros((half, LANES), jnp.float32)

        def advance(z, face, state):
            height = row(heights, z)
            new = []
            for n in range(2):
                inv, part = state[2 * n], state[2 * n + 1]
                inv = inverse_pivot(cond, heights, z, eigen[n], inv, face)
                right = height * jump[i, n, pl.ds(z, 1), :]
                new += [inv, (right + face * part) * inv]
            return tuple(new)

        def up(z, state):
            return advance(z, row(cond, z), state)

        def down(k, state):
            z = nz - 1 - k
            return advance(z, row(cond, z + 1), state)

        high = lax.fori_loop(0, nz - first - depth, down, (zero,) * 4)
        state = lax.fori_loop(0, first, up, (zero,) * 4)
        for k in range(depth):
            state = up(first + k, state)
            for n, tile in enumerate(tiles):
                inv_s[k, tile, :] = state[2 * n]
                part_s[k, tile, :] = state[2 * n + 1]
        face = row(cond, first + depth)
        value = []
        for n in range(2):
            inv, part = state[2 * n], state[2 * n + 1]
            top = part + (face * inv) * high[2 * n + 1]
            value.append(top * reciprocal(1.0 - (face * face) * inv * high[2 * n]))
        for k in reversed(range(depth)):
            if k < depth - 1:
                face = row(cond, first + k + 1)
            for n, tile in enumerate(tiles):
                if k < depth - 1:
                    value[n] = part_s[k, tile, :] + (face * inv_s[k, tile, :]) * value[n]
                a, b = split(modal[i, k, tile, :] - phi[tile, :] * value[n])
                columns = slice(side * LANES, (side + 1) * LANES)
                for place, part in enumerate((a, a, b)):
                    start = place * m + n * half
                    m3[k, start : start + half, columns] = part

    def pair(tt, carry):
        part = pl.ds(tt * per_pair, per_pair)
        pltpu.make_async_copy(modal_in.at[part], modal.at[part], sem_in.at[tt]).wait()
        for side in range(per_pair):
            correct(tt * per_pair + side, side)
        parity = tt // half_pairs
        offset = lax.rem(tt, half_pairs) * PAIR
        for k in range(depth):
            a, b = split(dot(tx[...], m3[k]))
            for place, part in enumerate((a, b, a)):
                columns = pl.ds(pl.multiple_of(place * mid + offset, PAIR), PAIR)
                g3[parity, k * m : (k + 1) * m, columns] = part
        return carry

    width = out.shape[1]
    mid = width // 2
    half_pairs = mid // PAIR

    lax.fori_loop(0, pairs, pair, 0)
    table.wait()

    rows = out.shape[0]
    chunk = min(256, rows)

    def store(c, side):
        start = c * PAIR if side == 0 else width - (c + 1) * PAIR
        columns = pl.ds(start if isinstance(c, int) else pl.multiple_of(start, PAIR), PAIR)
        return pltpu.make_async_copy(
            out.at[:, columns], out_hbm.at[:, columns], sem_out.at[2 * c + side]
        )

    def columns_of(c, carry):
        columns = pl.ds(pl.multiple_of(c * PAIR, PAIR), PAIR)

        def rows_of(r, inner):
            at = pl.ds(pl.multiple_of(r * chunk, chunk), chunk)
            even = dot(g3[0, at, :], ty[0, :, columns])
            odd = dot(g3[1, at, :], ty[1, :, columns])
            out[at, columns] = even + odd
            far = even - odd
            for q in range(PAIR // LANES):
                start = pl.multiple_of(width - c * PAIR - (q + 1) * LANES, LANES)
                out[at, pl.ds(start, LANES)] = mirror(far[:, q * LANES : (q + 1) * LANES])
            return inner

        lax.fori_loop(0, rows // chunk, rows_of, 0)
        for side in range(2):
            store(c, side).start()
        return carry

    lax.fori_loop(0, half_pairs, columns_of, 0)
    for c in range(half_pairs):
        for side in range(2):
            store(c, side).wait()


def per_device(source, spacing):
    depth, m, width = source.shape
    lanes_count = lax.axis_size("lat")
    slabs = lax.axis_size("growth")
    nz = slabs * depth
    points = m * lanes_count
    nblk = width // LANES
    cuts = lanes_count - 1
    f32 = jnp.float32

    order = np.concatenate([np.arange(0, m, 2), np.arange(1, m, 2)])
    local = cosine_table(m)[order]
    mid = width // 2
    along_y = cosine_table(width)
    halves = np.stack([along_y[0::2, :mid], along_y[1::2, :mid]])
    ty_forward = right_parts(np.swapaxes(halves, 1, 2))
    ty_back = right_parts(halves)
    tx_forward = left_parts(local)
    tx_back = left_parts(local.T)
    mode_y = np.concatenate([np.arange(0, width, 2), np.arange(1, width, 2)])

    def spread_lanes(column):
        return jnp.asarray(np.repeat(np.asarray(column, np.float32)[..., None], LANES, axis=-1))

    phi = spread_lanes(local[:, 0])
    lk = spread_lanes(eigenvalues(order, m))
    lb = jnp.asarray(eigenvalues(mode_y, width).astype(np.float32)[None, :])
    folds = []
    for j in range(1, lanes_count):
        ids = [k for k in range(1, points) if k % (2 * lanes_count) in (j, 2 * lanes_count - j)]
        folds.append(eigenvalues(ids, points))
    lam = spread_lanes(np.stack(folds))

    flat = source.reshape(depth * m, width)
    vmem = pl.BlockSpec(memory_space=pltpu.VMEM)
    smem = pl.BlockSpec(memory_space=pltpu.SMEM)
    anywhere = pl.BlockSpec(memory_space=pl.ANY)
    dma = pltpu.SemaphoreType.DMA
    V = pltpu.VMEM
    modal, jump, heights = pl.pallas_call(
        functools.partial(forward_kernel, slabs, lanes_count),
        out_shape=(
            jax.ShapeDtypeStruct((nblk, depth, m, LANES), f32),
            jax.ShapeDtypeStruct((nblk, 2, nz, LANES), f32),
            jax.ShapeDtypeStruct((nz, LANES), f32),
        ),
        in_specs=[anywhere, smem, anywhere] + [vmem] * 4 + [anywhere],
        out_specs=(vmem, vmem, vmem),
        scratch_shapes=[
            V((depth * m, width), f32),
            V((depth, LANES), f32),
            V((2, 3 * mid, mid), jnp.bfloat16),
            V((cuts, m, LANES), f32),
            V((nz, LANES), f32),
            V((nz + 1, LANES), f32),
            V((2, depth * m, 3 * mid), jnp.bfloat16),
            V((nblk, depth, m, LANES), f32),
            V((nblk, depth, m, LANES), f32),
            V((nblk, depth, m, LANES), f32),
            V((nblk, m, LANES), f32),
            V((nblk, m, LANES), f32),
            V((nblk, m, LANES), f32),
            V((nblk, m, LANES), f32),
            V((nblk, m, LANES), f32),
            V((nblk, 2 * depth, LANES), f32),
            V((lanes_count, 2 * depth, LANES), f32),
            V((cuts, depth, LANES), f32),
            V((slabs, cuts, depth, LANES), f32),
            V((cuts, nz, m, LANES), f32),
            V((nz, m, LANES), f32),
            V((cuts, nz, LANES), f32),
            V((cuts, nz, LANES), f32),
            V((lanes_count, 2, nz, LANES), f32),
            V((nblk, 2, nz, LANES), f32),
            dma((3,)),
            dma((2, slabs)),
            dma((2, nblk)),
            dma((2, nblk)),
            dma((2, lanes_count)),
            dma((2, slabs)),
            dma((2, lanes_count)),
        ],
        compiler_params=pltpu.CompilerParams(
            collective_id=0, has_side_effects=True, vmem_limit_bytes=VMEM_BYTES
        ),
        name="slab_solve",
    )(flat, spacing, ty_forward, tx_forward, phi, lk, lb, lam)

    result = pl.pallas_call(
        functools.partial(inverse_kernel, slabs),
        out_shape=jax.ShapeDtypeStruct((depth * m, width), f32),
        in_specs=[anywhere, vmem, vmem, anywhere] + [vmem] * 4,
        out_specs=anywhere,
        scratch_shapes=[
            V((nblk, depth, m, LANES), f32),
            V((2, 3 * mid, mid), jnp.bfloat16),
            V((depth * m, width), f32),
            dma((width // PAIR + 2,)),
            dma((width // PAIR,)),
            V((nz + 1, LANES), f32),
            V((depth, m, LANES), f32),
            V((depth, m, LANES), f32),
            V((depth, 3 * m, PAIR), jnp.bfloat16),
            V((2, depth * m, 3 * mid), jnp.bfloat16),
        ],
        compiler_params=pltpu.CompilerParams(vmem_limit_bytes=VMEM_BYTES),
        name="face_correction",
    )(modal, jump, heights, ty_back, tx_back, phi, lk, lb)
    return result.reshape(depth, m, width)


def solution(mesh):
    return jax.shard_map(
        per_device,
        mesh=mesh,
        in_specs=(P("growth", "lat", None), P("growth")),
        out_specs=P("growth", "lat", None),
        check_vma=False,
    )
```

```python
import functools
import math

import jax
import jax.numpy as jnp
import ml_dtypes
import numpy as np
from jax import lax
from jax.experimental import pallas as pl
from jax.experimental.pallas import tpu as pltpu
from jax.sharding import PartitionSpec as P

LANES = 128
PAIR = 256
LAG = 2
MESH = pl.DeviceIdType.MESH
VMEM_BYTES = 56 * 1024 * 1024


def cosine_table(points):
    ids = np.arange(points, dtype=np.int64)
    phase = (2 * ids[None, :] + 1) * ids[:, None] % (4 * points)
    scale = np.where(ids == 0, math.sqrt(1.0 / points), math.sqrt(2.0 / points))
    return scale[:, None] * np.cos(phase * (math.pi / (2.0 * points)))


def eigenvalues(ids, points):
    return 4.0 * np.sin(np.asarray(ids) * (math.pi / (2.0 * points))) ** 2


def two_parts(table):
    high = table.astype(ml_dtypes.bfloat16)
    low = (table - high.astype(np.float64)).astype(ml_dtypes.bfloat16)
    return high, low


def left_parts(table):
    high, low = two_parts(table)
    return jnp.asarray(np.concatenate([high, low, high], axis=-1))


def right_parts(table):
    high, low = two_parts(table)
    return jnp.asarray(np.concatenate([high, high, low], axis=-2))


def mirror(value):
    lanes = lax.broadcasted_iota(jnp.int32, value.shape, 1)
    return jnp.take_along_axis(value, LANES - 1 - lanes, axis=1, mode="promise_in_bounds")


def split(value):
    high = value.astype(jnp.bfloat16)
    low = (value - high.astype(jnp.float32)).astype(jnp.bfloat16)
    return high, low


def dot(a, b):
    return jnp.dot(a, b, preferred_element_type=jnp.float32)


def stacked(value):
    high, low = split(value)
    return jnp.concatenate([high, high, low], axis=0)


def reciprocal(x):
    guess = pl.reciprocal(x, approx=True)
    return guess * (2.0 - x * guess)


def fill_conduct(heights_ref, cond_ref):
    heights = heights_ref[...]
    zero = jnp.zeros((1, LANES), jnp.float32)
    cond_ref[...] = 2.0 / (
        jnp.concatenate([zero, heights], axis=0) + jnp.concatenate([heights, zero], axis=0)
    )


def row(ref, z):
    return ref[pl.ds(z, 1), :]


def inverse_pivot(cond_ref, heights_ref, z, eigen, behind, face):
    diagonal = (row(cond_ref, z) + row(cond_ref, z + 1)) + row(heights_ref, z) * eigen
    return reciprocal(diagonal - (face * face) * behind)


def leap(cond_ref, heights_ref, first, depth, eigen, inv, part, right, upward):
    newest, before = None, inv
    for k in range(depth):
        z = first + (k if upward else depth - 1 - k)
        face = row(cond_ref, z if upward else z + 1)
        diagonal = (row(cond_ref, z) + row(cond_ref, z + 1)) + row(heights_ref, z) * eigen
        if newest is None:
            part = right(z) + face * part if right else None
            newest, before = diagonal - (face * face) * before, 1.0
        else:
            part = right(z) * newest + face * part if right else None
            newest, before = diagonal * newest - (face * face) * before, newest
    scale = reciprocal(newest)
    return before * scale, part * scale if right else None


def forward_kernel(
    slabs, lanes_count, src_in, spacing, ty_in, tx, phi, lk, lb, lam_in,
    modal_out, jump_out, heights_out,
    modal, src, spread, ty, lam, heights, cond, x3, f, inv_s, part_s, inv_high, from_low, from_high,
    to_low, to_high, ends, ends_in, jumps, jumps_all, k_inv, k_part, g_modes, g_cuts,
    g_send, g_in, sem_in, sem_m, sem_h, sem_up, sem_down, sem_e, sem_r, sem_g,
):
    growth = lax.axis_index("growth")
    lat = lax.axis_index("lat")
    depth, m = f.shape[1], f.shape[2]
    half = m // 2
    nblk = f.shape[0]
    nz = slabs * depth
    width = src.shape[1]
    share = max(1, lanes_count // nblk)
    tiles = [slice(0, half), slice(half, m)]
    lag = LAG * (slabs - 1)

    loads = [
        pltpu.make_async_copy(a, b, sem_in.at[n])
        for n, (a, b) in enumerate(
            [(src_in, src), (ty_in, ty), (lam_in, lam)]
        )
    ]
    for load in loads:
        load.start()
    for k in range(depth):
        spread[k : k + 1, :] = jnp.full((1, LANES), spacing[k], jnp.float32)

    barrier = pltpu.get_barrier_semaphore()
    for off in range(1, slabs):
        pl.semaphore_signal(
            barrier, inc=1, device_id=(lax.rem(growth + off, slabs), lat), device_id_type=MESH
        )
    for off in range(1, lanes_count):
        pl.semaphore_signal(
            barrier, inc=1, device_id=(growth, lax.rem(lat + off, lanes_count)),
            device_id_type=MESH,
        )
    pl.semaphore_wait(barrier, slabs + lanes_count - 2)

    def height_copy(off, owner, target):
        return pltpu.make_async_remote_copy(
            src_ref=spread,
            dst_ref=heights.at[pl.ds(owner * depth, depth)],
            send_sem=sem_h.at[0, off],
            recv_sem=sem_h.at[1, off],
            device_id=(target, lat),
            device_id_type=MESH,
        )

    for off in range(1, slabs):
        height_copy(off, growth, lax.rem(growth + off, slabs)).start()
    heights[pl.ds(growth * depth, depth), :] = spread[...]
    rows = src.shape[0]
    loads[0].wait()

    mid = width // 2

    def split_rows(i, carry):
        at = pl.ds(pl.multiple_of(i * m, m), m)
        for q in range(mid // LANES):
            near = src[at, q * LANES : (q + 1) * LANES]
            far = mirror(src[at, width - (q + 1) * LANES : width - q * LANES])
            for n, value in enumerate((near + far, near - far)):
                high, low = split(value)
                for place, part in enumerate((high, low, high)):
                    start = place * mid + q * LANES
                    x3[n, at, start : start + LANES] = part
        return carry

    lax.fori_loop(0, depth, split_rows, 0)
    for off in range(1, slabs):
        behind = lax.rem(growth + slabs - off, slabs)
        copy = height_copy(off, behind, lax.rem(growth + off, slabs))
        copy.wait_send()
        copy.wait_recv()
    fill_conduct(heights, cond)
    heights_out[...] = heights[...]
    for load in loads[1:]:
        load.wait()

    def eigen_of(i, tile):
        at = pl.ds(pl.multiple_of(i * LANES, LANES), LANES)
        return lk[tile, :] + lb[:, at]

    def pivots_below(i):
        def one(tile):
            eigen = eigen_of(i, tile)
            return lax.fori_loop(
                0, growth,
                lambda n, inv: leap(
                    cond, heights, n * depth, depth, eigen, inv, None, None, True
                )[0],
                jnp.zeros((half, LANES), jnp.float32),
            )

        return [one(tile) for tile in tiles]

    def pivots_above(i):
        def one(tile):
            eigen = eigen_of(i, tile)
            return lax.fori_loop(
                0, slabs - 1 - growth,
                lambda n, inv: leap(
                    cond, heights, (slabs - 1 - n) * depth, depth, eigen, inv, None, None, False
                )[0],
                jnp.zeros((half, LANES), jnp.float32),
            )

        return [one(tile) for tile in tiles]

    @pl.when(growth == 0)
    def _():
        from_low[...] = jnp.zeros_like(from_low)

    @pl.when(growth == slabs - 1)
    def _():
        from_high[...] = jnp.zeros_like(from_high)

    first = growth * depth
    chunk = min(512, rows)
    planes = chunk // m

    half_pairs = mid // PAIR

    def transform(pair):
        parity = pair // half_pairs
        columns = pl.ds(pl.multiple_of(lax.rem(pair, half_pairs) * PAIR, PAIR), PAIR)

        def one(c, carry):
            at = pl.ds(pl.multiple_of(c * chunk, chunk), chunk)
            along_y = dot(x3[parity, at, :], ty[parity, :, columns])
            for k in range(planes):
                part = slice(k * m, (k + 1) * m)
                both = dot(tx[...], stacked(along_y[part, :]))
                for side in range(PAIR // LANES):
                    f[pair * (PAIR // LANES) + side, c * planes + k] = both[
                        :, side * LANES : (side + 1) * LANES
                    ]
            return carry

        lax.fori_loop(0, rows // chunk, one, 0)

    def up_copy(i):
        return pltpu.make_async_remote_copy(
            src_ref=to_high.at[i], dst_ref=from_low.at[i],
            send_sem=sem_up.at[0, i], recv_sem=sem_up.at[1, i],
            device_id=(lax.rem(growth + 1, slabs), lat), device_id_type=MESH,
        )

    def down_copy(i):
        return pltpu.make_async_remote_copy(
            src_ref=to_low.at[i], dst_ref=from_high.at[i],
            send_sem=sem_down.at[0, i], recv_sem=sem_down.at[1, i],
            device_id=(lax.rem(growth + slabs - 1, slabs), lat), device_id_type=MESH,
        )

    def sweep_up(i):
        inv = pivots_below(i)

        @pl.when(growth > 0)
        def _():
            up_copy(i).wait_recv()

        eigen = [eigen_of(i, tile) for tile in tiles]
        part = [from_low[i, tile, :] for tile in tiles]
        for k in range(depth):
            z = first + k
            face = row(cond, z)
            height = row(heights, z)
            for n, tile in enumerate(tiles):
                inv[n] = inverse_pivot(cond, heights, z, eigen[n], inv[n], face)
                part[n] = (height * f[i, k, tile, :] + face * part[n]) * inv[n]
                inv_s[i, k, tile, :] = inv[n]
                part_s[i, k, tile, :] = part[n]

        @pl.when(growth < slabs - 1)
        def _():
            for n, tile in enumerate(tiles):
                to_high[i, tile, :] = part[n]
            up_copy(i).start()

    def sweep_down(i):
        for tile, value in zip(tiles, pivots_above(i)):
            inv_high[i, tile, :] = value

        @pl.when(growth < slabs - 1)
        def _():
            down_copy(i).wait_recv()

        @pl.when(growth > 0)
        def _():
            for tile in tiles:
                _, part = leap(
                    cond, heights, first, depth, eigen_of(i, tile), inv_high[i, tile, :],
                    from_high[i, tile, :],
                    lambda z: row(heights, z) * f[i, z - first, tile, :], False,
                )
                to_low[i, tile, :] = part
            down_copy(i).start()

    def block_of(rank):
        return rank // share

    def ends_copy(off, owner, target):
        return pltpu.make_async_remote_copy(
            src_ref=ends.at[block_of(target)], dst_ref=ends_in.at[owner],
            send_sem=sem_e.at[0, off], recv_sem=sem_e.at[1, off],
            device_id=(growth, target), device_id_type=MESH,
        )

    def modal_copy(i):
        return pltpu.make_async_copy(modal.at[i], modal_out.at[i], sem_m.at[i])

    def finish(i):
        face = row(cond, first + depth)
        value = []
        weight = [phi[tile, :] for tile in tiles]
        for n, tile in enumerate(tiles):
            inv = inv_s[i, depth - 1, tile, :]
            top = part_s[i, depth - 1, tile, :] + (face * inv) * from_high[i, tile, :]
            value.append(top * reciprocal(1.0 - (face * face) * inv * inv_high[i, tile, :]))
        for k in reversed(range(depth)):
            if k < depth - 1:
                face = row(cond, first + k + 1)
                for n, tile in enumerate(tiles):
                    value[n] = part_s[i, k, tile, :] + (face * inv_s[i, k, tile, :]) * value[n]
            sums = []
            for n, tile in enumerate(tiles):
                modal[i, k, tile, :] = value[n]
                sums.append(jnp.sum(weight[n] * value[n], axis=0, keepdims=True))
            ends[i, k : k + 1, :] = sums[0] + sums[1]
            ends[i, depth + k : depth + k + 1, :] = sums[0] - sums[1]
        modal_copy(i).start()
        for n in range(share):
            target = i * share + n
            off = lax.rem(target + lanes_count - lat, lanes_count)
            pl.when(target != lat)(ends_copy(off, lat, target).start)

    per_pair = PAIR // LANES
    cuts = lanes_count - 1
    middle = nz // 2
    per_step = pl.cdiv(cuts, lag)

    def face_pivots(j):
        weight = [lam[j, tile, :] for tile in tiles]
        at = pl.ds(pl.multiple_of((lat // share) * LANES, LANES), LANES)
        eigen = [w + lb[:, at] for w in weight]
        low = [jnp.zeros((half, LANES), jnp.float32) for _ in tiles]
        high = list(low)
        for k in range(middle):
            face = row(cond, k)
            z = nz - 1 - k
            face_high = row(cond, z + 1)
            for n, tile in enumerate(tiles):
                low[n] = inverse_pivot(cond, heights, k, eigen[n], low[n], face)
                k_inv[j, k, tile, :] = low[n]
                high[n] = inverse_pivot(cond, heights, z, eigen[n], high[n], face_high)
                k_inv[j, z, tile, :] = high[n]

    def stage(tt, carry):
        @pl.when(tt < nblk // per_pair)
        def _():
            transform(tt)

        for side in range(per_pair):
            t = tt * per_pair + side
            up_i = t - LAG * growth
            down_i = t - LAG * (slabs - 1 - growth)
            end_i = t - lag

            for n in range(per_step):
                j = (t - nblk) * per_step + n
                pl.when((j >= 0) & (j < cuts))(functools.partial(face_pivots, j))

            @pl.when((up_i >= 0) & (up_i < nblk))
            def _():
                sweep_up(up_i)

            @pl.when((down_i >= 0) & (down_i < nblk))
            def _():
                sweep_down(down_i)

            @pl.when((end_i >= 0) & (end_i < nblk))
            def _():
                finish(end_i)

        return carry

    lax.fori_loop(0, pl.cdiv(nblk + lag, per_pair), stage, 0)

    ends_in[lat] = ends[block_of(lat)]

    for off in range(1, lanes_count):
        copy = ends_copy(
            off, lax.rem(lat + lanes_count - off, lanes_count), lax.rem(lat + off, lanes_count)
        )
        copy.wait_send()
        copy.wait_recv()

    sines = [
        [
            math.sqrt(2.0 / lanes_count) * math.sin(math.pi * (c + 1) * (j + 1) / lanes_count)
            for j in range(cuts)
        ]
        for c in range(cuts)
    ]
    jump = [ends_in[c, depth:, :] - ends_in[c + 1, :depth, :] for c in range(cuts)]
    for j in range(cuts):
        total = jump[0] * sines[0][j]
        for c in range(1, cuts):
            total += jump[c] * sines[c][j]
        jumps[j] = total
    jumps_all[growth] = jumps[...]

    def jumps_copy(off, owner, target):
        return pltpu.make_async_remote_copy(
            src_ref=jumps, dst_ref=jumps_all.at[owner],
            send_sem=sem_r.at[0, off], recv_sem=sem_r.at[1, off],
            device_id=(target, lat), device_id_type=MESH,
        )

    for off in range(1, slabs):
        jumps_copy(off, growth, lax.rem(growth + off, slabs)).start()
    for off in range(1, slabs):
        copy = jumps_copy(
            off, lax.rem(growth + slabs - off, slabs), lax.rem(growth + off, slabs)
        )
        copy.wait_send()
        copy.wait_recv()

    def correct(j, carry):
        def held(z):
            return jumps_all[z // depth, j, z % depth : z % depth + 1, :]

        weight = [lam[j, tile, :] for tile in tiles]
        low = [jnp.zeros((half, LANES), jnp.float32) for _ in tiles]
        high = list(low)
        for k in range(middle):
            z = nz - 1 - k
            face = row(cond, k)
            right = row(heights, k) * held(k)
            face_high = row(cond, z + 1)
            right_high = row(heights, z) * held(z)
            for n, tile in enumerate(tiles):
                low[n] = (right + face * low[n]) * k_inv[j, k, tile, :]
                k_part[k, tile, :] = low[n]
                high[n] = (right_high + face_high * high[n]) * k_inv[j, z, tile, :]
                k_part[z, tile, :] = high[n]

        def put(z, value):
            total = sum(
                jnp.sum(w * v, axis=0, keepdims=True) for w, v in zip(weight, value)
            )
            g_modes[j, z : z + 1, :] = held(z) - total * (1.0 / m)

        face = row(cond, middle)
        below, above = [], []
        for n, tile in enumerate(tiles):
            inv_a = face * k_inv[j, middle - 1, tile, :]
            inv_b = face * k_inv[j, middle, tile, :]
            below.append((low[n] + inv_a * high[n]) * reciprocal(1.0 - inv_a * inv_b))
            above.append(high[n] + inv_b * below[n])
        put(middle - 1, below)
        put(middle, above)
        for k in range(1, middle):
            z = middle - 1 - k
            face = row(cond, z + 1)
            for n, tile in enumerate(tiles):
                below[n] = k_part[z, tile, :] + (face * k_inv[j, z, tile, :]) * below[n]
            put(z, below)
            z = middle + k
            face = row(cond, z)
            for n, tile in enumerate(tiles):
                above[n] = k_part[z, tile, :] + (face * k_inv[j, z, tile, :]) * above[n]
            put(z, above)
        return carry

    lax.fori_loop(0, cuts, correct, 0)

    for c in range(cuts):
        total = g_modes[0] * sines[c][0]
        for j in range(1, cuts):
            total += g_modes[j] * sines[c][j]
        g_cuts[c] = total
    for d in range(lanes_count):
        low = g_cuts[d - 1] if d > 0 else jnp.zeros((nz, LANES), jnp.float32)
        high = g_cuts[d] if d < cuts else jnp.zeros((nz, LANES), jnp.float32)
        g_send[d, 0] = high - low
        g_send[d, 1] = -(high + low)

    def g_copy(off, owner, target):
        return pltpu.make_async_remote_copy(
            src_ref=g_send.at[target], dst_ref=g_in.at[block_of(owner)],
            send_sem=sem_g.at[0, off], recv_sem=sem_g.at[1, off],
            device_id=(growth, target), device_id_type=MESH,
        )

    def speaks(rank, act):
        if share == 1:
            act()
        else:
            pl.when(lax.rem(rank, share) == 0)(act)

    def own_block():
        g_in[block_of(lat)] = g_send[lat]

    for off in range(1, lanes_count):
        copy = g_copy(off, lat, lax.rem(lat + off, lanes_count))
        speaks(lat, copy.start)
    speaks(lat, own_block)
    for off in range(1, lanes_count):
        owner = lax.rem(lat + lanes_count - off, lanes_count)
        target = lax.rem(lat + off, lanes_count)
        speaks(lat, g_copy(off, lat, target).wait_send)
        speaks(owner, g_copy(off, owner, target).wait_recv)
    def drain(i, carry):
        @pl.when(growth < slabs - 1)
        def _():
            up_copy(i).wait_send()

        @pl.when(growth > 0)
        def _():
            down_copy(i).wait_send()

        modal_copy(i).wait()
        return carry

    lax.fori_loop(0, nblk, drain, 0)
    jump_out[...] = g_in[...]


def inverse_kernel(
    slabs, modal_in, jump, heights, ty_in, tx, phi, lk, lb,
    out_hbm,
    modal, ty, out, sem_in, sem_out, cond, inv_s, part_s, m3, g3,
):
    growth = lax.axis_index("growth")
    nblk, depth, m = modal.shape[:3]
    per_pair = PAIR // LANES
    pairs = nblk // per_pair
    for n in range(pairs):
        part = pl.ds(n * per_pair, per_pair)
        pltpu.make_async_copy(modal_in.at[part], modal.at[part], sem_in.at[n]).start()
    table = pltpu.make_async_copy(ty_in, ty, sem_in.at[pairs])
    table.start()
    half = m // 2
    tiles = [slice(0, half), slice(half, m)]
    first = growth * depth
    fill_conduct(heights, cond)

    def correct(i, side):
        at = pl.ds(pl.multiple_of(i * LANES, LANES), LANES)
        eigen = [lk[tile, :] + lb[:, at] for tile in tiles]
        zero = jnp.zeros((half, LANES), jnp.float32)

        def advance(z, face, state):
            height = row(heights, z)
            new = []
            for n in range(2):
                inv, part = state[2 * n], state[2 * n + 1]
                inv = inverse_pivot(cond, heights, z, eigen[n], inv, face)
                right = height * jump[i, n, pl.ds(z, 1), :]
                new += [inv, (right + face * part) * inv]
            return tuple(new)

        def up(z, state):
            return advance(z, row(cond, z), state)

        def outside(n, upward):
            def right(z):
                return row(heights, z) * jump[i, n, pl.ds(z, 1), :]

            def one(q, state):
                start = (q if upward else slabs - 1 - q) * depth
                return leap(cond, heights, start, depth, eigen[n], *state, right, upward)

            trips = growth if upward else slabs - 1 - growth
            return lax.fori_loop(0, trips, one, (zero, zero))

        high = outside(0, False) + outside(1, False)
        state = outside(0, True) + outside(1, True)
        for k in range(depth):
            state = up(first + k, state)
            for n, tile in enumerate(tiles):
                inv_s[k, tile, :] = state[2 * n]
                part_s[k, tile, :] = state[2 * n + 1]
        face = row(cond, first + depth)
        value = []
        for n in range(2):
            inv, part = state[2 * n], state[2 * n + 1]
            top = part + (face * inv) * high[2 * n + 1]
            value.append(top * reciprocal(1.0 - (face * face) * inv * high[2 * n]))
        for k in reversed(range(depth)):
            if k < depth - 1:
                face = row(cond, first + k + 1)
            for n, tile in enumerate(tiles):
                if k < depth - 1:
                    value[n] = part_s[k, tile, :] + (face * inv_s[k, tile, :]) * value[n]
                a, b = split(modal[i, k, tile, :] - phi[tile, :] * value[n])
                columns = slice(side * LANES, (side + 1) * LANES)
                for place, part in enumerate((a, a, b)):
                    start = place * m + n * half
                    m3[k, start : start + half, columns] = part

    def pair(tt, carry):
        part = pl.ds(tt * per_pair, per_pair)
        pltpu.make_async_copy(modal_in.at[part], modal.at[part], sem_in.at[tt]).wait()
        for side in range(per_pair):
            correct(tt * per_pair + side, side)
        parity = tt // half_pairs
        offset = lax.rem(tt, half_pairs) * PAIR
        for k in range(depth):
            a, b = split(dot(tx[...], m3[k]))
            for place, part in enumerate((a, b, a)):
                columns = pl.ds(pl.multiple_of(place * mid + offset, PAIR), PAIR)
                g3[parity, k * m : (k + 1) * m, columns] = part
        return carry

    width = out.shape[1]
    mid = width // 2
    half_pairs = mid // PAIR

    lax.fori_loop(0, pairs, pair, 0)
    table.wait()

    rows = out.shape[0]
    chunk = min(256, rows)

    def store(c, side):
        start = c * PAIR if side == 0 else width - (c + 1) * PAIR
        columns = pl.ds(start if isinstance(c, int) else pl.multiple_of(start, PAIR), PAIR)
        return pltpu.make_async_copy(
            out.at[:, columns], out_hbm.at[:, columns], sem_out.at[2 * c + side]
        )

    def columns_of(c, carry):
        columns = pl.ds(pl.multiple_of(c * PAIR, PAIR), PAIR)

        def rows_of(r, inner):
            at = pl.ds(pl.multiple_of(r * chunk, chunk), chunk)
            even = dot(g3[0, at, :], ty[0, :, columns])
            odd = dot(g3[1, at, :], ty[1, :, columns])
            out[at, columns] = even + odd
            far = even - odd
            for q in range(PAIR // LANES):
                start = pl.multiple_of(width - c * PAIR - (q + 1) * LANES, LANES)
                out[at, pl.ds(start, LANES)] = mirror(far[:, q * LANES : (q + 1) * LANES])
            return inner

        lax.fori_loop(0, rows // chunk, rows_of, 0)
        for side in range(2):
            store(c, side).start()
        return carry

    lax.fori_loop(0, half_pairs, columns_of, 0)
    for c in range(half_pairs):
        for side in range(2):
            store(c, side).wait()


def per_device(source, spacing):
    depth, m, width = source.shape
    lanes_count = lax.axis_size("lat")
    slabs = lax.axis_size("growth")
    nz = slabs * depth
    points = m * lanes_count
    nblk = width // LANES
    cuts = lanes_count - 1
    f32 = jnp.float32

    order = np.concatenate([np.arange(0, m, 2), np.arange(1, m, 2)])
    local = cosine_table(m)[order]
    mid = width // 2
    along_y = cosine_table(width)
    halves = np.stack([along_y[0::2, :mid], along_y[1::2, :mid]])
    ty_forward = right_parts(np.swapaxes(halves, 1, 2))
    ty_back = right_parts(halves)
    tx_forward = left_parts(local)
    tx_back = left_parts(local.T)
    mode_y = np.concatenate([np.arange(0, width, 2), np.arange(1, width, 2)])

    def spread_lanes(column):
        return jnp.asarray(np.repeat(np.asarray(column, np.float32)[..., None], LANES, axis=-1))

    phi = spread_lanes(local[:, 0])
    lk = spread_lanes(eigenvalues(order, m))
    lb = jnp.asarray(eigenvalues(mode_y, width).astype(np.float32)[None, :])
    folds = []
    for j in range(1, lanes_count):
        ids = [k for k in range(1, points) if k % (2 * lanes_count) in (j, 2 * lanes_count - j)]
        folds.append(eigenvalues(ids, points))
    lam = spread_lanes(np.stack(folds))

    flat = source.reshape(depth * m, width)
    vmem = pl.BlockSpec(memory_space=pltpu.VMEM)
    smem = pl.BlockSpec(memory_space=pltpu.SMEM)
    anywhere = pl.BlockSpec(memory_space=pl.ANY)
    dma = pltpu.SemaphoreType.DMA
    V = pltpu.VMEM
    modal, jump, heights = pl.pallas_call(
        functools.partial(forward_kernel, slabs, lanes_count),
        out_shape=(
            jax.ShapeDtypeStruct((nblk, depth, m, LANES), f32),
            jax.ShapeDtypeStruct((nblk, 2, nz, LANES), f32),
            jax.ShapeDtypeStruct((nz, LANES), f32),
        ),
        in_specs=[anywhere, smem, anywhere] + [vmem] * 4 + [anywhere],
        out_specs=(anywhere, vmem, vmem),
        scratch_shapes=[
            V((nblk, depth, m, LANES), f32),
            V((depth * m, width), f32),
            V((depth, LANES), f32),
            V((2, 3 * mid, mid), jnp.bfloat16),
            V((cuts, m, LANES), f32),
            V((nz, LANES), f32),
            V((nz + 1, LANES), f32),
            V((2, depth * m, 3 * mid), jnp.bfloat16),
            V((nblk, depth, m, LANES), f32),
            V((nblk, depth, m, LANES), f32),
            V((nblk, depth, m, LANES), f32),
            V((nblk, m, LANES), f32),
            V((nblk, m, LANES), f32),
            V((nblk, m, LANES), f32),
            V((nblk, m, LANES), f32),
            V((nblk, m, LANES), f32),
            V((nblk, 2 * depth, LANES), f32),
            V((lanes_count, 2 * depth, LANES), f32),
            V((cuts, depth, LANES), f32),
            V((slabs, cuts, depth, LANES), f32),
            V((cuts, nz, m, LANES), f32),
            V((nz, m, LANES), f32),
            V((cuts, nz, LANES), f32),
            V((cuts, nz, LANES), f32),
            V((lanes_count, 2, nz, LANES), f32),
            V((nblk, 2, nz, LANES), f32),
            dma((3,)),
            dma((nblk,)),
            dma((2, slabs)),
            dma((2, nblk)),
            dma((2, nblk)),
            dma((2, lanes_count)),
            dma((2, slabs)),
            dma((2, lanes_count)),
        ],
        compiler_params=pltpu.CompilerParams(
            collective_id=0, has_side_effects=True, vmem_limit_bytes=VMEM_BYTES
        ),
        name="slab_solve",
    )(flat, spacing, ty_forward, tx_forward, phi, lk, lb, lam)

    result = pl.pallas_call(
        functools.partial(inverse_kernel, slabs),
        out_shape=jax.ShapeDtypeStruct((depth * m, width), f32),
        in_specs=[anywhere, vmem, vmem, anywhere] + [vmem] * 4,
        out_specs=anywhere,
        scratch_shapes=[
            V((nblk, depth, m, LANES), f32),
            V((2, 3 * mid, mid), jnp.bfloat16),
            V((depth * m, width), f32),
            dma((width // PAIR + 2,)),
            dma((width // PAIR,)),
            V((nz + 1, LANES), f32),
            V((depth, m, LANES), f32),
            V((depth, m, LANES), f32),
            V((depth, 3 * m, PAIR), jnp.bfloat16),
            V((2, depth * m, 3 * mid), jnp.bfloat16),
        ],
        compiler_params=pltpu.CompilerParams(vmem_limit_bytes=VMEM_BYTES),
        name="face_correction",
    )(modal, jump, heights, ty_back, tx_back, phi, lk, lb)
    return result.reshape(depth, m, width)


def solution(mesh):
    return jax.shard_map(
        per_device,
        mesh=mesh,
        in_specs=(P("growth", "lat", None), P("growth")),
        out_specs=P("growth", "lat", None),
        check_vma=False,
    )
```

```python
import functools
import math

import jax
import jax.numpy as jnp
import ml_dtypes
import numpy as np
from jax import lax
from jax.experimental import pallas as pl
from jax.experimental.pallas import tpu as pltpu
from jax.sharding import PartitionSpec as P

LANES = 128
PAIR = 256
LAG = 2
MESH = pl.DeviceIdType.MESH
VMEM_BYTES = 56 * 1024 * 1024


def cosine_table(points):
    ids = np.arange(points, dtype=np.int64)
    phase = (2 * ids[None, :] + 1) * ids[:, None] % (4 * points)
    scale = np.where(ids == 0, math.sqrt(1.0 / points), math.sqrt(2.0 / points))
    return scale[:, None] * np.cos(phase * (math.pi / (2.0 * points)))


def eigenvalues(ids, points):
    return 4.0 * np.sin(np.asarray(ids) * (math.pi / (2.0 * points))) ** 2


def two_parts(table):
    high = table.astype(ml_dtypes.bfloat16)
    low = (table - high.astype(np.float64)).astype(ml_dtypes.bfloat16)
    return high, low


def left_parts(table):
    high, low = two_parts(table)
    return jnp.asarray(np.concatenate([high, low, high], axis=-1))


def right_parts(table):
    high, low = two_parts(table)
    return jnp.asarray(np.concatenate([high, high, low], axis=-2))


def mirror(value):
    lanes = lax.broadcasted_iota(jnp.int32, value.shape, 1)
    return jnp.take_along_axis(value, LANES - 1 - lanes, axis=1, mode="promise_in_bounds")


def split(value):
    high = value.astype(jnp.bfloat16)
    low = (value - high.astype(jnp.float32)).astype(jnp.bfloat16)
    return high, low


def dot(a, b):
    return jnp.dot(a, b, preferred_element_type=jnp.float32)


def stacked(value):
    high, low = split(value)
    return jnp.concatenate([high, high, low], axis=0)


def reciprocal(x):
    guess = pl.reciprocal(x, approx=True)
    return guess * (2.0 - x * guess)


def fill_conduct(heights_ref, cond_ref):
    heights = heights_ref[...]
    zero = jnp.zeros((1, LANES), jnp.float32)
    cond_ref[...] = 2.0 / (
        jnp.concatenate([zero, heights], axis=0) + jnp.concatenate([heights, zero], axis=0)
    )


def row(ref, z):
    return ref[pl.ds(z, 1), :]


def inverse_pivot(cond_ref, heights_ref, z, eigen, behind, face):
    diagonal = (row(cond_ref, z) + row(cond_ref, z + 1)) + row(heights_ref, z) * eigen
    return reciprocal(diagonal - (face * face) * behind)


def leap(cond_ref, heights_ref, first, depth, eigen, inv, part, right, upward):
    newest, before = None, inv
    for k in range(depth):
        z = first + (k if upward else depth - 1 - k)
        face = row(cond_ref, z if upward else z + 1)
        diagonal = (row(cond_ref, z) + row(cond_ref, z + 1)) + row(heights_ref, z) * eigen
        if newest is None:
            part = right(z) + face * part if right else None
            newest, before = diagonal - (face * face) * before, 1.0
        else:
            part = right(z) * newest + face * part if right else None
            newest, before = diagonal * newest - (face * face) * before, newest
    scale = reciprocal(newest)
    return before * scale, part * scale if right else None


def forward_kernel(
    slabs, lanes_count, src_in, spacing, ty_in, tx, phi, lk, lb, lam_in,
    modal_out, jump_out, heights_out,
    modal, src, spread, ty, lam, heights, cond, x3, f, inv_s, part_s, inv_high, from_low, from_high,
    to_low, to_high, ends, ends_in, jumps, jumps_all, k_inv, k_part, g_modes, g_cuts,
    g_send, g_in, sem_in, sem_m, sem_h, sem_up, sem_down, sem_e, sem_r, sem_j, sem_g,
):
    growth = lax.axis_index("growth")
    lat = lax.axis_index("lat")
    depth, m = f.shape[1], f.shape[2]
    half = m // 2
    nblk = f.shape[0]
    nz = slabs * depth
    width = src.shape[1]
    share = max(1, lanes_count // nblk)
    tiles = [slice(0, half), slice(half, m)]
    lag = LAG * (slabs - 1)
    per_slab = lam.shape[0]

    loads = [
        pltpu.make_async_copy(a, b, sem_in.at[n])
        for n, (a, b) in enumerate(
            [
                (src_in, src),
                (ty_in, ty),
                (lam_in.at[pl.ds(growth * per_slab, per_slab)], lam),
            ]
        )
    ]
    for load in loads:
        load.start()
    for k in range(depth):
        spread[k : k + 1, :] = jnp.full((1, LANES), spacing[k], jnp.float32)

    barrier = pltpu.get_barrier_semaphore()
    for off in range(1, slabs):
        pl.semaphore_signal(
            barrier, inc=1, device_id=(lax.rem(growth + off, slabs), lat), device_id_type=MESH
        )
    for off in range(1, lanes_count):
        pl.semaphore_signal(
            barrier, inc=1, device_id=(growth, lax.rem(lat + off, lanes_count)),
            device_id_type=MESH,
        )
    pl.semaphore_wait(barrier, slabs + lanes_count - 2)

    def height_copy(off, owner, target):
        return pltpu.make_async_remote_copy(
            src_ref=spread,
            dst_ref=heights.at[pl.ds(owner * depth, depth)],
            send_sem=sem_h.at[0, off],
            recv_sem=sem_h.at[1, off],
            device_id=(target, lat),
            device_id_type=MESH,
        )

    for off in range(1, slabs):
        height_copy(off, growth, lax.rem(growth + off, slabs)).start()
    heights[pl.ds(growth * depth, depth), :] = spread[...]
    rows = src.shape[0]
    loads[0].wait()

    mid = width // 2

    def split_rows(i, carry):
        at = pl.ds(pl.multiple_of(i * m, m), m)
        for q in range(mid // LANES):
            near = src[at, q * LANES : (q + 1) * LANES]
            far = mirror(src[at, width - (q + 1) * LANES : width - q * LANES])
            for n, value in enumerate((near + far, near - far)):
                high, low = split(value)
                for place, part in enumerate((high, low, high)):
                    start = place * mid + q * LANES
                    x3[n, at, start : start + LANES] = part
        return carry

    lax.fori_loop(0, depth, split_rows, 0)
    def eigen_of(i, tile):
        at = pl.ds(pl.multiple_of(i * LANES, LANES), LANES)
        return lk[tile, :] + lb[:, at]

    def pivots_below(i):
        def one(tile):
            eigen = eigen_of(i, tile)
            return lax.fori_loop(
                0, growth,
                lambda n, inv: leap(
                    cond, heights, n * depth, depth, eigen, inv, None, None, True
                )[0],
                jnp.zeros((half, LANES), jnp.float32),
            )

        return [one(tile) for tile in tiles]

    def pivots_above(i):
        def one(tile):
            eigen = eigen_of(i, tile)
            return lax.fori_loop(
                0, slabs - 1 - growth,
                lambda n, inv: leap(
                    cond, heights, (slabs - 1 - n) * depth, depth, eigen, inv, None, None, False
                )[0],
                jnp.zeros((half, LANES), jnp.float32),
            )

        return [one(tile) for tile in tiles]

    @pl.when(growth == 0)
    def _():
        from_low[...] = jnp.zeros_like(from_low)

    @pl.when(growth == slabs - 1)
    def _():
        from_high[...] = jnp.zeros_like(from_high)

    first = growth * depth
    chunk = min(512, rows)
    planes = chunk // m

    half_pairs = mid // PAIR

    def transform(pair):
        parity = pair // half_pairs
        columns = pl.ds(pl.multiple_of(lax.rem(pair, half_pairs) * PAIR, PAIR), PAIR)

        def one(c, carry):
            at = pl.ds(pl.multiple_of(c * chunk, chunk), chunk)
            along_y = dot(x3[parity, at, :], ty[parity, :, columns])
            for k in range(planes):
                part = slice(k * m, (k + 1) * m)
                both = dot(tx[...], stacked(along_y[part, :]))
                for side in range(PAIR // LANES):
                    f[pair * (PAIR // LANES) + side, c * planes + k] = both[
                        :, side * LANES : (side + 1) * LANES
                    ]
            return carry

        lax.fori_loop(0, rows // chunk, one, 0)

    loads[1].wait()
    transform(0)
    for off in range(1, slabs):
        behind = lax.rem(growth + slabs - off, slabs)
        copy = height_copy(off, behind, lax.rem(growth + off, slabs))
        copy.wait_send()
        copy.wait_recv()
    fill_conduct(heights, cond)
    heights_out[...] = heights[...]
    loads[2].wait()

    def up_copy(i):
        return pltpu.make_async_remote_copy(
            src_ref=to_high.at[i], dst_ref=from_low.at[i],
            send_sem=sem_up.at[0, i], recv_sem=sem_up.at[1, i],
            device_id=(lax.rem(growth + 1, slabs), lat), device_id_type=MESH,
        )

    def down_copy(i):
        return pltpu.make_async_remote_copy(
            src_ref=to_low.at[i], dst_ref=from_high.at[i],
            send_sem=sem_down.at[0, i], recv_sem=sem_down.at[1, i],
            device_id=(lax.rem(growth + slabs - 1, slabs), lat), device_id_type=MESH,
        )

    def sweep_up(i):
        inv = pivots_below(i)

        @pl.when(growth > 0)
        def _():
            up_copy(i).wait_recv()

        eigen = [eigen_of(i, tile) for tile in tiles]
        part = [from_low[i, tile, :] for tile in tiles]
        for k in range(depth):
            z = first + k
            face = row(cond, z)
            height = row(heights, z)
            for n, tile in enumerate(tiles):
                inv[n] = inverse_pivot(cond, heights, z, eigen[n], inv[n], face)
                part[n] = (height * f[i, k, tile, :] + face * part[n]) * inv[n]
                inv_s[i, k, tile, :] = inv[n]
                part_s[i, k, tile, :] = part[n]

        @pl.when(growth < slabs - 1)
        def _():
            for n, tile in enumerate(tiles):
                to_high[i, tile, :] = part[n]
            up_copy(i).start()

    def sweep_down(i):
        for tile, value in zip(tiles, pivots_above(i)):
            inv_high[i, tile, :] = value

        @pl.when(growth < slabs - 1)
        def _():
            down_copy(i).wait_recv()

        @pl.when(growth > 0)
        def _():
            for tile in tiles:
                _, part = leap(
                    cond, heights, first, depth, eigen_of(i, tile), inv_high[i, tile, :],
                    from_high[i, tile, :],
                    lambda z: row(heights, z) * f[i, z - first, tile, :], False,
                )
                to_low[i, tile, :] = part
            down_copy(i).start()

    def block_of(rank):
        return rank // share

    def ends_copy(off, owner, target):
        return pltpu.make_async_remote_copy(
            src_ref=ends.at[block_of(target)], dst_ref=ends_in.at[owner],
            send_sem=sem_e.at[0, off], recv_sem=sem_e.at[1, off],
            device_id=(growth, target), device_id_type=MESH,
        )

    def modal_copy(i):
        return pltpu.make_async_copy(modal.at[i], modal_out.at[i], sem_m.at[i])

    def finish(i):
        face = row(cond, first + depth)
        value = []
        weight = [phi[tile, :] for tile in tiles]
        for n, tile in enumerate(tiles):
            inv = inv_s[i, depth - 1, tile, :]
            top = part_s[i, depth - 1, tile, :] + (face * inv) * from_high[i, tile, :]
            value.append(top * reciprocal(1.0 - (face * face) * inv * inv_high[i, tile, :]))
        for k in reversed(range(depth)):
            if k < depth - 1:
                face = row(cond, first + k + 1)
                for n, tile in enumerate(tiles):
                    value[n] = part_s[i, k, tile, :] + (face * inv_s[i, k, tile, :]) * value[n]
            sums = []
            for n, tile in enumerate(tiles):
                modal[i, k, tile, :] = value[n]
                sums.append(jnp.sum(weight[n] * value[n], axis=0, keepdims=True))
            ends[i, k : k + 1, :] = sums[0] + sums[1]
            ends[i, depth + k : depth + k + 1, :] = sums[0] - sums[1]
        modal_copy(i).start()
        for n in range(share):
            target = i * share + n
            off = lax.rem(target + lanes_count - lat, lanes_count)
            pl.when(target != lat)(ends_copy(off, lat, target).start)

    per_pair = PAIR // LANES
    cuts = lanes_count - 1
    middle = nz // 2
    per_step = pl.cdiv(per_slab, lag)

    def face_pivots(j):
        weight = [lam[j, tile, :] for tile in tiles]
        at = pl.ds(pl.multiple_of((lat // share) * LANES, LANES), LANES)
        eigen = [w + lb[:, at] for w in weight]
        low = [jnp.zeros((half, LANES), jnp.float32) for _ in tiles]
        high = list(low)
        for k in range(middle):
            face = row(cond, k)
            z = nz - 1 - k
            face_high = row(cond, z + 1)
            for n, tile in enumerate(tiles):
                low[n] = inverse_pivot(cond, heights, k, eigen[n], low[n], face)
                k_inv[j, k, tile, :] = low[n]
                high[n] = inverse_pivot(cond, heights, z, eigen[n], high[n], face_high)
                k_inv[j, z, tile, :] = high[n]

    def stage(tt, carry):
        @pl.when((tt > 0) & (tt < nblk // per_pair))
        def _():
            transform(tt)

        for side in range(per_pair):
            t = tt * per_pair + side
            up_i = t - LAG * growth
            down_i = t - LAG * (slabs - 1 - growth)
            end_i = t - lag

            for n in range(per_step):
                j = (t - nblk) * per_step + n
                pl.when((j >= 0) & (j < per_slab))(functools.partial(face_pivots, j))

            @pl.when((up_i >= 0) & (up_i < nblk))
            def _():
                sweep_up(up_i)

            @pl.when((down_i >= 0) & (down_i < nblk))
            def _():
                sweep_down(down_i)

            @pl.when((end_i >= 0) & (end_i < nblk))
            def _():
                finish(end_i)

        return carry

    lax.fori_loop(0, pl.cdiv(nblk + lag, per_pair), stage, 0)

    ends_in[lat] = ends[block_of(lat)]

    for off in range(1, lanes_count):
        copy = ends_copy(
            off, lax.rem(lat + lanes_count - off, lanes_count), lax.rem(lat + off, lanes_count)
        )
        copy.wait_send()
        copy.wait_recv()

    sines = [
        [
            math.sqrt(2.0 / lanes_count) * math.sin(math.pi * (c + 1) * (j + 1) / lanes_count)
            for j in range(cuts)
        ]
        for c in range(cuts)
    ]
    jump = [ends_in[c, depth:, :] - ends_in[c + 1, :depth, :] for c in range(cuts)]
    for j in range(cuts):
        total = jump[0] * sines[0][j]
        for c in range(1, cuts):
            total += jump[c] * sines[c][j]
        jumps[j] = total
    for j in range(cuts, jumps.shape[0]):
        jumps[j] = jnp.zeros(jumps.shape[1:], jnp.float32)

    def share_of(rank):
        return pl.ds(rank * per_slab, per_slab)

    jumps_all[growth] = jumps[share_of(growth)]

    def jumps_copy(off, owner, target):
        return pltpu.make_async_remote_copy(
            src_ref=jumps.at[share_of(target)], dst_ref=jumps_all.at[owner],
            send_sem=sem_r.at[0, off], recv_sem=sem_r.at[1, off],
            device_id=(target, lat), device_id_type=MESH,
        )

    for off in range(1, slabs):
        jumps_copy(off, growth, lax.rem(growth + off, slabs)).start()
    for off in range(1, slabs):
        copy = jumps_copy(
            off, lax.rem(growth + slabs - off, slabs), lax.rem(growth + off, slabs)
        )
        copy.wait_send()
        copy.wait_recv()

    def correct(j, carry):
        def held(z):
            return jumps_all[z // depth, j, z % depth : z % depth + 1, :]

        weight = [lam[j, tile, :] for tile in tiles]
        low = [jnp.zeros((half, LANES), jnp.float32) for _ in tiles]
        high = list(low)
        for k in range(middle):
            z = nz - 1 - k
            face = row(cond, k)
            right = row(heights, k) * held(k)
            face_high = row(cond, z + 1)
            right_high = row(heights, z) * held(z)
            for n, tile in enumerate(tiles):
                low[n] = (right + face * low[n]) * k_inv[j, k, tile, :]
                k_part[k, tile, :] = low[n]
                high[n] = (right_high + face_high * high[n]) * k_inv[j, z, tile, :]
                k_part[z, tile, :] = high[n]

        def put(z, value):
            total = sum(
                jnp.sum(w * v, axis=0, keepdims=True) for w, v in zip(weight, value)
            )
            g_modes[growth, j, z : z + 1, :] = held(z) - total * (1.0 / m)

        face = row(cond, middle)
        below, above = [], []
        for n, tile in enumerate(tiles):
            inv_a = face * k_inv[j, middle - 1, tile, :]
            inv_b = face * k_inv[j, middle, tile, :]
            below.append((low[n] + inv_a * high[n]) * reciprocal(1.0 - inv_a * inv_b))
            above.append(high[n] + inv_b * below[n])
        put(middle - 1, below)
        put(middle, above)
        for k in range(1, middle):
            z = middle - 1 - k
            face = row(cond, z + 1)
            for n, tile in enumerate(tiles):
                below[n] = k_part[z, tile, :] + (face * k_inv[j, z, tile, :]) * below[n]
            put(z, below)
            z = middle + k
            face = row(cond, z)
            for n, tile in enumerate(tiles):
                above[n] = k_part[z, tile, :] + (face * k_inv[j, z, tile, :]) * above[n]
            put(z, above)
        for off in range(1, slabs):
            modes_copy(off, growth, j).start()
        return carry

    def modes_copy(off, owner, j):
        return pltpu.make_async_remote_copy(
            src_ref=g_modes.at[owner, j], dst_ref=g_modes.at[owner, j],
            send_sem=sem_j.at[0, off, j], recv_sem=sem_j.at[1, off, j],
            device_id=(lax.rem(growth + off, slabs), lat), device_id_type=MESH,
        )

    lax.fori_loop(0, per_slab, correct, 0)
    for off in range(1, slabs):
        for j in range(per_slab):
            modes_copy(off, growth, j).wait_send()
            modes_copy(off, lax.rem(growth + slabs - off, slabs), j).wait_recv()

    for c in range(cuts):
        total = g_modes[0, 0] * sines[c][0]
        for j in range(1, cuts):
            total += g_modes[j // per_slab, j % per_slab] * sines[c][j]
        g_cuts[c] = total
    for d in range(lanes_count):
        low = g_cuts[d - 1] if d > 0 else jnp.zeros((nz, LANES), jnp.float32)
        high = g_cuts[d] if d < cuts else jnp.zeros((nz, LANES), jnp.float32)
        g_send[d, 0] = high - low
        g_send[d, 1] = -(high + low)

    def g_copy(off, owner, target):
        return pltpu.make_async_remote_copy(
            src_ref=g_send.at[target], dst_ref=g_in.at[block_of(owner)],
            send_sem=sem_g.at[0, off], recv_sem=sem_g.at[1, off],
            device_id=(growth, target), device_id_type=MESH,
        )

    def speaks(rank, act):
        if share == 1:
            act()
        else:
            pl.when(lax.rem(rank, share) == 0)(act)

    def own_block():
        g_in[block_of(lat)] = g_send[lat]

    for off in range(1, lanes_count):
        copy = g_copy(off, lat, lax.rem(lat + off, lanes_count))
        speaks(lat, copy.start)
    speaks(lat, own_block)
    for off in range(1, lanes_count):
        owner = lax.rem(lat + lanes_count - off, lanes_count)
        target = lax.rem(lat + off, lanes_count)
        speaks(lat, g_copy(off, lat, target).wait_send)
        speaks(owner, g_copy(off, owner, target).wait_recv)
    def drain(i, carry):
        @pl.when(growth < slabs - 1)
        def _():
            up_copy(i).wait_send()

        @pl.when(growth > 0)
        def _():
            down_copy(i).wait_send()

        modal_copy(i).wait()
        return carry

    lax.fori_loop(0, nblk, drain, 0)
    jump_out[...] = g_in[...]


def inverse_kernel(
    slabs, modal_in, jump, heights, ty_in, tx, phi, lk, lb,
    out_hbm,
    modal, ty, out, sem_in, sem_out, cond, inv_s, part_s, m3, g3,
):
    growth = lax.axis_index("growth")
    nblk, depth, m = modal.shape[:3]
    per_pair = PAIR // LANES
    pairs = nblk // per_pair
    for n in range(pairs):
        part = pl.ds(n * per_pair, per_pair)
        pltpu.make_async_copy(modal_in.at[part], modal.at[part], sem_in.at[n]).start()
    table = pltpu.make_async_copy(ty_in, ty, sem_in.at[pairs])
    table.start()
    half = m // 2
    tiles = [slice(0, half), slice(half, m)]
    first = growth * depth
    fill_conduct(heights, cond)

    def correct(i, side):
        at = pl.ds(pl.multiple_of(i * LANES, LANES), LANES)
        eigen = [lk[tile, :] + lb[:, at] for tile in tiles]
        zero = jnp.zeros((half, LANES), jnp.float32)

        def advance(z, face, state):
            height = row(heights, z)
            new = []
            for n in range(2):
                inv, part = state[2 * n], state[2 * n + 1]
                inv = inverse_pivot(cond, heights, z, eigen[n], inv, face)
                right = height * jump[i, n, pl.ds(z, 1), :]
                new += [inv, (right + face * part) * inv]
            return tuple(new)

        def up(z, state):
            return advance(z, row(cond, z), state)

        def outside(n, upward):
            def right(z):
                return row(heights, z) * jump[i, n, pl.ds(z, 1), :]

            def one(q, state):
                start = (q if upward else slabs - 1 - q) * depth
                return leap(cond, heights, start, depth, eigen[n], *state, right, upward)

            trips = growth if upward else slabs - 1 - growth
            return lax.fori_loop(0, trips, one, (zero, zero))

        high = outside(0, False) + outside(1, False)
        state = outside(0, True) + outside(1, True)
        for k in range(depth):
            state = up(first + k, state)
            for n, tile in enumerate(tiles):
                inv_s[k, tile, :] = state[2 * n]
                part_s[k, tile, :] = state[2 * n + 1]
        face = row(cond, first + depth)
        value = []
        for n in range(2):
            inv, part = state[2 * n], state[2 * n + 1]
            top = part + (face * inv) * high[2 * n + 1]
            value.append(top * reciprocal(1.0 - (face * face) * inv * high[2 * n]))
        for k in reversed(range(depth)):
            if k < depth - 1:
                face = row(cond, first + k + 1)
            for n, tile in enumerate(tiles):
                if k < depth - 1:
                    value[n] = part_s[k, tile, :] + (face * inv_s[k, tile, :]) * value[n]
                a, b = split(modal[i, k, tile, :] - phi[tile, :] * value[n])
                columns = slice(side * LANES, (side + 1) * LANES)
                for place, part in enumerate((a, a, b)):
                    start = place * m + n * half
                    m3[k, start : start + half, columns] = part

    def pair(tt, carry):
        part = pl.ds(tt * per_pair, per_pair)
        pltpu.make_async_copy(modal_in.at[part], modal.at[part], sem_in.at[tt]).wait()
        for side in range(per_pair):
            correct(tt * per_pair + side, side)
        parity = tt // half_pairs
        offset = lax.rem(tt, half_pairs) * PAIR
        for k in range(depth):
            a, b = split(dot(tx[...], m3[k]))
            for place, part in enumerate((a, b, a)):
                columns = pl.ds(pl.multiple_of(place * mid + offset, PAIR), PAIR)
                g3[parity, k * m : (k + 1) * m, columns] = part
        return carry

    width = out.shape[1]
    mid = width // 2
    half_pairs = mid // PAIR

    lax.fori_loop(0, pairs, pair, 0)
    table.wait()

    rows = out.shape[0]
    chunk = min(256, rows)

    def store(c, side):
        start = c * PAIR if side == 0 else width - (c + 1) * PAIR
        columns = pl.ds(start if isinstance(c, int) else pl.multiple_of(start, PAIR), PAIR)
        return pltpu.make_async_copy(
            out.at[:, columns], out_hbm.at[:, columns], sem_out.at[2 * c + side]
        )

    def columns_of(c, carry):
        columns = pl.ds(pl.multiple_of(c * PAIR, PAIR), PAIR)

        def rows_of(r, inner):
            at = pl.ds(pl.multiple_of(r * chunk, chunk), chunk)
            even = dot(g3[0, at, :], ty[0, :, columns])
            odd = dot(g3[1, at, :], ty[1, :, columns])
            out[at, columns] = even + odd
            far = even - odd
            for q in range(PAIR // LANES):
                start = pl.multiple_of(width - c * PAIR - (q + 1) * LANES, LANES)
                out[at, pl.ds(start, LANES)] = mirror(far[:, q * LANES : (q + 1) * LANES])
            return inner

        lax.fori_loop(0, rows // chunk, rows_of, 0)
        for side in range(2):
            store(c, side).start()
        return carry

    lax.fori_loop(0, half_pairs, columns_of, 0)
    for c in range(half_pairs):
        for side in range(2):
            store(c, side).wait()


def per_device(source, spacing):
    depth, m, width = source.shape
    lanes_count = lax.axis_size("lat")
    slabs = lax.axis_size("growth")
    nz = slabs * depth
    points = m * lanes_count
    nblk = width // LANES
    cuts = lanes_count - 1
    f32 = jnp.float32

    order = np.concatenate([np.arange(0, m, 2), np.arange(1, m, 2)])
    local = cosine_table(m)[order]
    mid = width // 2
    along_y = cosine_table(width)
    halves = np.stack([along_y[0::2, :mid], along_y[1::2, :mid]])
    ty_forward = right_parts(np.swapaxes(halves, 1, 2))
    ty_back = right_parts(halves)
    tx_forward = left_parts(local)
    tx_back = left_parts(local.T)
    mode_y = np.concatenate([np.arange(0, width, 2), np.arange(1, width, 2)])

    def spread_lanes(column):
        return jnp.asarray(np.repeat(np.asarray(column, np.float32)[..., None], LANES, axis=-1))

    phi = spread_lanes(local[:, 0])
    lk = spread_lanes(eigenvalues(order, m))
    lb = jnp.asarray(eigenvalues(mode_y, width).astype(np.float32)[None, :])
    folds = []
    for j in range(1, lanes_count):
        ids = [k for k in range(1, points) if k % (2 * lanes_count) in (j, 2 * lanes_count - j)]
        folds.append(eigenvalues(ids, points))
    per_slab = pl.cdiv(cuts, slabs)
    folds += [folds[0]] * (slabs * per_slab - cuts)
    lam = spread_lanes(np.stack(folds))

    flat = source.reshape(depth * m, width)
    vmem = pl.BlockSpec(memory_space=pltpu.VMEM)
    smem = pl.BlockSpec(memory_space=pltpu.SMEM)
    anywhere = pl.BlockSpec(memory_space=pl.ANY)
    dma = pltpu.SemaphoreType.DMA
    V = pltpu.VMEM
    modal, jump, heights = pl.pallas_call(
        functools.partial(forward_kernel, slabs, lanes_count),
        out_shape=(
            jax.ShapeDtypeStruct((nblk, depth, m, LANES), f32),
            jax.ShapeDtypeStruct((nblk, 2, nz, LANES), f32),
            jax.ShapeDtypeStruct((nz, LANES), f32),
        ),
        in_specs=[anywhere, smem, anywhere] + [vmem] * 4 + [anywhere],
        out_specs=(anywhere, vmem, vmem),
        scratch_shapes=[
            V((nblk, depth, m, LANES), f32),
            V((depth * m, width), f32),
            V((depth, LANES), f32),
            V((2, 3 * mid, mid), jnp.bfloat16),
            V((per_slab, m, LANES), f32),
            V((nz, LANES), f32),
            V((nz + 1, LANES), f32),
            V((2, depth * m, 3 * mid), jnp.bfloat16),
            V((nblk, depth, m, LANES), f32),
            V((nblk, depth, m, LANES), f32),
            V((nblk, depth, m, LANES), f32),
            V((nblk, m, LANES), f32),
            V((nblk, m, LANES), f32),
            V((nblk, m, LANES), f32),
            V((nblk, m, LANES), f32),
            V((nblk, m, LANES), f32),
            V((nblk, 2 * depth, LANES), f32),
            V((lanes_count, 2 * depth, LANES), f32),
            V((slabs * per_slab, depth, LANES), f32),
            V((slabs, per_slab, depth, LANES), f32),
            V((per_slab, nz, m, LANES), f32),
            V((nz, m, LANES), f32),
            V((slabs, per_slab, nz, LANES), f32),
            V((cuts, nz, LANES), f32),
            V((lanes_count, 2, nz, LANES), f32),
            V((nblk, 2, nz, LANES), f32),
            dma((3,)),
            dma((nblk,)),
            dma((2, slabs)),
            dma((2, nblk)),
            dma((2, nblk)),
            dma((2, lanes_count)),
            dma((2, slabs)),
            dma((2, slabs, per_slab)),
            dma((2, lanes_count)),
        ],
        compiler_params=pltpu.CompilerParams(
            collective_id=0, has_side_effects=True, vmem_limit_bytes=VMEM_BYTES
        ),
        name="slab_solve",
    )(flat, spacing, ty_forward, tx_forward, phi, lk, lb, lam)

    result = pl.pallas_call(
        functools.partial(inverse_kernel, slabs),
        out_shape=jax.ShapeDtypeStruct((depth * m, width), f32),
        in_specs=[anywhere, vmem, vmem, anywhere] + [vmem] * 4,
        out_specs=anywhere,
        scratch_shapes=[
            V((nblk, depth, m, LANES), f32),
            V((2, 3 * mid, mid), jnp.bfloat16),
            V((depth * m, width), f32),
            dma((width // PAIR + 2,)),
            dma((width // PAIR,)),
            V((nz + 1, LANES), f32),
            V((depth, m, LANES), f32),
            V((depth, m, LANES), f32),
            V((depth, 3 * m, PAIR), jnp.bfloat16),
            V((2, depth * m, 3 * mid), jnp.bfloat16),
        ],
        compiler_params=pltpu.CompilerParams(vmem_limit_bytes=VMEM_BYTES),
        name="face_correction",
    )(modal, jump, heights, ty_back, tx_back, phi, lk, lb)
    return result.reshape(depth, m, width)


def solution(mesh):
    return jax.shard_map(
        per_device,
        mesh=mesh,
        in_specs=(P("growth", "lat", None), P("growth")),
        out_specs=P("growth", "lat", None),
        check_vma=False,
    )
```

```python
import functools
import math

import jax
import jax.numpy as jnp
import ml_dtypes
import numpy as np
from jax import lax
from jax.experimental import pallas as pl
from jax.experimental.pallas import tpu as pltpu
from jax.sharding import PartitionSpec as P

LANES = 128
PAIR = 256
LAG = 3
MESH = pl.DeviceIdType.MESH
VMEM_BYTES = 56 * 1024 * 1024


def cosine_table(points):
    ids = np.arange(points, dtype=np.int64)
    phase = (2 * ids[None, :] + 1) * ids[:, None] % (4 * points)
    scale = np.where(ids == 0, math.sqrt(1.0 / points), math.sqrt(2.0 / points))
    return scale[:, None] * np.cos(phase * (math.pi / (2.0 * points)))


def eigenvalues(ids, points):
    return 4.0 * np.sin(np.asarray(ids) * (math.pi / (2.0 * points))) ** 2


def two_parts(table):
    high = table.astype(ml_dtypes.bfloat16)
    low = (table - high.astype(np.float64)).astype(ml_dtypes.bfloat16)
    return high, low


def left_parts(table):
    high, low = two_parts(table)
    return jnp.asarray(np.concatenate([high, low, high], axis=-1))


def right_parts(table):
    high, low = two_parts(table)
    return jnp.asarray(np.concatenate([high, high, low], axis=-2))


def mirror(value):
    lanes = lax.broadcasted_iota(jnp.int32, value.shape, 1)
    return jnp.take_along_axis(value, LANES - 1 - lanes, axis=1, mode="promise_in_bounds")


def split(value):
    high = value.astype(jnp.bfloat16)
    low = (value - high.astype(jnp.float32)).astype(jnp.bfloat16)
    return high, low


def dot(a, b):
    return jnp.dot(a, b, preferred_element_type=jnp.float32)


def stacked(value):
    high, low = split(value)
    return jnp.concatenate([high, high, low], axis=0)


def reciprocal(x):
    guess = pl.reciprocal(x, approx=True)
    return guess * (2.0 - x * guess)


def fill_conduct(heights_ref, cond_ref):
    heights = heights_ref[...]
    zero = jnp.zeros((1, LANES), jnp.float32)
    cond_ref[...] = 2.0 / (
        jnp.concatenate([zero, heights], axis=0) + jnp.concatenate([heights, zero], axis=0)
    )


def row(ref, z):
    return ref[pl.ds(z, 1), :]


def inverse_pivot(cond_ref, heights_ref, z, eigen, behind, face):
    diagonal = (row(cond_ref, z) + row(cond_ref, z + 1)) + row(heights_ref, z) * eigen
    return reciprocal(diagonal - (face * face) * behind)


def leap(cond_ref, heights_ref, first, depth, eigen, inv, part, right, upward):
    newest, before = None, inv
    for k in range(depth):
        z = first + (k if upward else depth - 1 - k)
        face = row(cond_ref, z if upward else z + 1)
        diagonal = (row(cond_ref, z) + row(cond_ref, z + 1)) + row(heights_ref, z) * eigen
        if newest is None:
            part = right(z) + face * part if right else None
            newest, before = diagonal - (face * face) * before, 1.0
        else:
            part = right(z) * newest + face * part if right else None
            newest, before = diagonal * newest - (face * face) * before, newest
    scale = reciprocal(newest)
    return before * scale, part * scale if right else None


def forward_kernel(
    slabs, lanes_count, src_in, spacing, ty_in, tx, phi, lk, lb, lam_in,
    modal_out, jump_out, heights_out,
    modal, src, spread, ty, lam, heights, cond, x3, f, inv_s, part_s, inv_high, from_low, from_high,
    to_low, to_high, ends, ends_in, jumps, jumps_all, k_inv, k_part, g_modes, g_cuts,
    g_send, g_in, sem_in, sem_m, sem_h, sem_up, sem_down, sem_e, sem_r, sem_j, sem_g,
):
    growth = lax.axis_index("growth")
    lat = lax.axis_index("lat")
    depth, m = f.shape[1], f.shape[2]
    half = m // 2
    nblk = f.shape[0]
    nz = slabs * depth
    width = src.shape[1]
    share = max(1, lanes_count // nblk)
    tiles = [slice(0, half), slice(half, m)]
    lag = LAG * (slabs - 1)
    per_slab = lam.shape[0]

    loads = [
        pltpu.make_async_copy(a, b, sem_in.at[n])
        for n, (a, b) in enumerate(
            [
                (src_in, src),
                (ty_in, ty),
                (lam_in.at[pl.ds(growth * per_slab, per_slab)], lam),
            ]
        )
    ]
    for load in loads:
        load.start()
    for k in range(depth):
        spread[k : k + 1, :] = jnp.full((1, LANES), spacing[k], jnp.float32)

    barrier = pltpu.get_barrier_semaphore()
    for off in range(1, slabs):
        pl.semaphore_signal(
            barrier, inc=1, device_id=(lax.rem(growth + off, slabs), lat), device_id_type=MESH
        )
    for off in range(1, lanes_count):
        pl.semaphore_signal(
            barrier, inc=1, device_id=(growth, lax.rem(lat + off, lanes_count)),
            device_id_type=MESH,
        )
    pl.semaphore_wait(barrier, slabs + lanes_count - 2)

    def height_copy(off, owner, target):
        return pltpu.make_async_remote_copy(
            src_ref=spread,
            dst_ref=heights.at[pl.ds(owner * depth, depth)],
            send_sem=sem_h.at[0, off],
            recv_sem=sem_h.at[1, off],
            device_id=(target, lat),
            device_id_type=MESH,
        )

    for off in range(1, slabs):
        height_copy(off, growth, lax.rem(growth + off, slabs)).start()
    heights[pl.ds(growth * depth, depth), :] = spread[...]
    rows = src.shape[0]
    loads[0].wait()

    mid = width // 2

    def split_rows(i, carry):
        at = pl.ds(pl.multiple_of(i * m, m), m)
        for q in range(mid // LANES):
            near = src[at, q * LANES : (q + 1) * LANES]
            far = mirror(src[at, width - (q + 1) * LANES : width - q * LANES])
            for n, value in enumerate((near + far, near - far)):
                high, low = split(value)
                for place, part in enumerate((high, low, high)):
                    start = place * mid + q * LANES
                    x3[n, at, start : start + LANES] = part
        return carry

    lax.fori_loop(0, depth, split_rows, 0)
    def eigen_of(i, tile):
        at = pl.ds(pl.multiple_of(i * LANES, LANES), LANES)
        return lk[tile, :] + lb[:, at]

    def pivots_below(i):
        def one(tile):
            eigen = eigen_of(i, tile)
            return lax.fori_loop(
                0, growth,
                lambda n, inv: leap(
                    cond, heights, n * depth, depth, eigen, inv, None, None, True
                )[0],
                jnp.zeros((half, LANES), jnp.float32),
            )

        return [one(tile) for tile in tiles]

    def pivots_above(i):
        def one(tile):
            eigen = eigen_of(i, tile)
            return lax.fori_loop(
                0, slabs - 1 - growth,
                lambda n, inv: leap(
                    cond, heights, (slabs - 1 - n) * depth, depth, eigen, inv, None, None, False
                )[0],
                jnp.zeros((half, LANES), jnp.float32),
            )

        return [one(tile) for tile in tiles]

    @pl.when(growth == 0)
    def _():
        from_low[...] = jnp.zeros_like(from_low)

    @pl.when(growth == slabs - 1)
    def _():
        from_high[...] = jnp.zeros_like(from_high)

    first = growth * depth
    chunk = min(512, rows)
    planes = chunk // m

    half_pairs = mid // PAIR

    def transform(pair):
        parity = pair // half_pairs
        columns = pl.ds(pl.multiple_of(lax.rem(pair, half_pairs) * PAIR, PAIR), PAIR)

        def one(c, carry):
            at = pl.ds(pl.multiple_of(c * chunk, chunk), chunk)
            along_y = dot(x3[parity, at, :], ty[parity, :, columns])
            for k in range(planes):
                part = slice(k * m, (k + 1) * m)
                both = dot(tx[...], stacked(along_y[part, :]))
                for side in range(PAIR // LANES):
                    f[pair * (PAIR // LANES) + side, c * planes + k] = both[
                        :, side * LANES : (side + 1) * LANES
                    ]
            return carry

        lax.fori_loop(0, rows // chunk, one, 0)

    loads[1].wait()
    transform(0)
    for off in range(1, slabs):
        behind = lax.rem(growth + slabs - off, slabs)
        copy = height_copy(off, behind, lax.rem(growth + off, slabs))
        copy.wait_send()
        copy.wait_recv()
    fill_conduct(heights, cond)
    heights_out[...] = heights[...]
    loads[2].wait()

    def up_copy(i):
        return pltpu.make_async_remote_copy(
            src_ref=to_high.at[i], dst_ref=from_low.at[i],
            send_sem=sem_up.at[0, i], recv_sem=sem_up.at[1, i],
            device_id=(lax.rem(growth + 1, slabs), lat), device_id_type=MESH,
        )

    def down_copy(i):
        return pltpu.make_async_remote_copy(
            src_ref=to_low.at[i], dst_ref=from_high.at[i],
            send_sem=sem_down.at[0, i], recv_sem=sem_down.at[1, i],
            device_id=(lax.rem(growth + slabs - 1, slabs), lat), device_id_type=MESH,
        )

    def sweep_up(i):
        inv = pivots_below(i)

        @pl.when(growth > 0)
        def _():
            up_copy(i).wait_recv()

        eigen = [eigen_of(i, tile) for tile in tiles]
        part = [from_low[i, tile, :] for tile in tiles]
        for k in range(depth):
            z = first + k
            face = row(cond, z)
            height = row(heights, z)
            for n, tile in enumerate(tiles):
                inv[n] = inverse_pivot(cond, heights, z, eigen[n], inv[n], face)
                part[n] = (height * f[i, k, tile, :] + face * part[n]) * inv[n]
                inv_s[i, k, tile, :] = inv[n]
                part_s[i, k, tile, :] = part[n]

        @pl.when(growth < slabs - 1)
        def _():
            for n, tile in enumerate(tiles):
                to_high[i, tile, :] = part[n]
            up_copy(i).start()

    def sweep_down(i):
        for tile, value in zip(tiles, pivots_above(i)):
            inv_high[i, tile, :] = value

        @pl.when(growth < slabs - 1)
        def _():
            down_copy(i).wait_recv()

        @pl.when(growth > 0)
        def _():
            for tile in tiles:
                _, part = leap(
                    cond, heights, first, depth, eigen_of(i, tile), inv_high[i, tile, :],
                    from_high[i, tile, :],
                    lambda z: row(heights, z) * f[i, z - first, tile, :], False,
                )
                to_low[i, tile, :] = part
            down_copy(i).start()

    def block_of(rank):
        return rank // share

    def ends_copy(off, owner, target):
        return pltpu.make_async_remote_copy(
            src_ref=ends.at[block_of(target)], dst_ref=ends_in.at[owner],
            send_sem=sem_e.at[0, off], recv_sem=sem_e.at[1, off],
            device_id=(growth, target), device_id_type=MESH,
        )

    def modal_copy(i):
        return pltpu.make_async_copy(modal.at[i], modal_out.at[i], sem_m.at[i])

    def finish(i):
        face = row(cond, first + depth)
        value = []
        weight = [phi[tile, :] for tile in tiles]
        for n, tile in enumerate(tiles):
            inv = inv_s[i, depth - 1, tile, :]
            top = part_s[i, depth - 1, tile, :] + (face * inv) * from_high[i, tile, :]
            value.append(top * reciprocal(1.0 - (face * face) * inv * inv_high[i, tile, :]))
        for k in reversed(range(depth)):
            if k < depth - 1:
                face = row(cond, first + k + 1)
                for n, tile in enumerate(tiles):
                    value[n] = part_s[i, k, tile, :] + (face * inv_s[i, k, tile, :]) * value[n]
            sums = []
            for n, tile in enumerate(tiles):
                modal[i, k, tile, :] = value[n]
                sums.append(jnp.sum(weight[n] * value[n], axis=0, keepdims=True))
            ends[i, k : k + 1, :] = sums[0] + sums[1]
            ends[i, depth + k : depth + k + 1, :] = sums[0] - sums[1]
        modal_copy(i).start()
        for n in range(share):
            target = i * share + n
            off = lax.rem(target + lanes_count - lat, lanes_count)
            pl.when(target != lat)(ends_copy(off, lat, target).start)

    per_pair = PAIR // LANES
    cuts = lanes_count - 1
    middle = nz // 2
    per_step = pl.cdiv(per_slab, lag)

    def face_pivots(j):
        weight = [lam[j, tile, :] for tile in tiles]
        at = pl.ds(pl.multiple_of((lat // share) * LANES, LANES), LANES)
        eigen = [w + lb[:, at] for w in weight]
        low = [jnp.zeros((half, LANES), jnp.float32) for _ in tiles]
        high = list(low)
        for k in range(middle):
            face = row(cond, k)
            z = nz - 1 - k
            face_high = row(cond, z + 1)
            for n, tile in enumerate(tiles):
                low[n] = inverse_pivot(cond, heights, k, eigen[n], low[n], face)
                k_inv[j, k, tile, :] = low[n]
                high[n] = inverse_pivot(cond, heights, z, eigen[n], high[n], face_high)
                k_inv[j, z, tile, :] = high[n]

    def stage(tt, carry):
        @pl.when((tt > 0) & (tt < nblk // per_pair))
        def _():
            transform(tt)

        for side in range(per_pair):
            t = tt * per_pair + side
            up_i = t - LAG * growth
            down_i = t - LAG * (slabs - 1 - growth)
            end_i = t - lag

            for n in range(per_step):
                j = (t - nblk) * per_step + n
                pl.when((j >= 0) & (j < per_slab))(functools.partial(face_pivots, j))

            @pl.when((up_i >= 0) & (up_i < nblk))
            def _():
                sweep_up(up_i)

            @pl.when((down_i >= 0) & (down_i < nblk))
            def _():
                sweep_down(down_i)

            @pl.when((end_i >= 0) & (end_i < nblk))
            def _():
                finish(end_i)

        return carry

    lax.fori_loop(0, pl.cdiv(nblk + lag, per_pair), stage, 0)

    ends_in[lat] = ends[block_of(lat)]

    for off in range(1, lanes_count):
        copy = ends_copy(
            off, lax.rem(lat + lanes_count - off, lanes_count), lax.rem(lat + off, lanes_count)
        )
        copy.wait_send()
        copy.wait_recv()

    sines = [
        [
            math.sqrt(2.0 / lanes_count) * math.sin(math.pi * (c + 1) * (j + 1) / lanes_count)
            for j in range(cuts)
        ]
        for c in range(cuts)
    ]
    jump = [ends_in[c, depth:, :] - ends_in[c + 1, :depth, :] for c in range(cuts)]
    for j in range(cuts):
        total = jump[0] * sines[0][j]
        for c in range(1, cuts):
            total += jump[c] * sines[c][j]
        jumps[j] = total
    for j in range(cuts, jumps.shape[0]):
        jumps[j] = jnp.zeros(jumps.shape[1:], jnp.float32)

    def share_of(rank):
        return pl.ds(rank * per_slab, per_slab)

    jumps_all[growth] = jumps[share_of(growth)]

    def jumps_copy(off, owner, target):
        return pltpu.make_async_remote_copy(
            src_ref=jumps.at[share_of(target)], dst_ref=jumps_all.at[owner],
            send_sem=sem_r.at[0, off], recv_sem=sem_r.at[1, off],
            device_id=(target, lat), device_id_type=MESH,
        )

    for off in range(1, slabs):
        jumps_copy(off, growth, lax.rem(growth + off, slabs)).start()
    for off in range(1, slabs):
        copy = jumps_copy(
            off, lax.rem(growth + slabs - off, slabs), lax.rem(growth + off, slabs)
        )
        copy.wait_send()
        copy.wait_recv()

    def correct(j, carry):
        def held(z):
            return jumps_all[z // depth, j, z % depth : z % depth + 1, :]

        weight = [lam[j, tile, :] for tile in tiles]
        low = [jnp.zeros((half, LANES), jnp.float32) for _ in tiles]
        high = list(low)
        for k in range(middle):
            z = nz - 1 - k
            face = row(cond, k)
            right = row(heights, k) * held(k)
            face_high = row(cond, z + 1)
            right_high = row(heights, z) * held(z)
            for n, tile in enumerate(tiles):
                low[n] = (right + face * low[n]) * k_inv[j, k, tile, :]
                k_part[k, tile, :] = low[n]
                high[n] = (right_high + face_high * high[n]) * k_inv[j, z, tile, :]
                k_part[z, tile, :] = high[n]

        def put(z, value):
            total = sum(
                jnp.sum(w * v, axis=0, keepdims=True) for w, v in zip(weight, value)
            )
            g_modes[growth, j, z : z + 1, :] = held(z) - total * (1.0 / m)

        face = row(cond, middle)
        below, above = [], []
        for n, tile in enumerate(tiles):
            inv_a = face * k_inv[j, middle - 1, tile, :]
            inv_b = face * k_inv[j, middle, tile, :]
            below.append((low[n] + inv_a * high[n]) * reciprocal(1.0 - inv_a * inv_b))
            above.append(high[n] + inv_b * below[n])
        put(middle - 1, below)
        put(middle, above)
        for k in range(1, middle):
            z = middle - 1 - k
            face = row(cond, z + 1)
            for n, tile in enumerate(tiles):
                below[n] = k_part[z, tile, :] + (face * k_inv[j, z, tile, :]) * below[n]
            put(z, below)
            z = middle + k
            face = row(cond, z)
            for n, tile in enumerate(tiles):
                above[n] = k_part[z, tile, :] + (face * k_inv[j, z, tile, :]) * above[n]
            put(z, above)
        for off in range(1, slabs):
            modes_copy(off, growth, j).start()
        return carry

    def modes_copy(off, owner, j):
        return pltpu.make_async_remote_copy(
            src_ref=g_modes.at[owner, j], dst_ref=g_modes.at[owner, j],
            send_sem=sem_j.at[0, off, j], recv_sem=sem_j.at[1, off, j],
            device_id=(lax.rem(growth + off, slabs), lat), device_id_type=MESH,
        )

    lax.fori_loop(0, per_slab, correct, 0)
    for off in range(1, slabs):
        for j in range(per_slab):
            modes_copy(off, growth, j).wait_send()
            modes_copy(off, lax.rem(growth + slabs - off, slabs), j).wait_recv()

    for c in range(cuts):
        total = g_modes[0, 0] * sines[c][0]
        for j in range(1, cuts):
            total += g_modes[j // per_slab, j % per_slab] * sines[c][j]
        g_cuts[c] = total
    for d in range(lanes_count):
        low = g_cuts[d - 1] if d > 0 else jnp.zeros((nz, LANES), jnp.float32)
        high = g_cuts[d] if d < cuts else jnp.zeros((nz, LANES), jnp.float32)
        g_send[d, 0] = high - low
        g_send[d, 1] = -(high + low)

    def g_copy(off, owner, target):
        return pltpu.make_async_remote_copy(
            src_ref=g_send.at[target], dst_ref=g_in.at[block_of(owner)],
            send_sem=sem_g.at[0, off], recv_sem=sem_g.at[1, off],
            device_id=(growth, target), device_id_type=MESH,
        )

    def speaks(rank, act):
        if share == 1:
            act()
        else:
            pl.when(lax.rem(rank, share) == 0)(act)

    def own_block():
        g_in[block_of(lat)] = g_send[lat]

    for off in range(1, lanes_count):
        copy = g_copy(off, lat, lax.rem(lat + off, lanes_count))
        speaks(lat, copy.start)
    speaks(lat, own_block)
    for off in range(1, lanes_count):
        owner = lax.rem(lat + lanes_count - off, lanes_count)
        target = lax.rem(lat + off, lanes_count)
        speaks(lat, g_copy(off, lat, target).wait_send)
        speaks(owner, g_copy(off, owner, target).wait_recv)
    def drain(i, carry):
        @pl.when(growth < slabs - 1)
        def _():
            up_copy(i).wait_send()

        @pl.when(growth > 0)
        def _():
            down_copy(i).wait_send()

        modal_copy(i).wait()
        return carry

    lax.fori_loop(0, nblk, drain, 0)
    jump_out[...] = g_in[...]


def inverse_kernel(
    slabs, modal_in, jump, heights, ty_in, tx, phi, lk, lb,
    out_hbm,
    modal, ty, out, sem_in, sem_out, cond, inv_s, part_s, m3, g3,
):
    growth = lax.axis_index("growth")
    nblk, depth, m = modal.shape[:3]
    per_pair = PAIR // LANES
    pairs = nblk // per_pair
    for n in range(pairs):
        part = pl.ds(n * per_pair, per_pair)
        pltpu.make_async_copy(modal_in.at[part], modal.at[part], sem_in.at[n]).start()
    table = pltpu.make_async_copy(ty_in, ty, sem_in.at[pairs])
    table.start()
    half = m // 2
    tiles = [slice(0, half), slice(half, m)]
    first = growth * depth
    fill_conduct(heights, cond)

    def correct(i, side, slot, jobs):
        at = pl.ds(pl.multiple_of(i * LANES, LANES), LANES)
        eigen = [lk[tile, :] + lb[:, at] for tile in tiles]
        zero = jnp.zeros((half, LANES), jnp.float32)

        def advance(z, face, state):
            height = row(heights, z)
            new = []
            for n in range(2):
                inv, part = state[2 * n], state[2 * n + 1]
                inv = inverse_pivot(cond, heights, z, eigen[n], inv, face)
                right = height * jump[i, n, pl.ds(z, 1), :]
                new += [inv, (right + face * part) * inv]
            return tuple(new)

        def up(z, state):
            return advance(z, row(cond, z), state)

        def outside(n, upward):
            def right(z):
                return row(heights, z) * jump[i, n, pl.ds(z, 1), :]

            def one(q, state):
                start = (q if upward else slabs - 1 - q) * depth
                return leap(cond, heights, start, depth, eigen[n], *state, right, upward)

            trips = growth if upward else slabs - 1 - growth
            return lax.fori_loop(0, trips, one, (zero, zero))

        high = outside(0, False) + outside(1, False)
        state = outside(0, True) + outside(1, True)
        for k in range(depth):
            for job in jobs[k::depth]:
                job()
            state = up(first + k, state)
            for n, tile in enumerate(tiles):
                inv_s[k, tile, :] = state[2 * n]
                part_s[k, tile, :] = state[2 * n + 1]
        face = row(cond, first + depth)
        value = []
        for n in range(2):
            inv, part = state[2 * n], state[2 * n + 1]
            top = part + (face * inv) * high[2 * n + 1]
            value.append(top * reciprocal(1.0 - (face * face) * inv * high[2 * n]))
        for k in reversed(range(depth)):
            if k < depth - 1:
                face = row(cond, first + k + 1)
            for n, tile in enumerate(tiles):
                if k < depth - 1:
                    value[n] = part_s[k, tile, :] + (face * inv_s[k, tile, :]) * value[n]
                a, b = split(modal[i, k, tile, :] - phi[tile, :] * value[n])
                columns = slice(side * LANES, (side + 1) * LANES)
                for place, part in enumerate((a, a, b)):
                    start = place * m + n * half
                    m3[slot, k, start : start + half, columns] = part

    width = out.shape[1]
    mid = width // 2
    half_pairs = mid // PAIR
    rows = out.shape[0]
    chunk = min(256, rows)

    def along_x(tt, k):
        a, b = split(dot(tx[...], m3[tt % 2, k]))
        for place, part in enumerate((a, b, a)):
            start = place * mid + (tt % half_pairs) * PAIR
            g3[tt // half_pairs, k * m : (k + 1) * m, start : start + PAIR] = part

    def even_part(r, c):
        at = slice(r * chunk, (r + 1) * chunk)
        columns = slice(c * PAIR, (c + 1) * PAIR)
        out[at, columns] = dot(g3[0, at, :], ty[0, :, columns])

    for tt in range(pairs):
        part = pl.ds(tt * per_pair, per_pair)
        pltpu.make_async_copy(modal_in.at[part], modal.at[part], sem_in.at[tt]).wait()
        jobs = []
        if tt > 0:
            jobs += [functools.partial(along_x, tt - 1, k) for k in range(depth)]
        if tt == pairs - 1:
            table.wait()
            jobs += [
                functools.partial(even_part, r, c)
                for c in range(half_pairs)
                for r in range(rows // chunk)
            ]
        for side in range(per_pair):
            correct(tt * per_pair + side, side, tt % 2, jobs[side::per_pair])
    for k in range(depth):
        along_x(pairs - 1, k)

    def store(c, side):
        start = c * PAIR if side == 0 else width - (c + 1) * PAIR
        columns = pl.ds(start if isinstance(c, int) else pl.multiple_of(start, PAIR), PAIR)
        return pltpu.make_async_copy(
            out.at[:, columns], out_hbm.at[:, columns], sem_out.at[2 * c + side]
        )

    def columns_of(c, carry):
        columns = pl.ds(pl.multiple_of(c * PAIR, PAIR), PAIR)

        def rows_of(r, inner):
            at = pl.ds(pl.multiple_of(r * chunk, chunk), chunk)
            even = out[at, columns]
            odd = dot(g3[1, at, :], ty[1, :, columns])
            out[at, columns] = even + odd
            far = even - odd
            for q in range(PAIR // LANES):
                start = pl.multiple_of(width - c * PAIR - (q + 1) * LANES, LANES)
                out[at, pl.ds(start, LANES)] = mirror(far[:, q * LANES : (q + 1) * LANES])
            return inner

        lax.fori_loop(0, rows // chunk, rows_of, 0)
        for side in range(2):
            store(c, side).start()
        return carry

    lax.fori_loop(0, half_pairs, columns_of, 0)
    for c in range(half_pairs):
        for side in range(2):
            store(c, side).wait()


def per_device(source, spacing):
    depth, m, width = source.shape
    lanes_count = lax.axis_size("lat")
    slabs = lax.axis_size("growth")
    nz = slabs * depth
    points = m * lanes_count
    nblk = width // LANES
    cuts = lanes_count - 1
    f32 = jnp.float32

    order = np.concatenate([np.arange(0, m, 2), np.arange(1, m, 2)])
    local = cosine_table(m)[order]
    mid = width // 2
    along_y = cosine_table(width)
    halves = np.stack([along_y[0::2, :mid], along_y[1::2, :mid]])
    ty_forward = right_parts(np.swapaxes(halves, 1, 2))
    ty_back = right_parts(halves)
    tx_forward = left_parts(local)
    tx_back = left_parts(local.T)
    mode_y = np.concatenate([np.arange(0, width, 2), np.arange(1, width, 2)])

    def spread_lanes(column):
        return jnp.asarray(np.repeat(np.asarray(column, np.float32)[..., None], LANES, axis=-1))

    phi = spread_lanes(local[:, 0])
    lk = spread_lanes(eigenvalues(order, m))
    lb = jnp.asarray(eigenvalues(mode_y, width).astype(np.float32)[None, :])
    folds = []
    for j in range(1, lanes_count):
        ids = [k for k in range(1, points) if k % (2 * lanes_count) in (j, 2 * lanes_count - j)]
        folds.append(eigenvalues(ids, points))
    per_slab = pl.cdiv(cuts, slabs)
    folds += [folds[0]] * (slabs * per_slab - cuts)
    lam = spread_lanes(np.stack(folds))

    flat = source.reshape(depth * m, width)
    vmem = pl.BlockSpec(memory_space=pltpu.VMEM)
    smem = pl.BlockSpec(memory_space=pltpu.SMEM)
    anywhere = pl.BlockSpec(memory_space=pl.ANY)
    dma = pltpu.SemaphoreType.DMA
    V = pltpu.VMEM
    modal, jump, heights = pl.pallas_call(
        functools.partial(forward_kernel, slabs, lanes_count),
        out_shape=(
            jax.ShapeDtypeStruct((nblk, depth, m, LANES), f32),
            jax.ShapeDtypeStruct((nblk, 2, nz, LANES), f32),
            jax.ShapeDtypeStruct((nz, LANES), f32),
        ),
        in_specs=[anywhere, smem, anywhere] + [vmem] * 4 + [anywhere],
        out_specs=(anywhere, vmem, vmem),
        scratch_shapes=[
            V((nblk, depth, m, LANES), f32),
            V((depth * m, width), f32),
            V((depth, LANES), f32),
            V((2, 3 * mid, mid), jnp.bfloat16),
            V((per_slab, m, LANES), f32),
            V((nz, LANES), f32),
            V((nz + 1, LANES), f32),
            V((2, depth * m, 3 * mid), jnp.bfloat16),
            V((nblk, depth, m, LANES), f32),
            V((nblk, depth, m, LANES), f32),
            V((nblk, depth, m, LANES), f32),
            V((nblk, m, LANES), f32),
            V((nblk, m, LANES), f32),
            V((nblk, m, LANES), f32),
            V((nblk, m, LANES), f32),
            V((nblk, m, LANES), f32),
            V((nblk, 2 * depth, LANES), f32),
            V((lanes_count, 2 * depth, LANES), f32),
            V((slabs * per_slab, depth, LANES), f32),
            V((slabs, per_slab, depth, LANES), f32),
            V((per_slab, nz, m, LANES), f32),
            V((nz, m, LANES), f32),
            V((slabs, per_slab, nz, LANES), f32),
            V((cuts, nz, LANES), f32),
            V((lanes_count, 2, nz, LANES), f32),
            V((nblk, 2, nz, LANES), f32),
            dma((3,)),
            dma((nblk,)),
            dma((2, slabs)),
            dma((2, nblk)),
            dma((2, nblk)),
            dma((2, lanes_count)),
            dma((2, slabs)),
            dma((2, slabs, per_slab)),
            dma((2, lanes_count)),
        ],
        compiler_params=pltpu.CompilerParams(
            collective_id=0, has_side_effects=True, vmem_limit_bytes=VMEM_BYTES
        ),
        name="slab_solve",
    )(flat, spacing, ty_forward, tx_forward, phi, lk, lb, lam)

    result = pl.pallas_call(
        functools.partial(inverse_kernel, slabs),
        out_shape=jax.ShapeDtypeStruct((depth * m, width), f32),
        in_specs=[anywhere, vmem, vmem, anywhere] + [vmem] * 4,
        out_specs=anywhere,
        scratch_shapes=[
            V((nblk, depth, m, LANES), f32),
            V((2, 3 * mid, mid), jnp.bfloat16),
            V((depth * m, width), f32),
            dma((width // PAIR + 2,)),
            dma((width // PAIR,)),
            V((nz + 1, LANES), f32),
            V((depth, m, LANES), f32),
            V((depth, m, LANES), f32),
            V((2, depth, 3 * m, PAIR), jnp.bfloat16),
            V((2, depth * m, 3 * mid), jnp.bfloat16),
        ],
        compiler_params=pltpu.CompilerParams(vmem_limit_bytes=VMEM_BYTES),
        name="face_correction",
    )(modal, jump, heights, ty_back, tx_back, phi, lk, lb)
    return result.reshape(depth, m, width)


def solution(mesh):
    return jax.shard_map(
        per_device,
        mesh=mesh,
        in_specs=(P("growth", "lat", None), P("growth")),
        out_specs=P("growth", "lat", None),
        check_vma=False,
    )
```

```python
import functools
import math

import jax
import jax.numpy as jnp
import ml_dtypes
import numpy as np
from jax import lax
from jax.experimental import pallas as pl
from jax.experimental.pallas import tpu as pltpu
from jax.sharding import PartitionSpec as P

LANES = 128
PAIR = 256
LAG = 3
MESH = pl.DeviceIdType.MESH
VMEM_BYTES = 56 * 1024 * 1024


def cosine_table(points):
    ids = np.arange(points, dtype=np.int64)
    phase = (2 * ids[None, :] + 1) * ids[:, None] % (4 * points)
    scale = np.where(ids == 0, math.sqrt(1.0 / points), math.sqrt(2.0 / points))
    return scale[:, None] * np.cos(phase * (math.pi / (2.0 * points)))


def eigenvalues(ids, points):
    return 4.0 * np.sin(np.asarray(ids) * (math.pi / (2.0 * points))) ** 2


def two_parts(table):
    high = table.astype(ml_dtypes.bfloat16)
    low = (table - high.astype(np.float64)).astype(ml_dtypes.bfloat16)
    return high, low


def left_parts(table):
    high, low = two_parts(table)
    return jnp.asarray(np.concatenate([high, low, high], axis=-1))


def right_parts(table):
    high, low = two_parts(table)
    return jnp.asarray(np.concatenate([high, high, low], axis=-2))


def mirror(value):
    lanes = lax.broadcasted_iota(jnp.int32, value.shape, 1)
    return jnp.take_along_axis(value, LANES - 1 - lanes, axis=1, mode="promise_in_bounds")


def split(value):
    high = value.astype(jnp.bfloat16)
    low = (value - high.astype(jnp.float32)).astype(jnp.bfloat16)
    return high, low


def dot(a, b):
    return jnp.dot(a, b, preferred_element_type=jnp.float32)


def stacked(value):
    high, low = split(value)
    return jnp.concatenate([high, high, low], axis=0)


def reciprocal(x):
    guess = pl.reciprocal(x, approx=True)
    return guess * (2.0 - x * guess)


def fill_conduct(heights_ref, cond_ref):
    heights = heights_ref[...]
    zero = jnp.zeros((1, LANES), jnp.float32)
    cond_ref[...] = 2.0 / (
        jnp.concatenate([zero, heights], axis=0) + jnp.concatenate([heights, zero], axis=0)
    )


def row(ref, z):
    return ref[pl.ds(z, 1), :]


def inverse_pivot(cond_ref, heights_ref, z, eigen, behind, face):
    diagonal = (row(cond_ref, z) + row(cond_ref, z + 1)) + row(heights_ref, z) * eigen
    return reciprocal(diagonal - (face * face) * behind)


def leap(cond_ref, heights_ref, first, depth, eigen, inv, part, right, upward):
    newest, before = None, inv
    for k in range(depth):
        z = first + (k if upward else depth - 1 - k)
        face = row(cond_ref, z if upward else z + 1)
        diagonal = (row(cond_ref, z) + row(cond_ref, z + 1)) + row(heights_ref, z) * eigen
        if newest is None:
            part = right(z) + face * part if right else None
            newest, before = diagonal - (face * face) * before, 1.0
        else:
            part = right(z) * newest + face * part if right else None
            newest, before = diagonal * newest - (face * face) * before, newest
    scale = reciprocal(newest)
    return before * scale, part * scale if right else None


def forward_kernel(
    slabs, lanes_count, src_in, spacing, ty_in, tx, phi, lk, lb, lam_in,
    modal_out, jump_out, heights_out,
    modal, src, spread, ty, lam, heights, cond, x3, f, inv_s, part_s, inv_high, from_low, from_high,
    to_low, to_high, ends, ends_in, jumps, jumps_all, k_inv, k_part, g_modes, g_cuts,
    g_send, g_in, sem_in, sem_m, sem_h, sem_up, sem_down, sem_e, sem_r, sem_j, sem_g,
):
    growth = lax.axis_index("growth")
    lat = lax.axis_index("lat")
    depth, m = f.shape[1], f.shape[2]
    half = m // 2
    nblk = f.shape[0]
    nz = slabs * depth
    width = src.shape[1]
    share = max(1, lanes_count // nblk)
    tiles = [slice(0, half), slice(half, m)]
    lag = LAG * (slabs - 1)
    per_slab = lam.shape[0]

    loads = [
        pltpu.make_async_copy(a, b, sem_in.at[n])
        for n, (a, b) in enumerate(
            [
                (ty_in, ty),
                (lam_in.at[pl.ds(growth * per_slab, per_slab)], lam),
            ]
        )
    ]
    planes_in = [
        pltpu.make_async_copy(
            src_in.at[pl.ds(k * m, m)], src.at[pl.ds(k * m, m)], sem_in.at[2 + k]
        )
        for k in range(depth)
    ]
    for load in planes_in + loads:
        load.start()
    for k in range(depth):
        spread[k : k + 1, :] = jnp.full((1, LANES), spacing[k], jnp.float32)

    barrier = pltpu.get_barrier_semaphore()
    for off in range(1, slabs):
        pl.semaphore_signal(
            barrier, inc=1, device_id=(lax.rem(growth + off, slabs), lat), device_id_type=MESH
        )
    for off in range(1, lanes_count):
        pl.semaphore_signal(
            barrier, inc=1, device_id=(growth, lax.rem(lat + off, lanes_count)),
            device_id_type=MESH,
        )
    rows = src.shape[0]

    mid = width // 2

    def split_rows(i, carry):
        at = pl.ds(pl.multiple_of(i * m, m), m)
        pltpu.make_async_copy(src_in.at[at], src.at[at], sem_in.at[2 + i]).wait()
        for q in range(mid // LANES):
            near = src[at, q * LANES : (q + 1) * LANES]
            far = mirror(src[at, width - (q + 1) * LANES : width - q * LANES])
            for n, value in enumerate((near + far, near - far)):
                high, low = split(value)
                for place, part in enumerate((high, low, high)):
                    start = place * mid + q * LANES
                    x3[n, at, start : start + LANES] = part
        return carry

    lax.fori_loop(0, depth, split_rows, 0)
    pl.semaphore_wait(barrier, slabs + lanes_count - 2)

    def height_copy(off, owner, target):
        return pltpu.make_async_remote_copy(
            src_ref=spread,
            dst_ref=heights.at[pl.ds(owner * depth, depth)],
            send_sem=sem_h.at[0, off],
            recv_sem=sem_h.at[1, off],
            device_id=(target, lat),
            device_id_type=MESH,
        )

    for off in range(1, slabs):
        height_copy(off, growth, lax.rem(growth + off, slabs)).start()
    heights[pl.ds(growth * depth, depth), :] = spread[...]
    def eigen_of(i, tile):
        at = pl.ds(pl.multiple_of(i * LANES, LANES), LANES)
        return lk[tile, :] + lb[:, at]

    def pivots_below(i):
        def one(tile):
            eigen = eigen_of(i, tile)
            return lax.fori_loop(
                0, growth,
                lambda n, inv: leap(
                    cond, heights, n * depth, depth, eigen, inv, None, None, True
                )[0],
                jnp.zeros((half, LANES), jnp.float32),
            )

        return [one(tile) for tile in tiles]

    def pivots_above(i):
        def one(tile):
            eigen = eigen_of(i, tile)
            return lax.fori_loop(
                0, slabs - 1 - growth,
                lambda n, inv: leap(
                    cond, heights, (slabs - 1 - n) * depth, depth, eigen, inv, None, None, False
                )[0],
                jnp.zeros((half, LANES), jnp.float32),
            )

        return [one(tile) for tile in tiles]

    @pl.when(growth == 0)
    def _():
        from_low[...] = jnp.zeros_like(from_low)

    @pl.when(growth == slabs - 1)
    def _():
        from_high[...] = jnp.zeros_like(from_high)

    first = growth * depth
    chunk = min(512, rows)
    planes = chunk // m

    half_pairs = mid // PAIR

    def transform(pair):
        parity = pair // half_pairs
        columns = pl.ds(pl.multiple_of(lax.rem(pair, half_pairs) * PAIR, PAIR), PAIR)

        def one(c, carry):
            at = pl.ds(pl.multiple_of(c * chunk, chunk), chunk)
            along_y = dot(x3[parity, at, :], ty[parity, :, columns])
            for k in range(planes):
                part = slice(k * m, (k + 1) * m)
                both = dot(tx[...], stacked(along_y[part, :]))
                for side in range(PAIR // LANES):
                    f[pair * (PAIR // LANES) + side, c * planes + k] = both[
                        :, side * LANES : (side + 1) * LANES
                    ]
            return carry

        lax.fori_loop(0, rows // chunk, one, 0)

    loads[0].wait()
    transform(0)
    for off in range(1, slabs):
        behind = lax.rem(growth + slabs - off, slabs)
        copy = height_copy(off, behind, lax.rem(growth + off, slabs))
        copy.wait_send()
        copy.wait_recv()
    fill_conduct(heights, cond)
    heights_out[...] = heights[...]
    loads[1].wait()

    def up_copy(i):
        return pltpu.make_async_remote_copy(
            src_ref=to_high.at[i], dst_ref=from_low.at[i],
            send_sem=sem_up.at[0, i], recv_sem=sem_up.at[1, i],
            device_id=(lax.rem(growth + 1, slabs), lat), device_id_type=MESH,
        )

    def down_copy(i):
        return pltpu.make_async_remote_copy(
            src_ref=to_low.at[i], dst_ref=from_high.at[i],
            send_sem=sem_down.at[0, i], recv_sem=sem_down.at[1, i],
            device_id=(lax.rem(growth + slabs - 1, slabs), lat), device_id_type=MESH,
        )

    def sweep_up(i):
        inv = pivots_below(i)

        @pl.when(growth > 0)
        def _():
            up_copy(i).wait_recv()

        eigen = [eigen_of(i, tile) for tile in tiles]
        part = [from_low[i, tile, :] for tile in tiles]
        for k in range(depth):
            z = first + k
            face = row(cond, z)
            height = row(heights, z)
            for n, tile in enumerate(tiles):
                inv[n] = inverse_pivot(cond, heights, z, eigen[n], inv[n], face)
                part[n] = (height * f[i, k, tile, :] + face * part[n]) * inv[n]
                inv_s[i, k, tile, :] = inv[n]
                part_s[i, k, tile, :] = part[n]

        @pl.when(growth < slabs - 1)
        def _():
            for n, tile in enumerate(tiles):
                to_high[i, tile, :] = part[n]
            up_copy(i).start()

    def sweep_down(i):
        for tile, value in zip(tiles, pivots_above(i)):
            inv_high[i, tile, :] = value

        @pl.when(growth < slabs - 1)
        def _():
            down_copy(i).wait_recv()

        @pl.when(growth > 0)
        def _():
            for tile in tiles:
                _, part = leap(
                    cond, heights, first, depth, eigen_of(i, tile), inv_high[i, tile, :],
                    from_high[i, tile, :],
                    lambda z: row(heights, z) * f[i, z - first, tile, :], False,
                )
                to_low[i, tile, :] = part
            down_copy(i).start()

    def block_of(rank):
        return rank // share

    def ends_copy(off, owner, target):
        return pltpu.make_async_remote_copy(
            src_ref=ends.at[block_of(target)], dst_ref=ends_in.at[owner],
            send_sem=sem_e.at[0, off], recv_sem=sem_e.at[1, off],
            device_id=(growth, target), device_id_type=MESH,
        )

    def modal_copy(i):
        return pltpu.make_async_copy(modal.at[i], modal_out.at[i], sem_m.at[i])

    def finish(i):
        face = row(cond, first + depth)
        value = []
        weight = [phi[tile, :] for tile in tiles]
        for n, tile in enumerate(tiles):
            inv = inv_s[i, depth - 1, tile, :]
            top = part_s[i, depth - 1, tile, :] + (face * inv) * from_high[i, tile, :]
            value.append(top * reciprocal(1.0 - (face * face) * inv * inv_high[i, tile, :]))
        for k in reversed(range(depth)):
            if k < depth - 1:
                face = row(cond, first + k + 1)
                for n, tile in enumerate(tiles):
                    value[n] = part_s[i, k, tile, :] + (face * inv_s[i, k, tile, :]) * value[n]
            sums = []
            for n, tile in enumerate(tiles):
                modal[i, k, tile, :] = value[n]
                sums.append(jnp.sum(weight[n] * value[n], axis=0, keepdims=True))
            ends[i, k : k + 1, :] = sums[0] + sums[1]
            ends[i, depth + k : depth + k + 1, :] = sums[0] - sums[1]
        modal_copy(i).start()
        for n in range(share):
            target = i * share + n
            off = lax.rem(target + lanes_count - lat, lanes_count)
            pl.when(target != lat)(ends_copy(off, lat, target).start)

    per_pair = PAIR // LANES
    cuts = lanes_count - 1
    middle = nz // 2
    per_step = pl.cdiv(per_slab, lag)

    def face_pivots(j):
        weight = [lam[j, tile, :] for tile in tiles]
        at = pl.ds(pl.multiple_of((lat // share) * LANES, LANES), LANES)
        eigen = [w + lb[:, at] for w in weight]
        low = [jnp.zeros((half, LANES), jnp.float32) for _ in tiles]
        high = list(low)
        for k in range(middle):
            face = row(cond, k)
            z = nz - 1 - k
            face_high = row(cond, z + 1)
            for n, tile in enumerate(tiles):
                low[n] = inverse_pivot(cond, heights, k, eigen[n], low[n], face)
                k_inv[j, k, tile, :] = low[n]
                high[n] = inverse_pivot(cond, heights, z, eigen[n], high[n], face_high)
                k_inv[j, z, tile, :] = high[n]

    def stage(tt, carry):
        @pl.when((tt > 0) & (tt < nblk // per_pair))
        def _():
            transform(tt)

        for side in range(per_pair):
            t = tt * per_pair + side
            up_i = t - LAG * growth
            down_i = t - LAG * (slabs - 1 - growth)
            end_i = t - lag

            for n in range(per_step):
                j = (t - nblk) * per_step + n
                pl.when((j >= 0) & (j < per_slab))(functools.partial(face_pivots, j))

            @pl.when((up_i >= 0) & (up_i < nblk))
            def _():
                sweep_up(up_i)

            @pl.when((down_i >= 0) & (down_i < nblk))
            def _():
                sweep_down(down_i)

            @pl.when((end_i >= 0) & (end_i < nblk))
            def _():
                finish(end_i)

        return carry

    lax.fori_loop(0, pl.cdiv(nblk + lag, per_pair), stage, 0)

    ends_in[lat] = ends[block_of(lat)]

    for off in range(1, lanes_count):
        copy = ends_copy(
            off, lax.rem(lat + lanes_count - off, lanes_count), lax.rem(lat + off, lanes_count)
        )
        copy.wait_send()
        copy.wait_recv()

    sines = [
        [
            math.sqrt(2.0 / lanes_count) * math.sin(math.pi * (c + 1) * (j + 1) / lanes_count)
            for j in range(cuts)
        ]
        for c in range(cuts)
    ]
    jump = [ends_in[c, depth:, :] - ends_in[c + 1, :depth, :] for c in range(cuts)]
    for j in range(cuts):
        total = jump[0] * sines[0][j]
        for c in range(1, cuts):
            total += jump[c] * sines[c][j]
        jumps[j] = total
    for j in range(cuts, jumps.shape[0]):
        jumps[j] = jnp.zeros(jumps.shape[1:], jnp.float32)

    def share_of(rank):
        return pl.ds(rank * per_slab, per_slab)

    jumps_all[growth] = jumps[share_of(growth)]

    def jumps_copy(off, owner, target):
        return pltpu.make_async_remote_copy(
            src_ref=jumps.at[share_of(target)], dst_ref=jumps_all.at[owner],
            send_sem=sem_r.at[0, off], recv_sem=sem_r.at[1, off],
            device_id=(target, lat), device_id_type=MESH,
        )

    for off in range(1, slabs):
        jumps_copy(off, growth, lax.rem(growth + off, slabs)).start()
    for off in range(1, slabs):
        copy = jumps_copy(
            off, lax.rem(growth + slabs - off, slabs), lax.rem(growth + off, slabs)
        )
        copy.wait_send()
        copy.wait_recv()

    def correct(j, carry):
        def held(z):
            return jumps_all[z // depth, j, z % depth : z % depth + 1, :]

        weight = [lam[j, tile, :] for tile in tiles]
        low = [jnp.zeros((half, LANES), jnp.float32) for _ in tiles]
        high = list(low)
        for k in range(middle):
            z = nz - 1 - k
            face = row(cond, k)
            right = row(heights, k) * held(k)
            face_high = row(cond, z + 1)
            right_high = row(heights, z) * held(z)
            for n, tile in enumerate(tiles):
                low[n] = (right + face * low[n]) * k_inv[j, k, tile, :]
                k_part[k, tile, :] = low[n]
                high[n] = (right_high + face_high * high[n]) * k_inv[j, z, tile, :]
                k_part[z, tile, :] = high[n]

        def put(z, value):
            total = sum(
                jnp.sum(w * v, axis=0, keepdims=True) for w, v in zip(weight, value)
            )
            g_modes[growth, j, z : z + 1, :] = held(z) - total * (1.0 / m)

        face = row(cond, middle)
        below, above = [], []
        for n, tile in enumerate(tiles):
            inv_a = face * k_inv[j, middle - 1, tile, :]
            inv_b = face * k_inv[j, middle, tile, :]
            below.append((low[n] + inv_a * high[n]) * reciprocal(1.0 - inv_a * inv_b))
            above.append(high[n] + inv_b * below[n])
        put(middle - 1, below)
        put(middle, above)
        for k in range(1, middle):
            z = middle - 1 - k
            face = row(cond, z + 1)
            for n, tile in enumerate(tiles):
                below[n] = k_part[z, tile, :] + (face * k_inv[j, z, tile, :]) * below[n]
            put(z, below)
            z = middle + k
            face = row(cond, z)
            for n, tile in enumerate(tiles):
                above[n] = k_part[z, tile, :] + (face * k_inv[j, z, tile, :]) * above[n]
            put(z, above)
        for off in range(1, slabs):
            modes_copy(off, growth, j).start()
        return carry

    def modes_copy(off, owner, j):
        return pltpu.make_async_remote_copy(
            src_ref=g_modes.at[owner, j], dst_ref=g_modes.at[owner, j],
            send_sem=sem_j.at[0, off, j], recv_sem=sem_j.at[1, off, j],
            device_id=(lax.rem(growth + off, slabs), lat), device_id_type=MESH,
        )

    lax.fori_loop(0, per_slab, correct, 0)
    for off in range(1, slabs):
        for j in range(per_slab):
            modes_copy(off, growth, j).wait_send()
            modes_copy(off, lax.rem(growth + slabs - off, slabs), j).wait_recv()

    for c in range(cuts):
        total = g_modes[0, 0] * sines[c][0]
        for j in range(1, cuts):
            total += g_modes[j // per_slab, j % per_slab] * sines[c][j]
        g_cuts[c] = total
    for d in range(lanes_count):
        low = g_cuts[d - 1] if d > 0 else jnp.zeros((nz, LANES), jnp.float32)
        high = g_cuts[d] if d < cuts else jnp.zeros((nz, LANES), jnp.float32)
        g_send[d, 0] = high - low
        g_send[d, 1] = -(high + low)

    def g_copy(off, owner, target):
        return pltpu.make_async_remote_copy(
            src_ref=g_send.at[target], dst_ref=g_in.at[block_of(owner)],
            send_sem=sem_g.at[0, off], recv_sem=sem_g.at[1, off],
            device_id=(growth, target), device_id_type=MESH,
        )

    def speaks(rank, act):
        if share == 1:
            act()
        else:
            pl.when(lax.rem(rank, share) == 0)(act)

    def own_block():
        g_in[block_of(lat)] = g_send[lat]

    for off in range(1, lanes_count):
        copy = g_copy(off, lat, lax.rem(lat + off, lanes_count))
        speaks(lat, copy.start)
    speaks(lat, own_block)
    for off in range(1, lanes_count):
        owner = lax.rem(lat + lanes_count - off, lanes_count)
        target = lax.rem(lat + off, lanes_count)
        speaks(lat, g_copy(off, lat, target).wait_send)
        speaks(owner, g_copy(off, owner, target).wait_recv)
    def drain(i, carry):
        @pl.when(growth < slabs - 1)
        def _():
            up_copy(i).wait_send()

        @pl.when(growth > 0)
        def _():
            down_copy(i).wait_send()

        modal_copy(i).wait()
        return carry

    lax.fori_loop(0, nblk, drain, 0)
    jump_out[...] = g_in[...]


def inverse_kernel(
    slabs, modal_in, jump, heights, ty_in, tx, phi, lk, lb,
    out_hbm,
    modal, ty, out, sem_in, sem_out, cond, inv_s, part_s, m3, g3,
):
    growth = lax.axis_index("growth")
    nblk, depth, m = modal.shape[:3]
    per_pair = PAIR // LANES
    pairs = nblk // per_pair
    for n in range(pairs):
        part = pl.ds(n * per_pair, per_pair)
        pltpu.make_async_copy(modal_in.at[part], modal.at[part], sem_in.at[n]).start()
    table = pltpu.make_async_copy(ty_in, ty, sem_in.at[pairs])
    table.start()
    half = m // 2
    tiles = [slice(0, half), slice(half, m)]
    first = growth * depth
    fill_conduct(heights, cond)

    def correct(i, side, slot, jobs):
        at = pl.ds(pl.multiple_of(i * LANES, LANES), LANES)
        eigen = [lk[tile, :] + lb[:, at] for tile in tiles]
        zero = jnp.zeros((half, LANES), jnp.float32)

        def advance(z, face, state):
            height = row(heights, z)
            new = []
            for n in range(2):
                inv, part = state[2 * n], state[2 * n + 1]
                inv = inverse_pivot(cond, heights, z, eigen[n], inv, face)
                right = height * jump[i, n, pl.ds(z, 1), :]
                new += [inv, (right + face * part) * inv]
            return tuple(new)

        def up(z, state):
            return advance(z, row(cond, z), state)

        def outside(n, upward):
            def right(z):
                return row(heights, z) * jump[i, n, pl.ds(z, 1), :]

            def one(q, state):
                start = (q if upward else slabs - 1 - q) * depth
                return leap(cond, heights, start, depth, eigen[n], *state, right, upward)

            trips = growth if upward else slabs - 1 - growth
            return lax.fori_loop(0, trips, one, (zero, zero))

        high = outside(0, False) + outside(1, False)
        state = outside(0, True) + outside(1, True)
        for k in range(depth):
            for job in jobs[k::depth]:
                job()
            state = up(first + k, state)
            for n, tile in enumerate(tiles):
                inv_s[k, tile, :] = state[2 * n]
                part_s[k, tile, :] = state[2 * n + 1]
        face = row(cond, first + depth)
        value = []
        for n in range(2):
            inv, part = state[2 * n], state[2 * n + 1]
            top = part + (face * inv) * high[2 * n + 1]
            value.append(top * reciprocal(1.0 - (face * face) * inv * high[2 * n]))
        for k in reversed(range(depth)):
            if k < depth - 1:
                face = row(cond, first + k + 1)
            for n, tile in enumerate(tiles):
                if k < depth - 1:
                    value[n] = part_s[k, tile, :] + (face * inv_s[k, tile, :]) * value[n]
                a, b = split(modal[i, k, tile, :] - phi[tile, :] * value[n])
                columns = slice(side * LANES, (side + 1) * LANES)
                for place, part in enumerate((a, a, b)):
                    start = place * m + n * half
                    m3[slot, k, start : start + half, columns] = part

    width = out.shape[1]
    mid = width // 2
    half_pairs = mid // PAIR
    rows = out.shape[0]
    chunk = min(256, rows)

    def along_x(tt, k):
        a, b = split(dot(tx[...], m3[tt % 2, k]))
        for place, part in enumerate((a, b, a)):
            start = place * mid + (tt % half_pairs) * PAIR
            g3[tt // half_pairs, k * m : (k + 1) * m, start : start + PAIR] = part

    def even_part(r, c):
        at = slice(r * chunk, (r + 1) * chunk)
        columns = slice(c * PAIR, (c + 1) * PAIR)
        out[at, columns] = dot(g3[0, at, :], ty[0, :, columns])

    for tt in range(pairs):
        part = pl.ds(tt * per_pair, per_pair)
        pltpu.make_async_copy(modal_in.at[part], modal.at[part], sem_in.at[tt]).wait()
        jobs = []
        if tt > 0:
            jobs += [functools.partial(along_x, tt - 1, k) for k in range(depth)]
        if tt == pairs - 1:
            table.wait()
            jobs += [
                functools.partial(even_part, r, c)
                for c in range(half_pairs)
                for r in range(rows // chunk)
            ]
        for side in range(per_pair):
            correct(tt * per_pair + side, side, tt % 2, jobs[side::per_pair])
    for k in range(depth):
        along_x(pairs - 1, k)

    def store(r):
        at = pl.ds(r * chunk if isinstance(r, int) else pl.multiple_of(r * chunk, chunk), chunk)
        return pltpu.make_async_copy(out.at[at], out_hbm.at[at], sem_out.at[r])

    def rows_of(r, carry):
        at = pl.ds(pl.multiple_of(r * chunk, chunk), chunk)
        for c in range(half_pairs):
            columns = slice(c * PAIR, (c + 1) * PAIR)
            even = out[at, columns]
            odd = dot(g3[1, at, :], ty[1, :, columns])
            out[at, columns] = even + odd
            far = even - odd
            for q in range(PAIR // LANES):
                start = width - c * PAIR - (q + 1) * LANES
                out[at, start : start + LANES] = mirror(far[:, q * LANES : (q + 1) * LANES])
        store(r).start()
        return carry

    lax.fori_loop(0, rows // chunk, rows_of, 0)
    for r in range(rows // chunk):
        store(r).wait()


def per_device(source, spacing):
    depth, m, width = source.shape
    lanes_count = lax.axis_size("lat")
    slabs = lax.axis_size("growth")
    nz = slabs * depth
    points = m * lanes_count
    nblk = width // LANES
    cuts = lanes_count - 1
    f32 = jnp.float32

    order = np.concatenate([np.arange(0, m, 2), np.arange(1, m, 2)])
    local = cosine_table(m)[order]
    mid = width // 2
    along_y = cosine_table(width)
    halves = np.stack([along_y[0::2, :mid], along_y[1::2, :mid]])
    ty_forward = right_parts(np.swapaxes(halves, 1, 2))
    ty_back = right_parts(halves)
    tx_forward = left_parts(local)
    tx_back = left_parts(local.T)
    mode_y = np.concatenate([np.arange(0, width, 2), np.arange(1, width, 2)])

    def spread_lanes(column):
        return jnp.asarray(np.repeat(np.asarray(column, np.float32)[..., None], LANES, axis=-1))

    phi = spread_lanes(local[:, 0])
    lk = spread_lanes(eigenvalues(order, m))
    lb = jnp.asarray(eigenvalues(mode_y, width).astype(np.float32)[None, :])
    folds = []
    for j in range(1, lanes_count):
        ids = [k for k in range(1, points) if k % (2 * lanes_count) in (j, 2 * lanes_count - j)]
        folds.append(eigenvalues(ids, points))
    per_slab = pl.cdiv(cuts, slabs)
    folds += [folds[0]] * (slabs * per_slab - cuts)
    lam = spread_lanes(np.stack(folds))

    flat = source.reshape(depth * m, width)
    vmem = pl.BlockSpec(memory_space=pltpu.VMEM)
    smem = pl.BlockSpec(memory_space=pltpu.SMEM)
    anywhere = pl.BlockSpec(memory_space=pl.ANY)
    dma = pltpu.SemaphoreType.DMA
    V = pltpu.VMEM
    modal, jump, heights = pl.pallas_call(
        functools.partial(forward_kernel, slabs, lanes_count),
        out_shape=(
            jax.ShapeDtypeStruct((nblk, depth, m, LANES), f32),
            jax.ShapeDtypeStruct((nblk, 2, nz, LANES), f32),
            jax.ShapeDtypeStruct((nz, LANES), f32),
        ),
        in_specs=[anywhere, smem, anywhere] + [vmem] * 4 + [anywhere],
        out_specs=(anywhere, vmem, vmem),
        scratch_shapes=[
            V((nblk, depth, m, LANES), f32),
            V((depth * m, width), f32),
            V((depth, LANES), f32),
            V((2, 3 * mid, mid), jnp.bfloat16),
            V((per_slab, m, LANES), f32),
            V((nz, LANES), f32),
            V((nz + 1, LANES), f32),
            V((2, depth * m, 3 * mid), jnp.bfloat16),
            V((nblk, depth, m, LANES), f32),
            V((nblk, depth, m, LANES), f32),
            V((nblk, depth, m, LANES), f32),
            V((nblk, m, LANES), f32),
            V((nblk, m, LANES), f32),
            V((nblk, m, LANES), f32),
            V((nblk, m, LANES), f32),
            V((nblk, m, LANES), f32),
            V((nblk, 2 * depth, LANES), f32),
            V((lanes_count, 2 * depth, LANES), f32),
            V((slabs * per_slab, depth, LANES), f32),
            V((slabs, per_slab, depth, LANES), f32),
            V((per_slab, nz, m, LANES), f32),
            V((nz, m, LANES), f32),
            V((slabs, per_slab, nz, LANES), f32),
            V((cuts, nz, LANES), f32),
            V((lanes_count, 2, nz, LANES), f32),
            V((nblk, 2, nz, LANES), f32),
            dma((depth + 2,)),
            dma((nblk,)),
            dma((2, slabs)),
            dma((2, nblk)),
            dma((2, nblk)),
            dma((2, lanes_count)),
            dma((2, slabs)),
            dma((2, slabs, per_slab)),
            dma((2, lanes_count)),
        ],
        compiler_params=pltpu.CompilerParams(
            collective_id=0, has_side_effects=True, vmem_limit_bytes=VMEM_BYTES
        ),
        name="slab_solve",
    )(flat, spacing, ty_forward, tx_forward, phi, lk, lb, lam)

    result = pl.pallas_call(
        functools.partial(inverse_kernel, slabs),
        out_shape=jax.ShapeDtypeStruct((depth * m, width), f32),
        in_specs=[anywhere, vmem, vmem, anywhere] + [vmem] * 4,
        out_specs=anywhere,
        scratch_shapes=[
            V((nblk, depth, m, LANES), f32),
            V((2, 3 * mid, mid), jnp.bfloat16),
            V((depth * m, width), f32),
            dma((width // PAIR + 2,)),
            dma((width // PAIR,)),
            V((nz + 1, LANES), f32),
            V((depth, m, LANES), f32),
            V((depth, m, LANES), f32),
            V((2, depth, 3 * m, PAIR), jnp.bfloat16),
            V((2, depth * m, 3 * mid), jnp.bfloat16),
        ],
        compiler_params=pltpu.CompilerParams(vmem_limit_bytes=VMEM_BYTES),
        name="face_correction",
    )(modal, jump, heights, ty_back, tx_back, phi, lk, lb)
    return result.reshape(depth, m, width)


def solution(mesh):
    return jax.shard_map(
        per_device,
        mesh=mesh,
        in_specs=(P("growth", "lat", None), P("growth")),
        out_specs=P("growth", "lat", None),
        check_vma=False,
    )
```
